32 devices in a mesh: shot: 16 (over z, y, x), freq: 2 (over core).
Axes of the slice: x: 2, y: 2, z: 4, core: 2. Of those that a mesh axis runs over, the one named last changes fastest.
Arguments:
- traces: bfloat16 [32, 1024, 1024], P('shot', None, 'freq'), may hold values from -6 to 6
- frequency_bins: int32 [8], replicated, may hold values from 1 to 511
- aperture: int32 [32, 1024, 32], P(None, 'shot'), may hold values from 0 to 31, as said below
- lengths: int32 [32, 1024], P(None, 'shot'), may hold values from 1 to 32, as said below
- filters: bfloat16 [32, 31], P('shot'), may hold values from -1 to 1
Outputs:
- multiples: bfloat16 [32, 1024, 1024], P('shot', None, 'freq')
The draws below stay inside these ranges and needn't reach their ends.
Inputs may be any that keep to these rules, and one draw needn't show every extreme that they name: aperture[s, r, k] names a shot whose source lies at receiver station 32 times that number; only entries with k below lengths[s, r] are used. The lengths of the shots held by one device along `shot` (one index of the `shot` axis) and the receivers of one index of shot sum to at most 2112; in every draw the shots of some index reach 2112 with the receivers of every index.
All inputs are finite; a program needn't handle non-finite values.
Results may differ from the reference program's by a relative error of at most 0.015.
Values may be sent and summed in bfloat16 or wider, within the bound.
No kernel may reach another device: no remote copies, remote signals or barrier semaphores. Data moves between devices by JAX's collectives and lax.ppermute only.
A program may use at most 192 MiB of HBM per device.

```python
import math
import jax
import jax.numpy as jnp
from jax import lax

R = 1024
NT = 1024
NF = 8
KMAX = 32
TAPS = 31
SHOT_DEV = 2
SHOTS = 32
STRIDE = 32
HALF = 15
N_SHOT = 16


def draw_aperture(key, part):
    shot_ids = jnp.arange(SHOTS, dtype=jnp.int32)[:, None, None]
    receiver_ids = jnp.arange(R, dtype=jnp.int32)[None, :, None]
    middle = (shot_ids + receiver_ids // STRIDE) // 2
    offsets = jax.random.randint(key, (SHOTS, R, KMAX), -KMAX, KMAX + 1)
    return ((middle + offsets) % SHOTS).astype(jnp.int32)


def draw_lengths(key, part):
    groups = N_SHOT
    receiver_dev = R // N_SHOT
    block_size = SHOT_DEV * receiver_dev
    half_block = block_size // 2
    key_total, key_split, key_row, key_column = jax.random.split(key, 4)
    totals = jax.random.randint(key_total, (groups, groups), KMAX // 4 + 2, KMAX + 2)
    full_row = jax.random.randint(key_row, (), 0, groups)
    full_column = jax.random.randint(key_column, (), 0, groups)
    rows_index = jnp.arange(groups, dtype=jnp.int32)[:, None]
    totals = jnp.where(rows_index == full_row, KMAX + 1, totals)
    raw_bits = jax.random.randint(key_split, (groups, groups, half_block), 0, 1 << 20)
    first_part = raw_bits % (totals[:, :, None] - 1) + 1
    corner = (rows_index[:, :, None] == full_row) & (jnp.arange(groups, dtype=jnp.int32)[None, :, None] == full_column) & (jnp.arange(half_block, dtype=jnp.int32)[None, None, :] == 0)
    first_part = jnp.where(corner, 1, first_part)
    second_part = totals[:, :, None] - first_part
    blocks = jnp.concatenate([first_part, second_part], axis=2)
    blocks = blocks.reshape(groups, groups, SHOT_DEV, receiver_dev).transpose(0, 2, 1, 3)
    return blocks.reshape(SHOT_DEV * groups, R).astype(jnp.int32)


def touch_ends(drawn, own_key, least, high):
    longest = drawn.shape.index(max(drawn.shape))
    spots = []
    for shift in (0, 1):
        where = [jax.random.randint(jax.random.fold_in(own_key, axis), (), 0, length) for axis, length in enumerate(drawn.shape)]
        where[longest] = (where[longest] + shift) % drawn.shape[longest]
        spots.append(tuple(where))
    return drawn.at[spots[0]].set(least).at[spots[1]].set(high)


def shard_levels(rng, shape, cuts, least, high):
    level, own = 1.0, jax.random.fold_in(rng, 6)
    for position, blocks in cuts:
        steps = jnp.exp(jax.random.uniform(jax.random.fold_in(own, position), (blocks,), jnp.float32, least / len(cuts), high / len(cuts)))
        level = level * jnp.repeat(steps, shape[position] // blocks).reshape([-1 if axis == position else 1 for axis in range(len(shape))])
    return level


def centred(stream_key, extent, deviation, limit, pieces=(), kind=jnp.bfloat16):
    gain = shard_levels(stream_key, extent, pieces, -0.22, 0.18) if pieces else 1.0
    drawn = jax.random.normal(stream_key, extent, jnp.float32) * deviation * gain
    return jnp.minimum(jnp.maximum(drawn, -limit), limit).astype(kind)


def setup_inputs(seed: int = 0) -> dict:
    arg_keys = jax.random.split(jax.random.key(seed), 6)
    traces = centred(arg_keys[0], (SHOTS, R, NT), 1.0, 6.0, ((0, 16), (2, 2)))
    frequency_bins = touch_ends(jax.random.randint(arg_keys[1], (NF,), 1, NT // 2), jax.random.fold_in(arg_keys[1], 1), 1, (NT // 2) - 1).astype(jnp.int32)
    aperture = draw_aperture(jax.random.fold_in(arg_keys[5], 71), 0)
    lengths = draw_lengths(jax.random.fold_in(arg_keys[5], 71), 0)
    filters = centred(arg_keys[4], (SHOTS, TAPS), TAPS ** -0.5, 1.0, ((0, 16),))
    return dict(traces=traces, frequency_bins=frequency_bins, aperture=aperture, lengths=lengths, filters=filters)


def fourier_rows(bin_rows, first_time, sample_count, period):
    sample_times = first_time + jnp.arange(sample_count, dtype=jnp.int32)
    phases = (bin_rows[:, None] * sample_times[None, :]) % period
    angles = phases.astype(jnp.float32) * (2.0 * math.pi / period)
    return jnp.cos(angles), jnp.sin(angles)


def pair_product(first_leg, second):
    first_leg = first_leg.astype(jnp.float32)
    second = second.astype(jnp.float32)
    real_part = first_leg[:, 0] * second[:, 0] - first_leg[:, 1] * second[:, 1]
    imag_part = first_leg[:, 0] * second[:, 1] + first_leg[:, 1] * second[:, 0]
    return jnp.stack([real_part, imag_part], axis=1)


def reference(traces, frequency_bins, aperture, lengths, filters):
    cosines, sines = fourier_rows(frequency_bins, 0, NT, NT)
    basis_rows = (jnp.stack([cosines, -sines], axis=1) * (NT ** -0.5)).astype(jnp.bfloat16).reshape(NF * 2, NT)
    spectra = lax.dot_general(basis_rows, traces.reshape(SHOTS * R, NT), (((1,), (1,)), ((), ())), preferred_element_type=jnp.float32)
    spectra = spectra.astype(jnp.bfloat16).reshape(NF, 2, SHOTS, R)
    synthesis_rows = jnp.stack([cosines, -sines], axis=1).astype(jnp.bfloat16).reshape(NF * 2, NT)
    every_receiver = jnp.arange(R, dtype=jnp.int32)[:, None]
    list_slots = jnp.arange(KMAX, dtype=jnp.int32)[None, :]

    def one_shot(inputs):
        shot_index, shot_list, shot_lengths, shot_filter = inputs
        shot_spectra = spectra[:, :, shot_index, :]
        first_leg = shot_spectra[:, :, shot_list * STRIDE]
        second = spectra[:, :, shot_list, every_receiver]
        product_terms = pair_product(first_leg, second)
        keep_mask = (list_slots < shot_lengths[:, None])[None, None]
        summed = jnp.where(keep_mask, product_terms, 0.0).sum(axis=-1)
        spectra_out = (summed * (KMAX ** -0.5)).astype(jnp.bfloat16).reshape(NF * 2, R)
        predicted = lax.dot_general(spectra_out, synthesis_rows, (((0,), (0,)), ((), ())), preferred_element_type=jnp.float32).astype(jnp.bfloat16)
        padded = jnp.pad(predicted.astype(jnp.float32), ((0, 0), (HALF, HALF)))
        running = jnp.zeros((R, NT), jnp.float32)
        for tap in range(TAPS):
            running = running + shot_filter[tap].astype(jnp.float32) * padded[:, 2 * HALF - tap: 2 * HALF - tap + NT]
        return running.astype(jnp.bfloat16)

    return lax.map(one_shot, (jnp.arange(SHOTS, dtype=jnp.int32), aperture, lengths, filters))
```

```python
import math

import jax
import jax.numpy as jnp
from jax import lax
from jax.experimental import pallas as pl
from jax.experimental.pallas import tpu as pltpu
from jax.sharding import PartitionSpec as P

NT = 1024
NF = 8
KMAX = 32
TAPS = 31
HALF = (TAPS - 1) // 2
LANES = 128
PIECE = 32
DEVICES = ("shot", "freq")
F32 = jnp.float32
BF16 = jnp.bfloat16
VMEM_LIMIT = 48 * 1024 * 1024


def cosine_sine(phases):
    quarter = NT // 4
    turn = (phases + quarter // 2) // quarter
    angle = (phases - turn * quarter).astype(F32) * (2.0 * math.pi / NT)
    square = angle * angle
    sine = angle * (1.0 + square * (-1 / 6 + square * (1 / 120 + square * (-1 / 5040 + square / 362880))))
    cosine = 1.0 + square * (-1 / 2 + square * (1 / 24 + square * (-1 / 720 + square / 40320)))
    odd = turn % 2 == 1
    near, far = jnp.where(odd, sine, cosine), jnp.where(odd, cosine, sine)
    return (
        jnp.where((turn == 1) | (turn == 2), -near, near),
        jnp.where((turn == 2) | (turn == 3), -far, far),
    )


def basis_in_kernel(bins_ref, first_time, width):
    rows = lax.broadcasted_iota(jnp.int32, (NF, width), 0)
    times = lax.broadcasted_iota(jnp.int32, (NF, width), 1) + first_time
    bins = jnp.zeros((NF, width), jnp.int32)
    for f in range(NF):
        bins = jnp.where(rows == f, bins_ref[f], bins)
    cosines, sines = cosine_sine((bins * times) & (NT - 1))
    return jnp.concatenate([cosines, -sines], axis=0), times


def analysis_kernel(bins_ref, traces_ref, message_ref, basis_ref, rows_ref):
    step = pl.program_id(0)
    shot_dev, block, time_dev = traces_ref.shape

    @pl.when(step == 0)
    def _():
        first_time = lax.axis_index("freq") * time_dev
        basis, _ = basis_in_kernel(bins_ref, first_time, time_dev)
        basis_ref[...] = (basis * NT ** (-0.5)).astype(BF16)

    for s in range(shot_dev):
        rows_ref[s, pl.ds(pl.multiple_of(step * block, block), block), :] = lax.dot_general(
            traces_ref[s], basis_ref[...], (((1,), (1,)), ((), ())), preferred_element_type=F32
        )

    @pl.when(step == pl.num_programs(0) - 1)
    def _():
        count = message_ref.shape[0]
        stations = [rows_ref[s, pl.ds(0, count, stride=PIECE), :] for s in range(shot_dev)]
        for d in range(count):
            own = [rows_ref[s, d * PIECE : (d + 1) * PIECE, :] for s in range(shot_dev)]
            message_ref[d] = jnp.concatenate(own + stations, axis=0).T.astype(BF16)


def tables_kernel(bins_ref, aperture_ref, lengths_ref, filters_ref, counts_ref, filtered_ref, codes_ref):
    shots = aperture_ref.shape[0]
    half = lax.axis_index("freq")
    lane = lax.broadcasted_iota(jnp.int32, (shots, LANES), 1)
    group = lane // PIECE
    for s in range(shots):
        lists = aperture_ref[s, pl.ds(pl.multiple_of(half * PIECE, PIECE), PIECE), :]
        lists = jnp.concatenate([lists] * (LANES // PIECE), axis=0).T
        codes_ref[pl.ds(s, KMAX, stride=shots), :] = lists
    lengths = jnp.concatenate([lengths_ref[...]] * 2, axis=1)
    lengths = jnp.where(group % 2 == half, lengths, pltpu.roll(lengths, PIECE, 1))
    for k in range(KMAX):
        rows = pl.ds(k * shots, shots)
        codes_ref[rows, :] = jnp.where(lengths > k, codes_ref[rows, :] - group, -LANES)
    per_tile = LANES // PIECE
    for tile in range(counts_ref.shape[1] // LANES):
        count = jnp.zeros((shots, LANES), F32)
        for k in range(KMAX):
            hit = codes_ref[k * shots : (k + 1) * shots, :] == tile * per_tile
            count = count + jnp.where(hit, 1.0, 0.0)
        counts_ref[:, tile * LANES : (tile + 1) * LANES] = count

    shot_dev, _, time_dev = filtered_ref.shape
    width = time_dev + LANES
    basis, times = basis_in_kernel(bins_ref, half * time_dev - HALF, width)
    inside = (times >= 0) & (times < NT)
    inside = jnp.concatenate([inside, inside], axis=0)
    basis = jnp.where(inside, basis.astype(BF16).astype(F32), 0.0)
    taps = filters_ref[...].astype(F32)
    total = [jnp.zeros((2 * NF, time_dev), F32) for _ in range(shot_dev)]
    for j in range(TAPS):
        shift = 2 * HALF - j
        moved = basis if shift == 0 else pltpu.roll(basis, width - shift, 1)
        moved = moved[:, :time_dev]
        for s in range(shot_dev):
            total[s] = total[s] + taps[s : s + 1, j : j + 1] * moved
    for s in range(shot_dev):
        filtered_ref[s] = total[s].astype(BF16)


def product_kernel(received_ref, counts_ref, message_ref, station_ref, first_ref, second_ref):
    devices = received_ref.shape[0]
    groups = devices // 2
    lane = lax.broadcasted_iota(jnp.int32, (2 * NF, LANES), 1)
    for pair in range(groups // 2):
        sums = []
        for g in (2 * pair, 2 * pair + 1):
            total = received_ref[2 * g].astype(F32) + received_ref[2 * g + 1].astype(F32)
            rounded = total.astype(BF16)
            total = rounded.astype(F32)
            sums.append(total)
            station_ref[16 * g : 16 * g + 16, :] = rounded
            station_ref[16 * (groups + g) : 16 * (groups + g) + 16, :] = pltpu.roll(total, 96, 1).astype(BF16)
        second_ref[:, pair * LANES : (pair + 1) * LANES] = jnp.where(lane < 64, sums[0], pltpu.roll(sums[1], 64, 1))
    width = second_ref.shape[1]
    rows = lax.broadcasted_iota(jnp.int32, (LANES, width), 0)
    columns = lax.broadcasted_iota(jnp.int32, (LANES, width), 1)
    spread = jnp.where(rows - 2 * PIECE == columns // PIECE, 1.0, 0.0).astype(BF16)
    first_ref[...] = jnp.dot(station_ref[...], spread, preferred_element_type=F32)
    second_real, second_imag = second_ref[:NF, :], second_ref[NF:, :]
    group = lax.broadcasted_iota(jnp.int32, (NF, LANES), 1) // PIECE
    for g in range(groups):
        parts = []
        for odd in range(2):
            row = 16 * (odd * groups + g)
            first_real = first_ref[row : row + NF, :]
            first_imag = first_ref[row + NF : row + 2 * NF, :]
            count = counts_ref[2 * g + odd : 2 * g + odd + 1, :]
            real = count * (first_real * second_real - first_imag * second_imag)
            imag = count * (first_real * second_imag + first_imag * second_real)
            for part in (real, imag):
                total = part[:, :LANES]
                for tile in range(1, width // LANES):
                    total = total + part[:, tile * LANES : (tile + 1) * LANES]
                total = total + pltpu.roll(total, 64, 1)
                total = total + pltpu.roll(total, 32, 1)
                parts.append(total * KMAX ** (-0.5))
        message = jnp.where(group == 0, parts[0], parts[1])
        message = jnp.where(group == 2, parts[2], message)
        message = jnp.where(group == 3, parts[3], message)
        message_ref[16 * g : 16 * g + 16, :] = jnp.concatenate([message, message], axis=0).astype(BF16)


def synthesis_kernel(received_ref, filtered_ref, out_ref, spectra_ref):
    @pl.when((pl.program_id(0) == 0) & (pl.program_id(1) == 0))
    def _():
        group = lax.broadcasted_iota(jnp.int32, (NF, LANES), 1) // PIECE
        for tile in range(received_ref.shape[0] // 32):
            sources = []
            for pair in range(2):
                both = received_ref[32 * tile + 16 * pair : 32 * tile + 16 * pair + 16, :].astype(F32)
                sources += [both[:NF], both[NF:]]
            turned = [[x] + [pltpu.roll(x, 32 * m, 1) for m in range(1, 4)] for x in sources]
            for s in range(2):
                parts = []
                for c in range(2):
                    q = 2 * s + c
                    total = turned[0][(0 - q) % 4]
                    for i in range(1, 4):
                        total = jnp.where(group == i, turned[i][(i - q) % 4], total)
                    parts.append(total)
                spectra_ref[s, tile * LANES : (tile + 1) * LANES, :] = jnp.concatenate(parts, axis=0).T.astype(BF16)

    s, step = pl.program_id(0), pl.program_id(1)
    block = out_ref.shape[1]
    rows = spectra_ref[s, pl.ds(pl.multiple_of(step * block, block), block), :]
    out_ref[0] = jnp.dot(rows, filtered_ref[s], preferred_element_type=F32).astype(BF16)


def in_vmem():
    return pl.BlockSpec(memory_space=pltpu.VMEM)


def in_smem():
    return pl.BlockSpec(memory_space=pltpu.SMEM)


def shards(traces, frequency_bins, aperture, lengths, filters):
    shot_dev, receivers, time_dev = traces.shape
    devices = lax.axis_size("shot") * lax.axis_size("freq")
    shots = aperture.shape[0]
    params = pltpu.CompilerParams(vmem_limit_bytes=VMEM_LIMIT)

    block = 256
    messages = pl.pallas_call(
        analysis_kernel,
        grid=(receivers // block,),
        in_specs=[in_smem(), pl.BlockSpec((shot_dev, block, time_dev), lambda i: (0, i, 0))],
        out_specs=pl.BlockSpec((devices, 2 * NF, LANES), lambda i: (0, 0, 0)),
        out_shape=jax.ShapeDtypeStruct((devices, 2 * NF, LANES), BF16),
        scratch_shapes=[pltpu.VMEM((2 * NF, time_dev), BF16), pltpu.VMEM((shot_dev, receivers, 2 * NF), F32)],
        compiler_params=params,
        cost_estimate=pl.CostEstimate(flops=2 * 16 * traces.size, bytes_accessed=2 * traces.size, transcendentals=0),
    )(frequency_bins, traces)
    received = lax.all_to_all(messages, DEVICES, split_axis=0, concat_axis=0, tiled=True)

    counts, filtered = pl.pallas_call(
        tables_kernel,
        in_specs=[in_smem(), in_vmem(), in_vmem(), in_vmem()],
        out_specs=[in_vmem(), in_vmem()],
        out_shape=[
            jax.ShapeDtypeStruct((shots, receivers), F32),
            jax.ShapeDtypeStruct((shot_dev, 2 * NF, time_dev), BF16),
        ],
        scratch_shapes=[pltpu.VMEM((KMAX * shots, LANES), jnp.int32)],
        compiler_params=params,
        cost_estimate=pl.CostEstimate(flops=1 << 24, bytes_accessed=1 << 21, transcendentals=0),
    )(frequency_bins, aperture, lengths, filters)

    messages = pl.pallas_call(
        product_kernel,
        in_specs=[in_vmem(), in_vmem()],
        out_specs=in_vmem(),
        out_shape=jax.ShapeDtypeStruct((devices * NF, LANES), BF16),
        scratch_shapes=[
            pltpu.VMEM((devices * 2 * NF, LANES), BF16),
            pltpu.VMEM((devices * 2 * NF, receivers), F32),
            pltpu.VMEM((2 * NF, receivers), F32),
        ],
        compiler_params=params,
        cost_estimate=pl.CostEstimate(flops=1 << 23, bytes_accessed=1 << 19, transcendentals=0),
    )(received, counts)
    received = lax.all_to_all(
        messages.reshape(devices, NF, LANES), DEVICES, split_axis=0, concat_axis=0, tiled=True
    ).reshape(devices * NF, LANES)

    return pl.pallas_call(
        synthesis_kernel,
        grid=(shot_dev, receivers // block),
        in_specs=[in_vmem(), in_vmem()],
        out_specs=pl.BlockSpec((1, block, time_dev), lambda s, i: (s, i, 0)),
        out_shape=jax.ShapeDtypeStruct(traces.shape, BF16),
        scratch_shapes=[pltpu.VMEM((shot_dev, receivers, 2 * NF), BF16)],
        compiler_params=params,
        cost_estimate=pl.CostEstimate(flops=2 * 16 * traces.size, bytes_accessed=2 * traces.size, transcendentals=0),
    )(received, filtered)


def general_shards(traces, frequency_bins, aperture, lengths, filters):
    shot_dev, receivers, time_dev = traces.shape
    shots = aperture.shape[0]
    receiver_dev = aperture.shape[1]
    start = lax.axis_index("freq") * time_dev

    def basis_rows(times):
        cosines, sines = cosine_sine((frequency_bins[:, None] * times[None, :]) & (NT - 1))
        return jnp.stack([cosines, -sines], axis=1)

    times = start + jnp.arange(time_dev, dtype=jnp.int32)
    analysis = (basis_rows(times) * NT ** (-0.5)).astype(BF16).reshape(2 * NF, time_dev)
    term = lax.dot_general(
        analysis, traces.reshape(shot_dev * receivers, time_dev), (((1,), (1,)), ((), ())), preferred_element_type=F32
    )
    spectra = lax.psum_scatter(
        term.reshape(NF, 2, shot_dev, receivers), "freq", scatter_dimension=0, tiled=True
    ).astype(BF16)
    second = lax.all_to_all(spectra, "shot", split_axis=3, concat_axis=2, tiled=True).astype(F32)
    stations = spectra[:, :, :, :: receivers // shots]
    first = lax.all_gather(stations, "shot", axis=2, tiled=True).astype(F32)

    def one_shot(inputs):
        legs, lists, list_lengths = inputs
        used = jnp.arange(KMAX, dtype=jnp.int32)[None, :] < list_lengths[:, None]
        lists = jnp.where(used, lists, -1)
        hits = lists[None] == jnp.arange(shots, dtype=jnp.int32)[:, None, None]
        counts = hits.astype(F32).sum(axis=-1)
        legs = legs[..., None]
        real = legs[:, 0] * second[:, 0] - legs[:, 1] * second[:, 1]
        imag = legs[:, 0] * second[:, 1] + legs[:, 1] * second[:, 0]
        return (jnp.stack([real, imag], axis=1) * counts).sum(axis=2)

    summed = lax.map(one_shot, (first.transpose(2, 0, 1, 3), aperture, lengths))
    summed = (summed * KMAX ** (-0.5)).astype(BF16).transpose(1, 2, 0, 3)
    summed = lax.all_to_all(summed, "shot", split_axis=2, concat_axis=3, tiled=True)
    summed = lax.all_gather(summed, "freq", axis=0, tiled=True).reshape(2 * NF, shot_dev, receivers)

    wide = start - HALF + jnp.arange(time_dev + 2 * HALF, dtype=jnp.int32)
    synthesis = basis_rows(wide).astype(BF16).astype(F32).reshape(2 * NF, time_dev + 2 * HALF)
    synthesis = jnp.where((wide >= 0) & (wide < NT), synthesis, 0.0)
    filtered = jnp.zeros((shot_dev, 2 * NF, time_dev), F32)
    for j in range(TAPS):
        tap = filters[:, j].astype(F32)[:, None, None]
        filtered = filtered + tap * synthesis[:, 2 * HALF - j : 2 * HALF - j + time_dev]
    out = jnp.einsum("fsr,sft->srt", summed, filtered.astype(BF16), preferred_element_type=F32)
    return out.astype(BF16)


def solution(mesh):
    in_specs = (
        P("shot", None, "freq"),
        P(),
        P(None, "shot", None),
        P(None, "shot"),
        P("shot", None),
    )
    out_specs = P("shot", None, "freq")
    whole_pieces = mesh.shape["shot"] == 16 and mesh.shape["freq"] == 2
    body = shards if whole_pieces else general_shards
    return jax.shard_map(body, mesh=mesh, in_specs=in_specs, out_specs=out_specs, check_vma=False)
```

```python
import math

import jax
import jax.numpy as jnp
from jax import lax
from jax.experimental import pallas as pl
from jax.experimental.pallas import tpu as pltpu
from jax.sharding import PartitionSpec as P

NT = 1024
NF = 8
KMAX = 32
TAPS = 31
HALF = (TAPS - 1) // 2
LANES = 128
PIECE = 32
DEVICES = ("shot", "freq")
F32 = jnp.float32
BF16 = jnp.bfloat16
VMEM_LIMIT = 48 * 1024 * 1024


def cosine_sine(phases):
    quarter = NT // 4
    turn = (phases + quarter // 2) // quarter
    angle = (phases - turn * quarter).astype(F32) * (2.0 * math.pi / NT)
    square = angle * angle
    sine = angle * (1.0 + square * (-1 / 6 + square * (1 / 120 + square * (-1 / 5040 + square / 362880))))
    cosine = 1.0 + square * (-1 / 2 + square * (1 / 24 + square * (-1 / 720 + square / 40320)))
    odd = turn % 2 == 1
    near, far = jnp.where(odd, sine, cosine), jnp.where(odd, cosine, sine)
    return (
        jnp.where((turn == 1) | (turn == 2), -near, near),
        jnp.where((turn == 2) | (turn == 3), -far, far),
    )


def basis_in_kernel(bins_ref, first_time, width):
    rows = lax.broadcasted_iota(jnp.int32, (NF, width), 0)
    times = lax.broadcasted_iota(jnp.int32, (NF, width), 1) + first_time
    bins = jnp.zeros((NF, width), jnp.int32)
    for f in range(NF):
        bins = jnp.where(rows == f, bins_ref[f], bins)
    cosines, sines = cosine_sine((bins * times) & (NT - 1))
    return jnp.concatenate([cosines, -sines], axis=0), times


def analysis_kernel(bins_hbm, traces_hbm, message_ref, bins_ref, traces_ref, basis_ref, rows_ref, traces_sem, bins_sem):
    shot_dev, receivers, time_dev = traces_ref.shape
    steps = traces_sem.shape[0]
    block = receivers // steps
    bins_copy = pltpu.make_async_copy(bins_hbm, bins_ref, bins_sem)
    bins_copy.start()
    copies = []
    for i in range(steps):
        rows = pl.ds(i * block, block)
        copy = pltpu.make_async_copy(traces_hbm.at[:, rows, :], traces_ref.at[:, rows, :], traces_sem.at[i])
        copy.start()
        copies.append(copy)
    bins_copy.wait()
    basis, _ = basis_in_kernel(bins_ref, lax.axis_index("freq") * time_dev, time_dev)
    basis_ref[...] = (basis * NT ** (-0.5)).astype(BF16)
    for i in range(steps):
        copies[i].wait()
        columns = slice(i * block, (i + 1) * block)
        for s in range(shot_dev):
            rows_ref[s, :, columns] = lax.dot_general(
                basis_ref[...], traces_ref[s, columns, :], (((1,), (1,)), ((), ())), preferred_element_type=F32
            )

    lane = lax.broadcasted_iota(jnp.int32, (2 * NF, LANES), 1)
    group = lane // PIECE
    per_tile = LANES // PIECE
    stations = jnp.zeros((2 * NF, LANES), F32)
    for s in range(shot_dev):
        for tile in range(receivers // LANES):
            x = rows_ref[s, :, tile * LANES : (tile + 1) * LANES]
            for i in range(per_tile):
                target = (shot_dev + s) * PIECE + per_tile * tile + i
                stations = jnp.where(lane == target, pltpu.roll(x, (target - i * PIECE) % LANES, 1), stations)
    for tile in range(receivers // LANES):
        both = [rows_ref[s, :, tile * LANES : (tile + 1) * LANES] for s in range(shot_dev)]
        for i in range(per_tile):
            message = stations
            for s in range(shot_dev):
                shift = (s - i) * PIECE % LANES
                moved = pltpu.roll(both[s], shift, 1) if shift else both[s]
                message = jnp.where(group == s, moved, message)
            message_ref[per_tile * tile + i] = message.astype(BF16)


def tables_kernel(bins_ref, aperture_ref, lengths_ref, filters_ref, counts_ref, filtered_ref, codes_ref):
    shots = aperture_ref.shape[0]
    half = lax.axis_index("freq")
    lane = lax.broadcasted_iota(jnp.int32, (shots, LANES), 1)
    group = lane // PIECE

    def own_half(rows):
        rows = jnp.concatenate([rows, rows], axis=1)
        return jnp.where(group % 2 == half, rows, pltpu.roll(rows, PIECE, 1))

    for s in range(shots):
        codes_ref[pl.ds(s, KMAX, stride=shots), :] = own_half(aperture_ref[s])
    lengths = own_half(lengths_ref[...])
    for k in range(KMAX):
        rows = pl.ds(k * shots, shots)
        codes_ref[rows, :] = jnp.where(lengths > k, codes_ref[rows, :] - group, -LANES)
    per_tile = LANES // PIECE
    for tile in range(counts_ref.shape[1] // LANES):
        count = jnp.zeros((shots, LANES), F32)
        for k in range(KMAX):
            hit = codes_ref[k * shots : (k + 1) * shots, :] == tile * per_tile
            count = count + jnp.where(hit, 1.0, 0.0)
        counts_ref[:, tile * LANES : (tile + 1) * LANES] = count

    shot_dev, _, time_dev = filtered_ref.shape
    width = time_dev + LANES
    basis, times = basis_in_kernel(bins_ref, half * time_dev - HALF, width)
    inside = (times >= 0) & (times < NT)
    inside = jnp.concatenate([inside, inside], axis=0)
    basis = jnp.where(inside, basis.astype(BF16).astype(F32), 0.0)
    taps = filters_ref[...].astype(F32)
    total = [jnp.zeros((2 * NF, time_dev), F32) for _ in range(shot_dev)]
    for j in range(TAPS):
        shift = 2 * HALF - j
        moved = basis if shift == 0 else pltpu.roll(basis, width - shift, 1)
        moved = moved[:, :time_dev]
        for s in range(shot_dev):
            total[s] = total[s] + taps[s : s + 1, j : j + 1] * moved
    for s in range(shot_dev):
        filtered_ref[s] = total[s].astype(BF16)


def product_kernel(received_ref, counts_ref, message_ref, station_ref, first_ref, second_ref):
    devices = received_ref.shape[0]
    groups = devices // 2
    lane = lax.broadcasted_iota(jnp.int32, (2 * NF, LANES), 1)
    for pair in range(groups // 2):
        sums = []
        for g in (2 * pair, 2 * pair + 1):
            total = received_ref[2 * g].astype(F32) + received_ref[2 * g + 1].astype(F32)
            rounded = total.astype(BF16)
            total = rounded.astype(F32)
            sums.append(total)
            station_ref[16 * g : 16 * g + 16, :] = rounded
            station_ref[16 * (groups + g) : 16 * (groups + g) + 16, :] = pltpu.roll(total, 96, 1).astype(BF16)
        second_ref[:, pair * LANES : (pair + 1) * LANES] = jnp.where(lane < 64, sums[0], pltpu.roll(sums[1], 64, 1))
    width = second_ref.shape[1]
    rows = lax.broadcasted_iota(jnp.int32, (LANES, width), 0)
    columns = lax.broadcasted_iota(jnp.int32, (LANES, width), 1)
    spread = jnp.where(rows - 2 * PIECE == columns // PIECE, 1.0, 0.0).astype(BF16)
    first_ref[...] = jnp.dot(station_ref[...], spread, preferred_element_type=F32)
    second_real, second_imag = second_ref[:NF, :], second_ref[NF:, :]
    group = lax.broadcasted_iota(jnp.int32, (NF, LANES), 1) // PIECE
    for g in range(groups):
        parts = []
        for odd in range(2):
            row = 16 * (odd * groups + g)
            first_real = first_ref[row : row + NF, :]
            first_imag = first_ref[row + NF : row + 2 * NF, :]
            count = counts_ref[2 * g + odd : 2 * g + odd + 1, :]
            real = count * (first_real * second_real - first_imag * second_imag)
            imag = count * (first_real * second_imag + first_imag * second_real)
            for part in (real, imag):
                total = part[:, :LANES]
                for tile in range(1, width // LANES):
                    total = total + part[:, tile * LANES : (tile + 1) * LANES]
                total = total + pltpu.roll(total, 64, 1)
                total = total + pltpu.roll(total, 32, 1)
                parts.append(total * KMAX ** (-0.5))
        message = jnp.where(group == 0, parts[0], parts[1])
        message = jnp.where(group == 2, parts[2], message)
        message = jnp.where(group == 3, parts[3], message)
        message_ref[16 * g : 16 * g + 16, :] = jnp.concatenate([message, message], axis=0).astype(BF16)


def synthesis_kernel(received_ref, filtered_ref, out_hbm, out_ref, out_sem):
    group = lax.broadcasted_iota(jnp.int32, (NF, LANES), 1) // PIECE
    copies = []
    for tile in range(received_ref.shape[0] // 32):
        sources = []
        for pair in range(2):
            both = received_ref[32 * tile + 16 * pair : 32 * tile + 16 * pair + 16, :].astype(F32)
            sources += [both[:NF], both[NF:]]
        turned = [[x] + [pltpu.roll(x, 32 * m, 1) for m in range(1, 4)] for x in sources]
        rows = pl.ds(tile * LANES, LANES)
        for s in range(2):
            parts = []
            for c in range(2):
                q = 2 * s + c
                total = turned[0][(0 - q) % 4]
                for i in range(1, 4):
                    total = jnp.where(group == i, turned[i][(i - q) % 4], total)
                parts.append(total)
            spectra = jnp.concatenate(parts, axis=0).T.astype(BF16)
            out_ref[s, rows, :] = jnp.dot(spectra, filtered_ref[s], preferred_element_type=F32).astype(BF16)
            copy = pltpu.make_async_copy(out_ref.at[s, rows, :], out_hbm.at[s, rows, :], out_sem.at[2 * tile + s])
            copy.start()
            copies.append(copy)
    for copy in copies:
        copy.wait()


def in_vmem():
    return pl.BlockSpec(memory_space=pltpu.VMEM)


def in_hbm():
    return pl.BlockSpec(memory_space=pltpu.HBM)


def in_smem():
    return pl.BlockSpec(memory_space=pltpu.SMEM)


def shards(traces, frequency_bins, aperture, lengths, filters):
    shot_dev, receivers, time_dev = traces.shape
    devices = lax.axis_size("shot") * lax.axis_size("freq")
    shots = aperture.shape[0]
    params = pltpu.CompilerParams(vmem_limit_bytes=VMEM_LIMIT)

    steps = 4
    messages = pl.pallas_call(
        analysis_kernel,
        in_specs=[in_hbm(), in_hbm()],
        out_specs=in_vmem(),
        out_shape=jax.ShapeDtypeStruct((devices, 2 * NF, LANES), BF16),
        scratch_shapes=[
            pltpu.SMEM((NF,), jnp.int32),
            pltpu.VMEM(traces.shape, BF16),
            pltpu.VMEM((2 * NF, time_dev), BF16),
            pltpu.VMEM((shot_dev, 2 * NF, receivers), F32),
            pltpu.SemaphoreType.DMA((steps,)),
            pltpu.SemaphoreType.DMA,
        ],
        compiler_params=params,
        cost_estimate=pl.CostEstimate(flops=2 * 16 * traces.size, bytes_accessed=2 * traces.size, transcendentals=0),
    )(
        pltpu.with_memory_space_constraint(frequency_bins, pltpu.HBM),
        pltpu.with_memory_space_constraint(traces, pltpu.HBM),
    )
    received = lax.all_to_all(messages, DEVICES, split_axis=0, concat_axis=0, tiled=True)

    counts, filtered = pl.pallas_call(
        tables_kernel,
        in_specs=[in_smem(), in_vmem(), in_vmem(), in_vmem()],
        out_specs=[in_vmem(), in_vmem()],
        out_shape=[
            jax.ShapeDtypeStruct((shots, receivers), F32),
            jax.ShapeDtypeStruct((shot_dev, 2 * NF, time_dev), BF16),
        ],
        scratch_shapes=[pltpu.VMEM((KMAX * shots, LANES), jnp.int32)],
        compiler_params=params,
        cost_estimate=pl.CostEstimate(flops=1 << 24, bytes_accessed=1 << 21, transcendentals=0),
    )(frequency_bins, aperture.transpose(0, 2, 1), lengths, filters)

    messages = pl.pallas_call(
        product_kernel,
        in_specs=[in_vmem(), in_vmem()],
        out_specs=in_vmem(),
        out_shape=jax.ShapeDtypeStruct((devices * NF, LANES), BF16),
        scratch_shapes=[
            pltpu.VMEM((devices * 2 * NF, LANES), BF16),
            pltpu.VMEM((devices * 2 * NF, receivers), F32),
            pltpu.VMEM((2 * NF, receivers), F32),
        ],
        compiler_params=params,
        cost_estimate=pl.CostEstimate(flops=1 << 23, bytes_accessed=1 << 19, transcendentals=0),
    )(received, counts)
    received = lax.all_to_all(
        messages.reshape(devices, NF, LANES), DEVICES, split_axis=0, concat_axis=0, tiled=True
    ).reshape(devices * NF, LANES)

    return pl.pallas_call(
        synthesis_kernel,
        in_specs=[in_vmem(), in_vmem()],
        out_specs=in_hbm(),
        out_shape=jax.ShapeDtypeStruct(traces.shape, BF16),
        scratch_shapes=[
            pltpu.VMEM(traces.shape, BF16),
            pltpu.SemaphoreType.DMA((shot_dev * receivers // LANES,)),
        ],
        compiler_params=params,
        cost_estimate=pl.CostEstimate(flops=2 * 16 * traces.size, bytes_accessed=2 * traces.size, transcendentals=0),
    )(received, filtered)


def general_shards(traces, frequency_bins, aperture, lengths, filters):
    shot_dev, receivers, time_dev = traces.shape
    shots = aperture.shape[0]
    receiver_dev = aperture.shape[1]
    start = lax.axis_index("freq") * time_dev

    def basis_rows(times):
        cosines, sines = cosine_sine((frequency_bins[:, None] * times[None, :]) & (NT - 1))
        return jnp.stack([cosines, -sines], axis=1)

    times = start + jnp.arange(time_dev, dtype=jnp.int32)
    analysis = (basis_rows(times) * NT ** (-0.5)).astype(BF16).reshape(2 * NF, time_dev)
    term = lax.dot_general(
        analysis, traces.reshape(shot_dev * receivers, time_dev), (((1,), (1,)), ((), ())), preferred_element_type=F32
    )
    spectra = lax.psum_scatter(
        term.reshape(NF, 2, shot_dev, receivers), "freq", scatter_dimension=0, tiled=True
    ).astype(BF16)
    second = lax.all_to_all(spectra, "shot", split_axis=3, concat_axis=2, tiled=True).astype(F32)
    stations = spectra[:, :, :, :: receivers // shots]
    first = lax.all_gather(stations, "shot", axis=2, tiled=True).astype(F32)

    def one_shot(inputs):
        legs, lists, list_lengths = inputs
        used = jnp.arange(KMAX, dtype=jnp.int32)[None, :] < list_lengths[:, None]
        lists = jnp.where(used, lists, -1)
        hits = lists[None] == jnp.arange(shots, dtype=jnp.int32)[:, None, None]
        counts = hits.astype(F32).sum(axis=-1)
        legs = legs[..., None]
        real = legs[:, 0] * second[:, 0] - legs[:, 1] * second[:, 1]
        imag = legs[:, 0] * second[:, 1] + legs[:, 1] * second[:, 0]
        return (jnp.stack([real, imag], axis=1) * counts).sum(axis=2)

    summed = lax.map(one_shot, (first.transpose(2, 0, 1, 3), aperture, lengths))
    summed = (summed * KMAX ** (-0.5)).astype(BF16).transpose(1, 2, 0, 3)
    summed = lax.all_to_all(summed, "shot", split_axis=2, concat_axis=3, tiled=True)
    summed = lax.all_gather(summed, "freq", axis=0, tiled=True).reshape(2 * NF, shot_dev, receivers)

    wide = start - HALF + jnp.arange(time_dev + 2 * HALF, dtype=jnp.int32)
    synthesis = basis_rows(wide).astype(BF16).astype(F32).reshape(2 * NF, time_dev + 2 * HALF)
    synthesis = jnp.where((wide >= 0) & (wide < NT), synthesis, 0.0)
    filtered = jnp.zeros((shot_dev, 2 * NF, time_dev), F32)
    for j in range(TAPS):
        tap = filters[:, j].astype(F32)[:, None, None]
        filtered = filtered + tap * synthesis[:, 2 * HALF - j : 2 * HALF - j + time_dev]
    out = jnp.einsum("fsr,sft->srt", summed, filtered.astype(BF16), preferred_element_type=F32)
    return out.astype(BF16)


def solution(mesh):
    in_specs = (
        P("shot", None, "freq"),
        P(),
        P(None, "shot", None),
        P(None, "shot"),
        P("shot", None),
    )
    out_specs = P("shot", None, "freq")
    whole_pieces = mesh.shape["shot"] == 16 and mesh.shape["freq"] == 2
    body = shards if whole_pieces else general_shards
    return jax.shard_map(body, mesh=mesh, in_specs=in_specs, out_specs=out_specs, check_vma=False)
```

```python
import math

import jax
import jax.numpy as jnp
from jax import lax
from jax.experimental import pallas as pl
from jax.experimental.pallas import tpu as pltpu
from jax.sharding import PartitionSpec as P

NT = 1024
NF = 8
KMAX = 32
TAPS = 31
HALF = (TAPS - 1) // 2
LANES = 128
PIECE = 32
DEVICES = ("shot", "freq")
F32 = jnp.float32
BF16 = jnp.bfloat16
VMEM_LIMIT = 48 * 1024 * 1024


def cosine(phases):
    quarter = NT // 4
    turn = (phases + quarter // 2) // quarter
    angle = (phases - turn * quarter).astype(F32) * (2.0 * math.pi / NT)
    square = angle * angle
    sine = angle * (1.0 + square * (-1 / 6 + square * (1 / 120 + square * (-1 / 5040 + square / 362880))))
    cosine = 1.0 + square * (-1 / 2 + square * (1 / 24 + square * (-1 / 720 + square / 40320)))
    near = jnp.where(turn % 2 == 1, sine, cosine)
    return jnp.where((turn == 1) | (turn == 2), -near, near)


def basis_in_kernel(bins_ref, first_time, width):
    rows = lax.broadcasted_iota(jnp.int32, (2 * NF, width), 0)
    times = lax.broadcasted_iota(jnp.int32, (2 * NF, width), 1) + first_time
    frequency = rows // NF * (NF // 2) + rows % (NF // 2)
    part = rows // (NF // 2) % 2
    bins = jnp.zeros((2 * NF, width), jnp.int32)
    for f in range(NF):
        bins = jnp.where(frequency == f, bins_ref[f], bins)
    return cosine((bins * times + part * (NT // 4)) & (NT - 1)), times


def analysis_kernel(bins_hbm, traces_hbm, message_ref, bins_ref, traces_ref, basis_ref, traces_sem, bins_sem):
    shot_dev, receivers, time_dev = traces_ref.shape
    steps = traces_sem.shape[0]
    block = receivers // steps
    bins_copy = pltpu.make_async_copy(bins_hbm, bins_ref, bins_sem)
    bins_copy.start()
    copies = []
    for i in range(steps):
        rows = pl.ds(i * block, block)
        copy = pltpu.make_async_copy(traces_hbm.at[:, rows, :], traces_ref.at[:, rows, :], traces_sem.at[i])
        copy.start()
        copies.append(copy)
    bins_copy.wait()
    basis, _ = basis_in_kernel(bins_ref, lax.axis_index("freq") * time_dev, time_dev)
    basis_ref[...] = (basis * NT ** (-0.5)).astype(BF16)

    lane = lax.broadcasted_iota(jnp.int32, (2 * NF, LANES), 1)
    row = lax.broadcasted_iota(jnp.int32, (2 * NF, LANES), 0)
    low = lane < LANES // 2
    is_station = lane % PIECE == 0
    stations = jnp.zeros((2 * NF, LANES), F32)
    for i in range(steps):
        copies[i].wait()
        terms = [
            lax.dot_general(
                basis_ref[...],
                traces_ref[s, i * block : (i + 1) * block, :],
                (((1,), (1,)), ((), ())),
                preferred_element_type=F32,
            )
            for s in range(shot_dev)
        ]
        for j in range(block // LANES):
            tile = i * (block // LANES) + j
            first, second = [x[:, j * LANES : (j + 1) * LANES] for x in terms]
            for s, x in enumerate((first, second)):
                marked = jnp.where(is_station, x, 0.0)
                shift = 8 * s + tile
                stations = stations + (pltpu.roll(marked, shift, 1) if shift else marked)
            even = jnp.where(low, first, pltpu.roll(second, LANES // 2, 1))
            odd = jnp.where(low, pltpu.roll(first, LANES // 2, 1), second)
            for g, x in ((2 * tile, even), (2 * tile + 1, odd)):
                for h in range(2):
                    message_ref[2 * g + h, 0] = x[8 * h : 8 * h + 4].astype(BF16)
                    message_ref[2 * g + h, 1] = x[8 * h + 4 : 8 * h + 8].astype(BF16)
    stations = jnp.where(row // 4 % 2 == 1, pltpu.roll(stations, 16, 1), stations)
    for h in range(2):
        slab = (stations[8 * h : 8 * h + 4] + stations[8 * h + 4 : 8 * h + 8]).astype(BF16)
        for g in range(message_ref.shape[0] // 2):
            message_ref[2 * g + h, 2] = slab


def tables_kernel(bins_ref, aperture_ref, lengths_ref, filters_ref, counts_ref, spread_ref, filtered_ref, codes_ref):
    shots = aperture_ref.shape[0]
    tiles = counts_ref.shape[1] // LANES
    for s in range(shots):
        lists = aperture_ref[s]
        codes_ref[pl.ds(s, KMAX, stride=shots), :] = jnp.concatenate([lists, lists], axis=1)
    lengths = jnp.concatenate([lengths_ref[...]] * 2, axis=1)
    upper = lax.broadcasted_iota(jnp.int32, (shots, LANES), 1) // (LANES // 2)
    totals = [jnp.zeros((shots, LANES), BF16) for _ in range(tiles)]
    for k in range(KMAX):
        codes = codes_ref[k * shots : (k + 1) * shots, :]
        codes = jnp.where(lengths > k, codes - upper, -LANES).astype(F32).astype(BF16)
        for tile in range(tiles):
            hit = jnp.where(codes == BF16(2 * tile), BF16(1.0), BF16(0.0))
            totals[tile] = totals[tile] + hit
    for tile in range(tiles):
        counts_ref[:, tile * LANES : (tile + 1) * LANES] = totals[tile].astype(F32)

    lane = lax.broadcasted_iota(jnp.int32, (LANES, LANES), 0)
    station = lane % PIECE * 4 + lane // PIECE - lax.broadcasted_iota(jnp.int32, (LANES, LANES), 1) // (LANES // 2)
    for tile in range(tiles):
        here = jnp.where(station == 2 * tile, 1.0, 0.0)
        spread_ref[:, tile * LANES : (tile + 1) * LANES] = here.astype(BF16)

    shot_dev, _, time_dev = filtered_ref.shape
    width = time_dev + LANES
    basis, times = basis_in_kernel(bins_ref, lax.axis_index("freq") * time_dev - HALF, width)
    basis = jnp.where((times >= 0) & (times < NT), basis.astype(BF16).astype(F32), 0.0)
    taps = filters_ref[...].astype(F32)
    total = [jnp.zeros((2 * NF, time_dev), F32) for _ in range(shot_dev)]
    for j in range(TAPS):
        shift = 2 * HALF - j
        moved = basis if shift == 0 else pltpu.roll(basis, width - shift, 1)
        moved = moved[:, :time_dev]
        for s in range(shot_dev):
            total[s] = total[s] + taps[s : s + 1, j : j + 1] * moved
    for s in range(shot_dev):
        filtered_ref[s] = total[s].astype(BF16)


def product_kernel(received_ref, counts_ref, spread_ref, message_ref, station_ref, first_ref, second_ref):
    groups = received_ref.shape[0] // 2
    for g in range(groups):
        rounded = (received_ref[2 * g].astype(F32) + received_ref[2 * g + 1].astype(F32)).astype(BF16).astype(F32)
        second_ref[:, g * LANES : (g + 1) * LANES] = jnp.concatenate([rounded[0], rounded[1]], axis=0)
        legs = [rounded[2]] + [pltpu.roll(rounded[2], LANES - shift, 1) for shift in (16, 8, 24)]
        station_ref[16 * g : 16 * g + 16, :] = jnp.concatenate(legs, axis=0).astype(BF16)
    first_ref[...] = jnp.dot(station_ref[...], spread_ref[...], preferred_element_type=F32)
    second = second_ref[...]
    crossed = jnp.concatenate([second[4:], second[:4]], axis=0)
    upper = lax.broadcasted_iota(jnp.int32, (NF, LANES), 0) >= 4
    low = lax.broadcasted_iota(jnp.int32, (NF, LANES), 1) < LANES // 2

    def total(x):
        x = sum(x[:, i * LANES : (i + 1) * LANES] for i in range(x.shape[1] // LANES))
        return x + pltpu.roll(x, LANES // 2, 1)

    for g in range(groups):
        spectra = []
        for s in (2 * g, 2 * g + 1):
            first = counts_ref[s : s + 1, :] * first_ref[8 * s : 8 * s + 8, :]
            same, other = total(first * second), total(first * crossed)
            same, other = same - pltpu.roll(same, 4, 0), other + pltpu.roll(other, 4, 0)
            spectra.append(jnp.where(upper, other, same) * KMAX ** (-0.5))
        message = jnp.where(low, spectra[0], spectra[1])
        message_ref[16 * g : 16 * g + 16, :] = jnp.concatenate([message, message], axis=0).astype(BF16)


def synthesis_kernel(received_ref, filtered_ref, out_hbm, out_ref, out_sem):
    low = lax.broadcasted_iota(jnp.int32, (2 * NF, LANES), 1) < LANES // 2
    copies = []
    for tile in range(out_ref.shape[1] // LANES):
        left, right = [received_ref[32 * tile + i : 32 * tile + i + 16, :].astype(F32) for i in (0, 16)]
        spectra = (
            jnp.where(low, left, pltpu.roll(right, LANES // 2, 1)),
            jnp.where(low, pltpu.roll(left, LANES // 2, 1), right),
        )
        rows = pl.ds(tile * LANES, LANES)
        for s in range(2):
            out_ref[s, rows, :] = jnp.dot(
                spectra[s].T.astype(BF16), filtered_ref[s], preferred_element_type=F32
            ).astype(BF16)
            copy = pltpu.make_async_copy(out_ref.at[s, rows, :], out_hbm.at[s, rows, :], out_sem.at[2 * tile + s])
            copy.start()
            copies.append(copy)
    for copy in copies:
        copy.wait()


def in_vmem():
    return pl.BlockSpec(memory_space=pltpu.VMEM)


def in_hbm():
    return pl.BlockSpec(memory_space=pltpu.HBM)


def in_smem():
    return pl.BlockSpec(memory_space=pltpu.SMEM)


def shards(traces, frequency_bins, aperture, lengths, filters):
    shot_dev, receivers, time_dev = traces.shape
    devices = lax.axis_size("shot") * lax.axis_size("freq")
    shots = aperture.shape[0]
    params = pltpu.CompilerParams(vmem_limit_bytes=VMEM_LIMIT)

    steps = 2
    messages = pl.pallas_call(
        analysis_kernel,
        in_specs=[in_hbm(), in_hbm()],
        out_specs=in_vmem(),
        out_shape=jax.ShapeDtypeStruct((devices, 3, NF // 2, LANES), BF16),
        scratch_shapes=[
            pltpu.SMEM((NF,), jnp.int32),
            pltpu.VMEM(traces.shape, BF16),
            pltpu.VMEM((2 * NF, time_dev), BF16),
            pltpu.SemaphoreType.DMA((steps,)),
            pltpu.SemaphoreType.DMA,
        ],
        compiler_params=params,
        cost_estimate=pl.CostEstimate(flops=2 * 16 * traces.size, bytes_accessed=2 * traces.size, transcendentals=0),
    )(
        pltpu.with_memory_space_constraint(frequency_bins, pltpu.HBM),
        pltpu.with_memory_space_constraint(traces, pltpu.HBM),
    )
    received = lax.all_to_all(messages, DEVICES, split_axis=0, concat_axis=0, tiled=True)

    pairs = shots * aperture.shape[1]
    counts, spread, filtered = pl.pallas_call(
        tables_kernel,
        in_specs=[in_smem(), in_vmem(), in_vmem(), in_vmem()],
        out_specs=[in_vmem(), in_vmem(), in_vmem()],
        out_shape=[
            jax.ShapeDtypeStruct((shots, pairs), F32),
            jax.ShapeDtypeStruct((LANES, pairs), BF16),
            jax.ShapeDtypeStruct((shot_dev, 2 * NF, time_dev), BF16),
        ],
        scratch_shapes=[pltpu.VMEM((KMAX * shots, LANES), jnp.int32)],
        compiler_params=params,
        cost_estimate=pl.CostEstimate(flops=1 << 24, bytes_accessed=1 << 21, transcendentals=0),
    )(frequency_bins, aperture.transpose(0, 2, 1), lengths, filters)

    messages = pl.pallas_call(
        product_kernel,
        in_specs=[in_vmem(), in_vmem(), in_vmem()],
        out_specs=in_vmem(),
        out_shape=jax.ShapeDtypeStruct((devices * NF, LANES), BF16),
        scratch_shapes=[
            pltpu.VMEM((shots * NF, LANES), BF16),
            pltpu.VMEM((shots * NF, pairs), F32),
            pltpu.VMEM((NF, pairs), F32),
        ],
        compiler_params=params,
        cost_estimate=pl.CostEstimate(flops=1 << 23, bytes_accessed=1 << 19, transcendentals=0),
    )(received, counts, spread)
    received = lax.all_to_all(
        messages.reshape(devices, NF, LANES), DEVICES, split_axis=0, concat_axis=0, tiled=True
    ).reshape(devices * NF, LANES)

    return pl.pallas_call(
        synthesis_kernel,
        in_specs=[in_vmem(), in_vmem()],
        out_specs=in_hbm(),
        out_shape=jax.ShapeDtypeStruct(traces.shape, BF16),
        scratch_shapes=[
            pltpu.VMEM(traces.shape, BF16),
            pltpu.SemaphoreType.DMA((shot_dev * receivers // LANES,)),
        ],
        compiler_params=params,
        cost_estimate=pl.CostEstimate(flops=2 * 16 * traces.size, bytes_accessed=2 * traces.size, transcendentals=0),
    )(received, filtered)


def general_shards(traces, frequency_bins, aperture, lengths, filters):
    shot_dev, receivers, time_dev = traces.shape
    shots = aperture.shape[0]
    receiver_dev = aperture.shape[1]
    start = lax.axis_index("freq") * time_dev

    def basis_rows(times):
        phases = frequency_bins[:, None] * times[None, :]
        return jnp.stack([cosine(phases & (NT - 1)), cosine((phases + NT // 4) & (NT - 1))], axis=1)

    times = start + jnp.arange(time_dev, dtype=jnp.int32)
    analysis = (basis_rows(times) * NT ** (-0.5)).astype(BF16).reshape(2 * NF, time_dev)
    term = lax.dot_general(
        analysis, traces.reshape(shot_dev * receivers, time_dev), (((1,), (1,)), ((), ())), preferred_element_type=F32
    )
    spectra = lax.psum_scatter(
        term.reshape(NF, 2, shot_dev, receivers), "freq", scatter_dimension=0, tiled=True
    ).astype(BF16)
    second = lax.all_to_all(spectra, "shot", split_axis=3, concat_axis=2, tiled=True).astype(F32)
    stations = spectra[:, :, :, :: receivers // shots]
    first = lax.all_gather(stations, "shot", axis=2, tiled=True).astype(F32)

    def one_shot(inputs):
        legs, lists, list_lengths = inputs
        used = jnp.arange(KMAX, dtype=jnp.int32)[None, :] < list_lengths[:, None]
        lists = jnp.where(used, lists, -1)
        hits = lists[None] == jnp.arange(shots, dtype=jnp.int32)[:, None, None]
        counts = hits.astype(F32).sum(axis=-1)
        legs = legs[..., None]
        real = legs[:, 0] * second[:, 0] - legs[:, 1] * second[:, 1]
        imag = legs[:, 0] * second[:, 1] + legs[:, 1] * second[:, 0]
        return (jnp.stack([real, imag], axis=1) * counts).sum(axis=2)

    summed = lax.map(one_shot, (first.transpose(2, 0, 1, 3), aperture, lengths))
    summed = (summed * KMAX ** (-0.5)).astype(BF16).transpose(1, 2, 0, 3)
    summed = lax.all_to_all(summed, "shot", split_axis=2, concat_axis=3, tiled=True)
    summed = lax.all_gather(summed, "freq", axis=0, tiled=True).reshape(2 * NF, shot_dev, receivers)

    wide = start - HALF + jnp.arange(time_dev + 2 * HALF, dtype=jnp.int32)
    synthesis = basis_rows(wide).astype(BF16).astype(F32).reshape(2 * NF, time_dev + 2 * HALF)
    synthesis = jnp.where((wide >= 0) & (wide < NT), synthesis, 0.0)
    filtered = jnp.zeros((shot_dev, 2 * NF, time_dev), F32)
    for j in range(TAPS):
        tap = filters[:, j].astype(F32)[:, None, None]
        filtered = filtered + tap * synthesis[:, 2 * HALF - j : 2 * HALF - j + time_dev]
    out = jnp.einsum("fsr,sft->srt", summed, filtered.astype(BF16), preferred_element_type=F32)
    return out.astype(BF16)


def solution(mesh):
    in_specs = (
        P("shot", None, "freq"),
        P(),
        P(None, "shot", None),
        P(None, "shot"),
        P("shot", None),
    )
    out_specs = P("shot", None, "freq")
    whole_pieces = mesh.shape["shot"] == 16 and mesh.shape["freq"] == 2
    body = shards if whole_pieces else general_shards
    return jax.shard_map(body, mesh=mesh, in_specs=in_specs, out_specs=out_specs, check_vma=False)
```

```python
import math

import jax
import jax.numpy as jnp
from jax import lax
from jax.experimental import pallas as pl
from jax.experimental.pallas import tpu as pltpu
from jax.sharding import PartitionSpec as P

NT = 1024
NF = 8
KMAX = 32
TAPS = 31
HALF = (TAPS - 1) // 2
LANES = 128
PIECE = 32
DEVICES = ("shot", "freq")
F32 = jnp.float32
BF16 = jnp.bfloat16
VMEM_LIMIT = 48 * 1024 * 1024


def cosine(phases):
    quarter = NT // 4
    turn = (phases + quarter // 2) // quarter
    angle = (phases - turn * quarter).astype(F32) * (2.0 * math.pi / NT)
    square = angle * angle
    sine = angle * (1.0 + square * (-1 / 6 + square * (1 / 120 + square * (-1 / 5040 + square / 362880))))
    cosine = 1.0 + square * (-1 / 2 + square * (1 / 24 + square * (-1 / 720 + square / 40320)))
    near = jnp.where(turn % 2 == 1, sine, cosine)
    return jnp.where((turn == 1) | (turn == 2), -near, near)


def basis_in_kernel(bins_ref, first_time, width):
    rows = lax.broadcasted_iota(jnp.int32, (2 * NF, width), 0)
    times = lax.broadcasted_iota(jnp.int32, (2 * NF, width), 1) + first_time
    frequency = rows // NF * (NF // 2) + rows % (NF // 2)
    part = rows // (NF // 2) % 2
    bins = jnp.zeros((2 * NF, width), jnp.int32)
    for f in range(NF):
        bins = jnp.where(frequency == f, bins_ref[f], bins)
    return cosine((bins * times + part * (NT // 4)) & (NT - 1)), times


def analysis_kernel(bins_hbm, traces_hbm, message_ref, bins_ref, traces_ref, basis_ref, traces_sem, bins_sem):
    shot_dev, receivers, time_dev = traces_ref.shape
    starts = [0, 3 * LANES, receivers]
    blocks = list(zip(starts, starts[1:]))
    bins_copy = pltpu.make_async_copy(bins_hbm, bins_ref, bins_sem)
    bins_copy.start()
    copies = []
    for i, (start, end) in enumerate(blocks):
        rows = pl.ds(start, end - start)
        copy = pltpu.make_async_copy(traces_hbm.at[:, rows, :], traces_ref.at[:, rows, :], traces_sem.at[i])
        copy.start()
        copies.append(copy)
    bins_copy.wait()
    basis, _ = basis_in_kernel(bins_ref, lax.axis_index("freq") * time_dev, time_dev)
    basis_ref[...] = (basis * NT ** (-0.5)).astype(BF16)

    lane = lax.broadcasted_iota(jnp.int32, (2 * NF, LANES), 1)
    row = lax.broadcasted_iota(jnp.int32, (2 * NF, LANES), 0)
    low = lane < LANES // 2
    is_station = lane % PIECE == 0
    stations = jnp.zeros((2 * NF, LANES), F32)
    for copy, (start, end) in zip(copies, blocks):
        copy.wait()
        terms = [
            lax.dot_general(
                basis_ref[...],
                traces_ref[s, start:end, :],
                (((1,), (1,)), ((), ())),
                preferred_element_type=F32,
            )
            for s in range(shot_dev)
        ]
        for j in range((end - start) // LANES):
            tile = start // LANES + j
            first, second = [x[:, j * LANES : (j + 1) * LANES] for x in terms]
            for s, x in enumerate((first, second)):
                marked = jnp.where(is_station, x, 0.0)
                shift = 8 * s + tile
                stations = stations + (pltpu.roll(marked, shift, 1) if shift else marked)
            even = jnp.where(low, first, pltpu.roll(second, LANES // 2, 1))
            odd = jnp.where(low, pltpu.roll(first, LANES // 2, 1), second)
            for g, x in ((2 * tile, even), (2 * tile + 1, odd)):
                for h in range(2):
                    message_ref[2 * g + h, 0] = x[8 * h : 8 * h + 4].astype(BF16)
                    message_ref[2 * g + h, 1] = x[8 * h + 4 : 8 * h + 8].astype(BF16)
    stations = jnp.where(row // 4 % 2 == 1, pltpu.roll(stations, 16, 1), stations)
    for h in range(2):
        slab = (stations[8 * h : 8 * h + 4] + stations[8 * h + 4 : 8 * h + 8]).astype(BF16)
        for g in range(message_ref.shape[0] // 2):
            message_ref[2 * g + h, 2] = slab


def tables_kernel(
    bins_hbm, filters_hbm, lengths_hbm, aperture_hbm, counts_ref, spread_ref, filtered_ref,
    bins_ref, filters_ref, lengths_ref, aperture_ref, codes_ref, sems,
):
    sources = (bins_hbm, filters_hbm, lengths_hbm, aperture_hbm)
    targets = (bins_ref, filters_ref, lengths_ref, aperture_ref)
    copies = [pltpu.make_async_copy(x, y, sems.at[i]) for i, (x, y) in enumerate(zip(sources, targets))]
    for copy in copies:
        copy.start()
    shots = aperture_ref.shape[0]
    tiles = counts_ref.shape[1] // LANES
    lane = lax.broadcasted_iota(jnp.int32, (LANES, LANES), 0)
    station = lane % PIECE * 4 + lane // PIECE - lax.broadcasted_iota(jnp.int32, (LANES, LANES), 1) // (LANES // 2)
    for tile in range(tiles):
        here = jnp.where(station == 2 * tile, 1.0, 0.0)
        spread_ref[:, tile * LANES : (tile + 1) * LANES] = here.astype(BF16)

    copies[0].wait()
    copies[1].wait()
    shot_dev, _, time_dev = filtered_ref.shape
    width = time_dev + LANES
    basis, times = basis_in_kernel(bins_ref, lax.axis_index("freq") * time_dev - HALF, width)
    basis = jnp.where((times >= 0) & (times < NT), basis.astype(BF16).astype(F32), 0.0)
    taps = filters_ref[...].astype(F32)
    total = [jnp.zeros((2 * NF, time_dev), F32) for _ in range(shot_dev)]
    for j in range(TAPS):
        shift = 2 * HALF - j
        moved = basis if shift == 0 else pltpu.roll(basis, width - shift, 1)
        moved = moved[:, :time_dev]
        for s in range(shot_dev):
            total[s] = total[s] + taps[s : s + 1, j : j + 1] * moved
    for s in range(shot_dev):
        filtered_ref[s] = total[s].astype(BF16)

    copies[2].wait()
    copies[3].wait()
    for s in range(shots):
        lists = aperture_ref[s]
        codes_ref[pl.ds(s, KMAX, stride=shots), :] = jnp.concatenate([lists, lists], axis=1)
    lengths = jnp.concatenate([lengths_ref[...]] * 2, axis=1)
    upper = lax.broadcasted_iota(jnp.int32, (shots, LANES), 1) // (LANES // 2)
    totals = [jnp.zeros((shots, LANES), BF16) for _ in range(tiles)]
    for k in range(KMAX):
        codes = codes_ref[k * shots : (k + 1) * shots, :]
        codes = jnp.where(lengths > k, codes - upper, -LANES).astype(F32).astype(BF16)
        for tile in range(tiles):
            hit = jnp.where(codes == BF16(2 * tile), BF16(1.0), BF16(0.0))
            totals[tile] = totals[tile] + hit
    for tile in range(tiles):
        counts_ref[:, tile * LANES : (tile + 1) * LANES] = totals[tile].astype(F32)


def product_kernel(received_ref, counts_ref, spread_ref, message_ref, station_ref, first_ref, second_ref):
    groups = received_ref.shape[0] // 2
    for g in range(groups):
        rounded = (received_ref[2 * g].astype(F32) + received_ref[2 * g + 1].astype(F32)).astype(BF16).astype(F32)
        second_ref[:, g * LANES : (g + 1) * LANES] = jnp.concatenate([rounded[0], rounded[1]], axis=0)
        legs = [rounded[2]] + [pltpu.roll(rounded[2], LANES - shift, 1) for shift in (16, 8, 24)]
        station_ref[16 * g : 16 * g + 16, :] = jnp.concatenate(legs, axis=0).astype(BF16)
    first_ref[...] = jnp.dot(station_ref[...], spread_ref[...], preferred_element_type=F32)
    second = second_ref[...]
    crossed = jnp.concatenate([second[4:], second[:4]], axis=0)
    upper = lax.broadcasted_iota(jnp.int32, (NF, LANES), 0) >= 4
    low = lax.broadcasted_iota(jnp.int32, (NF, LANES), 1) < LANES // 2

    def total(x):
        x = sum(x[:, i * LANES : (i + 1) * LANES] for i in range(x.shape[1] // LANES))
        return x + pltpu.roll(x, LANES // 2, 1)

    for g in range(groups):
        spectra = []
        for s in (2 * g, 2 * g + 1):
            first = counts_ref[s : s + 1, :] * first_ref[8 * s : 8 * s + 8, :]
            same, other = total(first * second), total(first * crossed)
            same, other = same - pltpu.roll(same, 4, 0), other + pltpu.roll(other, 4, 0)
            spectra.append(jnp.where(upper, other, same) * KMAX ** (-0.5))
        message = jnp.where(low, spectra[0], spectra[1])
        message_ref[16 * g : 16 * g + 16, :] = jnp.concatenate([message, message], axis=0).astype(BF16)


def synthesis_kernel(received_ref, filtered_ref, out_hbm, out_ref, out_sem):
    low = lax.broadcasted_iota(jnp.int32, (2 * NF, LANES), 1) < LANES // 2
    copies = []
    for tile in range(out_ref.shape[1] // LANES):
        left, right = [received_ref[32 * tile + i : 32 * tile + i + 16, :].astype(F32) for i in (0, 16)]
        spectra = (
            jnp.where(low, left, pltpu.roll(right, LANES // 2, 1)),
            jnp.where(low, pltpu.roll(left, LANES // 2, 1), right),
        )
        rows = pl.ds(tile * LANES, LANES)
        for s in range(2):
            out_ref[s, rows, :] = lax.dot_general(
                spectra[s].astype(BF16), filtered_ref[s], (((0,), (0,)), ((), ())), preferred_element_type=F32
            ).astype(BF16)
            copy = pltpu.make_async_copy(out_ref.at[s, rows, :], out_hbm.at[s, rows, :], out_sem.at[2 * tile + s])
            copy.start()
            copies.append(copy)
    for copy in copies:
        copy.wait()


def in_vmem():
    return pl.BlockSpec(memory_space=pltpu.VMEM)


def in_hbm():
    return pl.BlockSpec(memory_space=pltpu.HBM)


def shards(traces, frequency_bins, aperture, lengths, filters):
    shot_dev, receivers, time_dev = traces.shape
    devices = lax.axis_size("shot") * lax.axis_size("freq")
    shots = aperture.shape[0]
    params = pltpu.CompilerParams(vmem_limit_bytes=VMEM_LIMIT)

    messages = pl.pallas_call(
        analysis_kernel,
        in_specs=[in_hbm(), in_hbm()],
        out_specs=in_vmem(),
        out_shape=jax.ShapeDtypeStruct((devices, 3, NF // 2, LANES), BF16),
        scratch_shapes=[
            pltpu.SMEM((NF,), jnp.int32),
            pltpu.VMEM(traces.shape, BF16),
            pltpu.VMEM((2 * NF, time_dev), BF16),
            pltpu.SemaphoreType.DMA((2,)),
            pltpu.SemaphoreType.DMA,
        ],
        compiler_params=params,
        cost_estimate=pl.CostEstimate(flops=2 * 16 * traces.size, bytes_accessed=2 * traces.size, transcendentals=0),
    )(
        pltpu.with_memory_space_constraint(frequency_bins, pltpu.HBM),
        pltpu.with_memory_space_constraint(traces, pltpu.HBM),
    )
    received = lax.all_to_all(messages, DEVICES, split_axis=0, concat_axis=0, tiled=True)

    pairs = shots * aperture.shape[1]
    lists = aperture.transpose(0, 2, 1)
    counts, spread, filtered = pl.pallas_call(
        tables_kernel,
        in_specs=[in_hbm()] * 4,
        out_specs=[in_vmem()] * 3,
        out_shape=[
            jax.ShapeDtypeStruct((shots, pairs), F32),
            jax.ShapeDtypeStruct((LANES, pairs), BF16),
            jax.ShapeDtypeStruct((shot_dev, 2 * NF, time_dev), BF16),
        ],
        scratch_shapes=[
            pltpu.SMEM((NF,), jnp.int32),
            pltpu.VMEM(filters.shape, BF16),
            pltpu.VMEM(lengths.shape, jnp.int32),
            pltpu.VMEM(lists.shape, jnp.int32),
            pltpu.VMEM((KMAX * shots, LANES), jnp.int32),
            pltpu.SemaphoreType.DMA((4,)),
        ],
        compiler_params=params,
        cost_estimate=pl.CostEstimate(flops=1 << 24, bytes_accessed=1 << 21, transcendentals=0),
    )(*[pltpu.with_memory_space_constraint(x, pltpu.HBM) for x in (frequency_bins, filters, lengths, lists)])

    messages = pl.pallas_call(
        product_kernel,
        in_specs=[in_vmem(), in_vmem(), in_vmem()],
        out_specs=in_vmem(),
        out_shape=jax.ShapeDtypeStruct((devices * NF, LANES), BF16),
        scratch_shapes=[
            pltpu.VMEM((shots * NF, LANES), BF16),
            pltpu.VMEM((shots * NF, pairs), F32),
            pltpu.VMEM((NF, pairs), F32),
        ],
        compiler_params=params,
        cost_estimate=pl.CostEstimate(flops=1 << 23, bytes_accessed=1 << 19, transcendentals=0),
    )(received, counts, spread)
    received = lax.all_to_all(
        messages.reshape(devices, NF, LANES), DEVICES, split_axis=0, concat_axis=0, tiled=True
    ).reshape(devices * NF, LANES)

    return pl.pallas_call(
        synthesis_kernel,
        in_specs=[in_vmem(), in_vmem()],
        out_specs=in_hbm(),
        out_shape=jax.ShapeDtypeStruct(traces.shape, BF16),
        scratch_shapes=[
            pltpu.VMEM(traces.shape, BF16),
            pltpu.SemaphoreType.DMA((shot_dev * receivers // LANES,)),
        ],
        compiler_params=params,
        cost_estimate=pl.CostEstimate(flops=2 * 16 * traces.size, bytes_accessed=2 * traces.size, transcendentals=0),
    )(received, filtered)


def general_shards(traces, frequency_bins, aperture, lengths, filters):
    shot_dev, receivers, time_dev = traces.shape
    shots = aperture.shape[0]
    receiver_dev = aperture.shape[1]
    start = lax.axis_index("freq") * time_dev

    def basis_rows(times):
        phases = frequency_bins[:, None] * times[None, :]
        return jnp.stack([cosine(phases & (NT - 1)), cosine((phases + NT // 4) & (NT - 1))], axis=1)

    times = start + jnp.arange(time_dev, dtype=jnp.int32)
    analysis = (basis_rows(times) * NT ** (-0.5)).astype(BF16).reshape(2 * NF, time_dev)
    term = lax.dot_general(
        analysis, traces.reshape(shot_dev * receivers, time_dev), (((1,), (1,)), ((), ())), preferred_element_type=F32
    )
    spectra = lax.psum_scatter(
        term.reshape(NF, 2, shot_dev, receivers), "freq", scatter_dimension=0, tiled=True
    ).astype(BF16)
    second = lax.all_to_all(spectra, "shot", split_axis=3, concat_axis=2, tiled=True).astype(F32)
    stations = spectra[:, :, :, :: receivers // shots]
    first = lax.all_gather(stations, "shot", axis=2, tiled=True).astype(F32)

    def one_shot(inputs):
        legs, lists, list_lengths = inputs
        used = jnp.arange(KMAX, dtype=jnp.int32)[None, :] < list_lengths[:, None]
        lists = jnp.where(used, lists, -1)
        hits = lists[None] == jnp.arange(shots, dtype=jnp.int32)[:, None, None]
        counts = hits.astype(F32).sum(axis=-1)
        legs = legs[..., None]
        real = legs[:, 0] * second[:, 0] - legs[:, 1] * second[:, 1]
        imag = legs[:, 0] * second[:, 1] + legs[:, 1] * second[:, 0]
        return (jnp.stack([real, imag], axis=1) * counts).sum(axis=2)

    summed = lax.map(one_shot, (first.transpose(2, 0, 1, 3), aperture, lengths))
    summed = (summed * KMAX ** (-0.5)).astype(BF16).transpose(1, 2, 0, 3)
    summed = lax.all_to_all(summed, "shot", split_axis=2, concat_axis=3, tiled=True)
    summed = lax.all_gather(summed, "freq", axis=0, tiled=True).reshape(2 * NF, shot_dev, receivers)

    wide = start - HALF + jnp.arange(time_dev + 2 * HALF, dtype=jnp.int32)
    synthesis = basis_rows(wide).astype(BF16).astype(F32).reshape(2 * NF, time_dev + 2 * HALF)
    synthesis = jnp.where((wide >= 0) & (wide < NT), synthesis, 0.0)
    filtered = jnp.zeros((shot_dev, 2 * NF, time_dev), F32)
    for j in range(TAPS):
        tap = filters[:, j].astype(F32)[:, None, None]
        filtered = filtered + tap * synthesis[:, 2 * HALF - j : 2 * HALF - j + time_dev]
    out = jnp.einsum("fsr,sft->srt", summed, filtered.astype(BF16), preferred_element_type=F32)
    return out.astype(BF16)


def solution(mesh):
    in_specs = (
        P("shot", None, "freq"),
        P(),
        P(None, "shot", None),
        P(None, "shot"),
        P("shot", None),
    )
    out_specs = P("shot", None, "freq")
    whole_pieces = mesh.shape["shot"] == 16 and mesh.shape["freq"] == 2
    body = shards if whole_pieces else general_shards
    return jax.shard_map(body, mesh=mesh, in_specs=in_specs, out_specs=out_specs, check_vma=False)
```

```python
import math

import jax
import jax.numpy as jnp
from jax import lax
from jax.experimental import pallas as pl
from jax.experimental.pallas import tpu as pltpu
from jax.sharding import PartitionSpec as P

NT = 1024
NF = 8
KMAX = 32
TAPS = 31
HALF = (TAPS - 1) // 2
LANES = 128
PIECE = 32
DEVICES = ("shot", "freq")
F32 = jnp.float32
BF16 = jnp.bfloat16
VMEM_LIMIT = 48 * 1024 * 1024


def cosine(phases):
    quarter = NT // 4
    turn = (phases + quarter // 2) // quarter
    angle = (phases - turn * quarter).astype(F32) * (2.0 * math.pi / NT)
    square = angle * angle
    sine = angle * (1.0 + square * (-1 / 6 + square * (1 / 120 + square * (-1 / 5040 + square / 362880))))
    cosine = 1.0 + square * (-1 / 2 + square * (1 / 24 + square * (-1 / 720 + square / 40320)))
    near = jnp.where(turn % 2 == 1, sine, cosine)
    return jnp.where((turn == 1) | (turn == 2), -near, near)


def basis_in_kernel(bins_ref, first_time, width):
    rows = lax.broadcasted_iota(jnp.int32, (2 * NF, width), 0)
    times = lax.broadcasted_iota(jnp.int32, (2 * NF, width), 1) + first_time
    frequency = rows // NF * (NF // 2) + rows % (NF // 2)
    part = rows // (NF // 2) % 2
    bins = jnp.zeros((2 * NF, width), jnp.int32)
    for f in range(NF):
        bins = jnp.where(frequency == f, bins_ref[f], bins)
    return cosine((bins * times + part * (NT // 4)) & (NT - 1)), times


def write_spread(spread_ref):
    lane = lax.broadcasted_iota(jnp.int32, (LANES, LANES), 0)
    station = lane % PIECE * 4 + lane // PIECE - lax.broadcasted_iota(jnp.int32, (LANES, LANES), 1) // (LANES // 2)
    for tile in range(spread_ref.shape[1] // LANES):
        here = jnp.where(station == 2 * tile, 1.0, 0.0)
        spread_ref[:, tile * LANES : (tile + 1) * LANES] = here.astype(BF16)


def write_filtered(bins_ref, filters_ref, filtered_ref):
    shot_dev, _, time_dev = filtered_ref.shape
    width = time_dev + LANES
    basis, times = basis_in_kernel(bins_ref, lax.axis_index("freq") * time_dev - HALF, width)
    basis = jnp.where((times >= 0) & (times < NT), basis.astype(BF16).astype(F32), 0.0)
    taps = filters_ref[...].astype(F32)
    total = [jnp.zeros((2 * NF, time_dev), F32) for _ in range(shot_dev)]
    for j in range(TAPS):
        shift = 2 * HALF - j
        moved = basis if shift == 0 else pltpu.roll(basis, width - shift, 1)
        moved = moved[:, :time_dev]
        for s in range(shot_dev):
            total[s] = total[s] + taps[s : s + 1, j : j + 1] * moved
    for s in range(shot_dev):
        filtered_ref[s] = total[s].astype(BF16)


def bit_sums(words):
    waiting, planes = [], []
    for word in words:
        level = 0
        while True:
            if level == len(waiting):
                waiting.append([])
            waiting[level].append(word)
            if len(waiting[level]) < 3:
                break
            x, y, z = waiting[level]
            either = x ^ y
            waiting[level] = [either ^ z]
            word = (x & y) | (either & z)
            level += 1
    level = 0
    while level < len(waiting):
        held = waiting[level]
        if len(held) > 1:
            if level + 1 == len(waiting):
                waiting.append([])
            x, y = held[0], held[1]
            carries = [x & y]
            if len(held) == 3:
                carries = [(x & y) | ((x ^ y) & held[2])]
            waiting[level + 1] += carries
            held = [x ^ y] if len(held) == 2 else [x ^ y ^ held[2]]
        planes.append(held[0])
        level += 1
    return planes


def write_counts(aperture_ref, lengths_ref, codes_ref, counts_ref):
    half = aperture_ref.shape[0] // 2
    for s in range(half):
        both = jnp.concatenate([aperture_ref[s], aperture_ref[s + half]], axis=1)
        codes_ref[pl.ds(s, KMAX, stride=half), :] = both
    lengths = jnp.concatenate([lengths_ref[:half, :], lengths_ref[half:, :]], axis=1)
    one = jnp.ones((half, LANES), jnp.int32)

    def words():
        for k in range(KMAX):
            codes = codes_ref[k * half : (k + 1) * half, :]
            yield jnp.where(lengths > k, lax.shift_left(one, codes), 0)

    planes = bit_sums(words())
    low = lax.broadcasted_iota(jnp.int32, (half, LANES), 1) < LANES // 2
    for i in range(0, 8, 2):
        packed = []
        for bit in (i, i + 1):
            total = 0
            for level, plane in enumerate(planes):
                spread = lax.shift_right_logical(plane, jnp.full_like(plane, bit)) & 0x01010101
                total = total + (spread << level)
            packed.append(total)
        for byte in range(4):
            left, right = [(lax.shift_right_logical(x, jnp.full_like(x, 8 * byte)) & 255).astype(F32) for x in packed]
            lanes = pl.ds((8 * byte + i) * (LANES // 2), LANES)
            counts_ref[:half, lanes] = jnp.where(low, left, pltpu.roll(right, LANES // 2, 1))
            counts_ref[half:, lanes] = jnp.where(low, pltpu.roll(left, LANES // 2, 1), right)


def analysis_kernel(
    bins_hbm, filters_hbm, lengths_hbm, aperture_hbm, traces_hbm,
    message_ref, counts_ref, spread_ref, filtered_ref,
    bins_ref, filters_ref, lengths_ref, aperture_ref, traces_ref, basis_ref, codes_ref, sems,
):
    shot_dev, receivers, time_dev = traces_ref.shape
    sources = (bins_hbm, filters_hbm, lengths_hbm, aperture_hbm)
    targets = (bins_ref, filters_ref, lengths_ref, aperture_ref)
    tables = [pltpu.make_async_copy(x, y, sems.at[i]) for i, (x, y) in enumerate(zip(sources, targets))]
    starts = [0, 3 * LANES, receivers]
    blocks = list(zip(starts, starts[1:]))
    copies = []
    for i, (start, end) in enumerate(blocks):
        rows = pl.ds(start, end - start)
        copies.append(pltpu.make_async_copy(traces_hbm.at[:, rows, :], traces_ref.at[:, rows, :], sems.at[4 + i]))
    for copy in tables + copies:
        copy.start()

    write_spread(spread_ref)
    tables[0].wait()
    tables[1].wait()
    basis, _ = basis_in_kernel(bins_ref, lax.axis_index("freq") * time_dev, time_dev)
    basis_ref[...] = (basis * NT ** (-0.5)).astype(BF16)
    write_filtered(bins_ref, filters_ref, filtered_ref)
    tables[2].wait()
    tables[3].wait()
    write_counts(aperture_ref, lengths_ref, codes_ref, counts_ref)

    lane = lax.broadcasted_iota(jnp.int32, (2 * NF, LANES), 1)
    row = lax.broadcasted_iota(jnp.int32, (2 * NF, LANES), 0)
    low = lane < LANES // 2
    is_station = lane % PIECE == 0
    stations = jnp.zeros((2 * NF, LANES), F32)
    for copy, (start, end) in zip(copies, blocks):
        copy.wait()
        terms = [
            lax.dot_general(
                basis_ref[...],
                traces_ref[s, start:end, :],
                (((1,), (1,)), ((), ())),
                preferred_element_type=F32,
            )
            for s in range(shot_dev)
        ]
        for j in range((end - start) // LANES):
            tile = start // LANES + j
            first, second = [x[:, j * LANES : (j + 1) * LANES] for x in terms]
            for s, x in enumerate((first, second)):
                marked = jnp.where(is_station, x, 0.0)
                shift = 8 * s + tile
                stations = stations + (pltpu.roll(marked, shift, 1) if shift else marked)
            even = jnp.where(low, first, pltpu.roll(second, LANES // 2, 1))
            odd = jnp.where(low, pltpu.roll(first, LANES // 2, 1), second)
            for g, x in ((2 * tile, even), (2 * tile + 1, odd)):
                for h in range(2):
                    message_ref[2 * g + h, 0] = x[8 * h : 8 * h + 4].astype(BF16)
                    message_ref[2 * g + h, 1] = x[8 * h + 4 : 8 * h + 8].astype(BF16)
    stations = jnp.where(row // 4 % 2 == 1, pltpu.roll(stations, 16, 1), stations)
    for h in range(2):
        slab = (stations[8 * h : 8 * h + 4] + stations[8 * h + 4 : 8 * h + 8]).astype(BF16)
        for g in range(message_ref.shape[0] // 2):
            message_ref[2 * g + h, 2] = slab


def product_kernel(received_ref, counts_ref, spread_ref, message_ref, station_ref, first_ref, second_ref):
    groups = received_ref.shape[0] // 2
    for g in range(groups):
        rounded = (received_ref[2 * g].astype(F32) + received_ref[2 * g + 1].astype(F32)).astype(BF16).astype(F32)
        second_ref[:, g * LANES : (g + 1) * LANES] = jnp.concatenate([rounded[0], rounded[1]], axis=0)
        legs = [rounded[2]] + [pltpu.roll(rounded[2], LANES - shift, 1) for shift in (16, 8, 24)]
        station_ref[16 * g : 16 * g + 16, :] = jnp.concatenate(legs, axis=0).astype(BF16)
    first_ref[...] = jnp.dot(station_ref[...], spread_ref[...], preferred_element_type=F32)
    second = second_ref[...]
    crossed = jnp.concatenate([second[4:], second[:4]], axis=0)
    upper = lax.broadcasted_iota(jnp.int32, (NF, LANES), 0) >= 4
    low = lax.broadcasted_iota(jnp.int32, (NF, LANES), 1) < LANES // 2

    def total(x):
        x = sum(x[:, i * LANES : (i + 1) * LANES] for i in range(x.shape[1] // LANES))
        return x + pltpu.roll(x, LANES // 2, 1)

    for g in range(groups):
        spectra = []
        for s in (2 * g, 2 * g + 1):
            first = counts_ref[s : s + 1, :] * first_ref[8 * s : 8 * s + 8, :]
            same, other = total(first * second), total(first * crossed)
            same, other = same - pltpu.roll(same, 4, 0), other + pltpu.roll(other, 4, 0)
            spectra.append(jnp.where(upper, other, same) * KMAX ** (-0.5))
        message = jnp.where(low, spectra[0], spectra[1])
        message_ref[16 * g : 16 * g + 16, :] = jnp.concatenate([message, message], axis=0).astype(BF16)


def synthesis_kernel(received_ref, filtered_ref, out_hbm, out_ref, out_sem):
    low = lax.broadcasted_iota(jnp.int32, (2 * NF, LANES), 1) < LANES // 2
    copies = []
    for tile in range(out_ref.shape[1] // LANES):
        left, right = [received_ref[32 * tile + i : 32 * tile + i + 16, :].astype(F32) for i in (0, 16)]
        spectra = (
            jnp.where(low, left, pltpu.roll(right, LANES // 2, 1)),
            jnp.where(low, pltpu.roll(left, LANES // 2, 1), right),
        )
        rows = pl.ds(tile * LANES, LANES)
        for s in range(2):
            out_ref[s, rows, :] = lax.dot_general(
                spectra[s].astype(BF16), filtered_ref[s], (((0,), (0,)), ((), ())), preferred_element_type=F32
            ).astype(BF16)
            copy = pltpu.make_async_copy(out_ref.at[s, rows, :], out_hbm.at[s, rows, :], out_sem.at[2 * tile + s])
            copy.start()
            copies.append(copy)
    for copy in copies:
        copy.wait()


def in_vmem():
    return pl.BlockSpec(memory_space=pltpu.VMEM)


def in_hbm():
    return pl.BlockSpec(memory_space=pltpu.HBM)


def shards(traces, frequency_bins, aperture, lengths, filters):
    shot_dev, receivers, time_dev = traces.shape
    devices = lax.axis_size("shot") * lax.axis_size("freq")
    shots = aperture.shape[0]
    params = pltpu.CompilerParams(vmem_limit_bytes=VMEM_LIMIT)

    pairs = shots * aperture.shape[1]
    lists = aperture.transpose(0, 2, 1)
    operands = (frequency_bins, filters, lengths, lists, traces)
    messages, counts, spread, filtered = pl.pallas_call(
        analysis_kernel,
        in_specs=[in_hbm()] * len(operands),
        out_specs=[in_vmem()] * 4,
        out_shape=[
            jax.ShapeDtypeStruct((devices, 3, NF // 2, LANES), BF16),
            jax.ShapeDtypeStruct((shots, pairs), F32),
            jax.ShapeDtypeStruct((LANES, pairs), BF16),
            jax.ShapeDtypeStruct((shot_dev, 2 * NF, time_dev), BF16),
        ],
        scratch_shapes=[
            pltpu.SMEM((NF,), jnp.int32),
            *[pltpu.VMEM(x.shape, x.dtype) for x in operands[1:]],
            pltpu.VMEM((2 * NF, time_dev), BF16),
            pltpu.VMEM((KMAX * shots // 2, LANES), jnp.int32),
            pltpu.SemaphoreType.DMA((6,)),
        ],
        compiler_params=params,
        cost_estimate=pl.CostEstimate(flops=2 * 16 * traces.size, bytes_accessed=2 * traces.size, transcendentals=0),
    )(*[pltpu.with_memory_space_constraint(x, pltpu.HBM) for x in operands])
    received = lax.all_to_all(messages, DEVICES, split_axis=0, concat_axis=0, tiled=True)

    messages = pl.pallas_call(
        product_kernel,
        in_specs=[in_vmem(), in_vmem(), in_vmem()],
        out_specs=in_vmem(),
        out_shape=jax.ShapeDtypeStruct((devices * NF, LANES), BF16),
        scratch_shapes=[
            pltpu.VMEM((shots * NF, LANES), BF16),
            pltpu.VMEM((shots * NF, pairs), F32),
            pltpu.VMEM((NF, pairs), F32),
        ],
        compiler_params=params,
        cost_estimate=pl.CostEstimate(flops=1 << 23, bytes_accessed=1 << 19, transcendentals=0),
    )(received, counts, spread)
    received = lax.all_to_all(
        messages.reshape(devices, NF, LANES), DEVICES, split_axis=0, concat_axis=0, tiled=True
    ).reshape(devices * NF, LANES)

    return pl.pallas_call(
        synthesis_kernel,
        in_specs=[in_vmem(), in_vmem()],
        out_specs=in_hbm(),
        out_shape=jax.ShapeDtypeStruct(traces.shape, BF16),
        scratch_shapes=[
            pltpu.VMEM(traces.shape, BF16),
            pltpu.SemaphoreType.DMA((shot_dev * receivers // LANES,)),
        ],
        compiler_params=params,
        cost_estimate=pl.CostEstimate(flops=2 * 16 * traces.size, bytes_accessed=2 * traces.size, transcendentals=0),
    )(received, filtered)


def general_shards(traces, frequency_bins, aperture, lengths, filters):
    shot_dev, receivers, time_dev = traces.shape
    shots = aperture.shape[0]
    receiver_dev = aperture.shape[1]
    start = lax.axis_index("freq") * time_dev

    def basis_rows(times):
        phases = frequency_bins[:, None] * times[None, :]
        return jnp.stack([cosine(phases & (NT - 1)), cosine((phases + NT // 4) & (NT - 1))], axis=1)

    times = start + jnp.arange(time_dev, dtype=jnp.int32)
    analysis = (basis_rows(times) * NT ** (-0.5)).astype(BF16).reshape(2 * NF, time_dev)
    term = lax.dot_general(
        analysis, traces.reshape(shot_dev * receivers, time_dev), (((1,), (1,)), ((), ())), preferred_element_type=F32
    )
    spectra = lax.psum_scatter(
        term.reshape(NF, 2, shot_dev, receivers), "freq", scatter_dimension=0, tiled=True
    ).astype(BF16)
    second = lax.all_to_all(spectra, "shot", split_axis=3, concat_axis=2, tiled=True).astype(F32)
    stations = spectra[:, :, :, :: receivers // shots]
    first = lax.all_gather(stations, "shot", axis=2, tiled=True).astype(F32)

    def one_shot(inputs):
        legs, lists, list_lengths = inputs
        used = jnp.arange(KMAX, dtype=jnp.int32)[None, :] < list_lengths[:, None]
        lists = jnp.where(used, lists, -1)
        hits = lists[None] == jnp.arange(shots, dtype=jnp.int32)[:, None, None]
        counts = hits.astype(F32).sum(axis=-1)
        legs = legs[..., None]
        real = legs[:, 0] * second[:, 0] - legs[:, 1] * second[:, 1]
        imag = legs[:, 0] * second[:, 1] + legs[:, 1] * second[:, 0]
        return (jnp.stack([real, imag], axis=1) * counts).sum(axis=2)

    summed = lax.map(one_shot, (first.transpose(2, 0, 1, 3), aperture, lengths))
    summed = (summed * KMAX ** (-0.5)).astype(BF16).transpose(1, 2, 0, 3)
    summed = lax.all_to_all(summed, "shot", split_axis=2, concat_axis=3, tiled=True)
    summed = lax.all_gather(summed, "freq", axis=0, tiled=True).reshape(2 * NF, shot_dev, receivers)

    wide = start - HALF + jnp.arange(time_dev + 2 * HALF, dtype=jnp.int32)
    synthesis = basis_rows(wide).astype(BF16).astype(F32).reshape(2 * NF, time_dev + 2 * HALF)
    synthesis = jnp.where((wide >= 0) & (wide < NT), synthesis, 0.0)
    filtered = jnp.zeros((shot_dev, 2 * NF, time_dev), F32)
    for j in range(TAPS):
        tap = filters[:, j].astype(F32)[:, None, None]
        filtered = filtered + tap * synthesis[:, 2 * HALF - j : 2 * HALF - j + time_dev]
    out = jnp.einsum("fsr,sft->srt", summed, filtered.astype(BF16), preferred_element_type=F32)
    return out.astype(BF16)


def solution(mesh):
    in_specs = (
        P("shot", None, "freq"),
        P(),
        P(None, "shot", None),
        P(None, "shot"),
        P("shot", None),
    )
    out_specs = P("shot", None, "freq")
    whole_pieces = mesh.shape["shot"] == 16 and mesh.shape["freq"] == 2
    body = shards if whole_pieces else general_shards
    return jax.shard_map(body, mesh=mesh, in_specs=in_specs, out_specs=out_specs, check_vma=False)
```

```python
import math

import jax
import jax.numpy as jnp
from jax import lax
from jax.experimental import pallas as pl
from jax.experimental.pallas import tpu as pltpu
from jax.sharding import PartitionSpec as P

NT = 1024
NF = 8
KMAX = 32
TAPS = 31
HALF = (TAPS - 1) // 2
LANES = 128
PIECE = 32
DEVICES = ("shot", "freq")
F32 = jnp.float32
BF16 = jnp.bfloat16
VMEM_LIMIT = 48 * 1024 * 1024


def cosine(phases):
    quarter = NT // 4
    turn = (phases + quarter // 2) // quarter
    angle = (phases - turn * quarter).astype(F32) * (2.0 * math.pi / NT)
    square = angle * angle
    sine = angle * (1.0 + square * (-1 / 6 + square * (1 / 120 + square * (-1 / 5040 + square / 362880))))
    cosine = 1.0 + square * (-1 / 2 + square * (1 / 24 + square * (-1 / 720 + square / 40320)))
    near = jnp.where(turn % 2 == 1, sine, cosine)
    return jnp.where((turn == 1) | (turn == 2), -near, near)


def basis_in_kernel(bins_ref, first_time, width):
    rows = lax.broadcasted_iota(jnp.int32, (2 * NF, width), 0)
    times = lax.broadcasted_iota(jnp.int32, (2 * NF, width), 1) + first_time
    frequency = rows // NF * (NF // 2) + rows % (NF // 2)
    part = rows // (NF // 2) % 2
    bins = jnp.zeros((2 * NF, width), jnp.int32)
    for f in range(NF):
        bins = jnp.where(frequency == f, bins_ref[f], bins)
    return cosine((bins * times + part * (NT // 4)) & (NT - 1)), times


def write_spread(spread_ref):
    lane = lax.broadcasted_iota(jnp.int32, (LANES, LANES), 0)
    station = lane % PIECE * 4 + lane // PIECE - lax.broadcasted_iota(jnp.int32, (LANES, LANES), 1) // (LANES // 2)
    for tile in range(spread_ref.shape[1] // LANES):
        here = jnp.where(station == 2 * tile, 1.0, 0.0)
        spread_ref[:, tile * LANES : (tile + 1) * LANES] = here.astype(BF16)


def write_filtered(bins_ref, filters_ref, filtered_ref):
    shot_dev, _, time_dev = filtered_ref.shape
    width = time_dev + LANES
    basis, times = basis_in_kernel(bins_ref, lax.axis_index("freq") * time_dev - HALF, width)
    basis = jnp.where((times >= 0) & (times < NT), basis.astype(BF16).astype(F32), 0.0)
    taps = filters_ref[...].astype(F32)
    total = [jnp.zeros((2 * NF, time_dev), F32) for _ in range(shot_dev)]
    for j in range(TAPS):
        shift = 2 * HALF - j
        moved = basis if shift == 0 else pltpu.roll(basis, width - shift, 1)
        moved = moved[:, :time_dev]
        for s in range(shot_dev):
            total[s] = total[s] + taps[s : s + 1, j : j + 1] * moved
    for s in range(shot_dev):
        filtered_ref[s] = total[s].astype(BF16)


def bit_sums(words):
    waiting, planes = [], []
    for word in words:
        level = 0
        while True:
            if level == len(waiting):
                waiting.append([])
            waiting[level].append(word)
            if len(waiting[level]) < 3:
                break
            x, y, z = waiting[level]
            either = x ^ y
            waiting[level] = [either ^ z]
            word = (x & y) | (either & z)
            level += 1
    level = 0
    while level < len(waiting):
        held = waiting[level]
        if len(held) > 1:
            if level + 1 == len(waiting):
                waiting.append([])
            x, y = held[0], held[1]
            carries = [x & y]
            if len(held) == 3:
                carries = [(x & y) | ((x ^ y) & held[2])]
            waiting[level + 1] += carries
            held = [x ^ y] if len(held) == 2 else [x ^ y ^ held[2]]
        planes.append(held[0])
        level += 1
    return planes


def write_counts(aperture_ref, lengths_ref, codes_ref, counts_ref):
    half = aperture_ref.shape[0] // 2
    for s in range(half):
        both = jnp.concatenate([aperture_ref[s], aperture_ref[s + half]], axis=1)
        codes_ref[pl.ds(s, KMAX, stride=half), :] = both
    lengths = jnp.concatenate([lengths_ref[:half, :], lengths_ref[half:, :]], axis=1)
    one = jnp.ones((half, LANES), jnp.int32)

    def words():
        for k in range(KMAX):
            codes = codes_ref[k * half : (k + 1) * half, :]
            yield jnp.where(lengths > k, lax.shift_left(one, codes), 0)

    planes = bit_sums(words())
    low = lax.broadcasted_iota(jnp.int32, (half, LANES), 1) < LANES // 2
    for i in range(0, 8, 2):
        packed = []
        for bit in (i, i + 1):
            total = 0
            for level, plane in enumerate(planes):
                spread = lax.shift_right_logical(plane, jnp.full_like(plane, bit)) & 0x01010101
                total = total + (spread << level)
            packed.append(total)
        for byte in range(4):
            left, right = [(lax.shift_right_logical(x, jnp.full_like(x, 8 * byte)) & 255).astype(F32) for x in packed]
            lanes = pl.ds((8 * byte + i) * (LANES // 2), LANES)
            counts_ref[:half, lanes] = jnp.where(low, left, pltpu.roll(right, LANES // 2, 1))
            counts_ref[half:, lanes] = jnp.where(low, pltpu.roll(left, LANES // 2, 1), right)


def analysis_kernel(
    bins_hbm, filters_hbm, lengths_hbm, aperture_hbm, traces_hbm,
    message_ref, counts_ref, spread_ref, filtered_ref,
    bins_ref, filters_ref, lengths_ref, aperture_ref, traces_ref, basis_ref, codes_ref, sems,
):
    shot_dev, receivers, time_dev = traces_ref.shape
    sources = (bins_hbm, filters_hbm, lengths_hbm, aperture_hbm)
    targets = (bins_ref, filters_ref, lengths_ref, aperture_ref)
    tables = [pltpu.make_async_copy(x, y, sems.at[i]) for i, (x, y) in enumerate(zip(sources, targets))]
    starts = [0, 3 * LANES, receivers]
    blocks = list(zip(starts, starts[1:]))
    copies = []
    for i, (start, end) in enumerate(blocks):
        rows = pl.ds(start, end - start)
        copies.append(pltpu.make_async_copy(traces_hbm.at[:, rows, :], traces_ref.at[:, rows, :], sems.at[4 + i]))
    for copy in tables + copies:
        copy.start()

    write_spread(spread_ref)
    tables[0].wait()
    tables[1].wait()
    basis, _ = basis_in_kernel(bins_ref, lax.axis_index("freq") * time_dev, time_dev)
    basis_ref[...] = (basis * NT ** (-0.5)).astype(BF16)
    write_filtered(bins_ref, filters_ref, filtered_ref)

    lane = lax.broadcasted_iota(jnp.int32, (2 * NF, LANES), 1)
    row = lax.broadcasted_iota(jnp.int32, (2 * NF, LANES), 0)
    low = lane < LANES // 2
    is_station = lane % PIECE == 0
    stations = jnp.zeros((2 * NF, LANES), F32)
    for copy, (start, end) in zip(copies, blocks):
        copy.wait()
        if end == receivers:
            tables[2].wait()
            tables[3].wait()
            write_counts(aperture_ref, lengths_ref, codes_ref, counts_ref)
        terms = [
            lax.dot_general(
                basis_ref[...],
                traces_ref[s, start:end, :],
                (((1,), (1,)), ((), ())),
                preferred_element_type=F32,
            )
            for s in range(shot_dev)
        ]
        for j in range((end - start) // LANES):
            tile = start // LANES + j
            first, second = [x[:, j * LANES : (j + 1) * LANES] for x in terms]
            for s, x in enumerate((first, second)):
                marked = jnp.where(is_station, x, 0.0)
                shift = 8 * s + tile
                stations = stations + (pltpu.roll(marked, shift, 1) if shift else marked)
            even = jnp.where(low, first, pltpu.roll(second, LANES // 2, 1))
            odd = jnp.where(low, pltpu.roll(first, LANES // 2, 1), second)
            for g, x in ((2 * tile, even), (2 * tile + 1, odd)):
                for h in range(2):
                    message_ref[2 * g + h, 0] = x[8 * h : 8 * h + 4].astype(BF16)
                    message_ref[2 * g + h, 1] = x[8 * h + 4 : 8 * h + 8].astype(BF16)
    stations = jnp.where(row // 4 % 2 == 1, pltpu.roll(stations, 16, 1), stations)
    for h in range(2):
        slab = (stations[8 * h : 8 * h + 4] + stations[8 * h + 4 : 8 * h + 8]).astype(BF16)
        for g in range(message_ref.shape[0] // 2):
            message_ref[2 * g + h, 2] = slab


def product_kernel(received_ref, counts_ref, spread_ref, message_ref, station_ref, first_ref, second_ref):
    groups = received_ref.shape[0] // 2
    for g in range(groups):
        rounded = (received_ref[2 * g].astype(F32) + received_ref[2 * g + 1].astype(F32)).astype(BF16).astype(F32)
        second_ref[:, g * LANES : (g + 1) * LANES] = jnp.concatenate([rounded[0], rounded[1]], axis=0)
        legs = [rounded[2]] + [pltpu.roll(rounded[2], LANES - shift, 1) for shift in (16, 8, 24)]
        station_ref[16 * g : 16 * g + 16, :] = jnp.concatenate(legs, axis=0).astype(BF16)
    first_ref[...] = jnp.dot(station_ref[...], spread_ref[...], preferred_element_type=F32)
    second = second_ref[...]
    crossed = jnp.concatenate([second[4:], second[:4]], axis=0)
    upper = lax.broadcasted_iota(jnp.int32, (NF, LANES), 0) >= 4
    low = lax.broadcasted_iota(jnp.int32, (NF, LANES), 1) < LANES // 2

    def total(x):
        x = sum(x[:, i * LANES : (i + 1) * LANES] for i in range(x.shape[1] // LANES))
        return x + pltpu.roll(x, LANES // 2, 1)

    for g in range(groups):
        spectra = []
        for s in (2 * g, 2 * g + 1):
            first = counts_ref[s : s + 1, :] * first_ref[8 * s : 8 * s + 8, :]
            same, other = total(first * second), total(first * crossed)
            same, other = same - pltpu.roll(same, 4, 0), other + pltpu.roll(other, 4, 0)
            spectra.append(jnp.where(upper, other, same) * KMAX ** (-0.5))
        message = jnp.where(low, spectra[0], spectra[1])
        message_ref[16 * g : 16 * g + 16, :] = jnp.concatenate([message, message], axis=0).astype(BF16)


def synthesis_kernel(received_ref, filtered_ref, out_hbm, out_ref, out_sem):
    low = lax.broadcasted_iota(jnp.int32, (2 * NF, LANES), 1) < LANES // 2
    copies = []
    for tile in range(out_ref.shape[1] // LANES):
        left, right = [received_ref[32 * tile + i : 32 * tile + i + 16, :].astype(F32) for i in (0, 16)]
        spectra = (
            jnp.where(low, left, pltpu.roll(right, LANES // 2, 1)),
            jnp.where(low, pltpu.roll(left, LANES // 2, 1), right),
        )
        rows = pl.ds(tile * LANES, LANES)
        for s in range(2):
            out_ref[s, rows, :] = lax.dot_general(
                spectra[s].astype(BF16), filtered_ref[s], (((0,), (0,)), ((), ())), preferred_element_type=F32
            ).astype(BF16)
            copy = pltpu.make_async_copy(out_ref.at[s, rows, :], out_hbm.at[s, rows, :], out_sem.at[2 * tile + s])
            copy.start()
            copies.append(copy)
    for copy in copies:
        copy.wait()


def in_vmem():
    return pl.BlockSpec(memory_space=pltpu.VMEM)


def in_hbm():
    return pl.BlockSpec(memory_space=pltpu.HBM)


def shards(traces, frequency_bins, aperture, lengths, filters):
    shot_dev, receivers, time_dev = traces.shape
    devices = lax.axis_size("shot") * lax.axis_size("freq")
    shots = aperture.shape[0]
    params = pltpu.CompilerParams(vmem_limit_bytes=VMEM_LIMIT)

    pairs = shots * aperture.shape[1]
    lists = aperture.transpose(0, 2, 1)
    operands = (frequency_bins, filters, lengths, lists, traces)
    messages, counts, spread, filtered = pl.pallas_call(
        analysis_kernel,
        in_specs=[in_hbm()] * len(operands),
        out_specs=[in_vmem()] * 4,
        out_shape=[
            jax.ShapeDtypeStruct((devices, 3, NF // 2, LANES), BF16),
            jax.ShapeDtypeStruct((shots, pairs), F32),
            jax.ShapeDtypeStruct((LANES, pairs), BF16),
            jax.ShapeDtypeStruct((shot_dev, 2 * NF, time_dev), BF16),
        ],
        scratch_shapes=[
            pltpu.SMEM((NF,), jnp.int32),
            *[pltpu.VMEM(x.shape, x.dtype) for x in operands[1:]],
            pltpu.VMEM((2 * NF, time_dev), BF16),
            pltpu.VMEM((KMAX * shots // 2, LANES), jnp.int32),
            pltpu.SemaphoreType.DMA((6,)),
        ],
        compiler_params=params,
        cost_estimate=pl.CostEstimate(flops=2 * 16 * traces.size, bytes_accessed=2 * traces.size, transcendentals=0),
    )(*[pltpu.with_memory_space_constraint(x, pltpu.HBM) for x in operands])
    received = lax.all_to_all(messages, DEVICES, split_axis=0, concat_axis=0, tiled=True)

    messages = pl.pallas_call(
        product_kernel,
        in_specs=[in_vmem(), in_vmem(), in_vmem()],
        out_specs=in_vmem(),
        out_shape=jax.ShapeDtypeStruct((devices * NF, LANES), BF16),
        scratch_shapes=[
            pltpu.VMEM((shots * NF, LANES), BF16),
            pltpu.VMEM((shots * NF, pairs), F32),
            pltpu.VMEM((NF, pairs), F32),
        ],
        compiler_params=params,
        cost_estimate=pl.CostEstimate(flops=1 << 23, bytes_accessed=1 << 19, transcendentals=0),
    )(received, counts, spread)
    received = lax.all_to_all(
        messages.reshape(devices, NF, LANES), DEVICES, split_axis=0, concat_axis=0, tiled=True
    ).reshape(devices * NF, LANES)

    return pl.pallas_call(
        synthesis_kernel,
        in_specs=[in_vmem(), in_vmem()],
        out_specs=in_hbm(),
        out_shape=jax.ShapeDtypeStruct(traces.shape, BF16),
        scratch_shapes=[
            pltpu.VMEM(traces.shape, BF16),
            pltpu.SemaphoreType.DMA((shot_dev * receivers // LANES,)),
        ],
        compiler_params=params,
        cost_estimate=pl.CostEstimate(flops=2 * 16 * traces.size, bytes_accessed=2 * traces.size, transcendentals=0),
    )(received, filtered)


def general_shards(traces, frequency_bins, aperture, lengths, filters):
    shot_dev, receivers, time_dev = traces.shape
    shots = aperture.shape[0]
    receiver_dev = aperture.shape[1]
    start = lax.axis_index("freq") * time_dev

    def basis_rows(times):
        phases = frequency_bins[:, None] * times[None, :]
        return jnp.stack([cosine(phases & (NT - 1)), cosine((phases + NT // 4) & (NT - 1))], axis=1)

    times = start + jnp.arange(time_dev, dtype=jnp.int32)
    analysis = (basis_rows(times) * NT ** (-0.5)).astype(BF16).reshape(2 * NF, time_dev)
    term = lax.dot_general(
        analysis, traces.reshape(shot_dev * receivers, time_dev), (((1,), (1,)), ((), ())), preferred_element_type=F32
    )
    spectra = lax.psum_scatter(
        term.reshape(NF, 2, shot_dev, receivers), "freq", scatter_dimension=0, tiled=True
    ).astype(BF16)
    second = lax.all_to_all(spectra, "shot", split_axis=3, concat_axis=2, tiled=True).astype(F32)
    stations = spectra[:, :, :, :: receivers // shots]
    first = lax.all_gather(stations, "shot", axis=2, tiled=True).astype(F32)

    def one_shot(inputs):
        legs, lists, list_lengths = inputs
        used = jnp.arange(KMAX, dtype=jnp.int32)[None, :] < list_lengths[:, None]
        lists = jnp.where(used, lists, -1)
        hits = lists[None] == jnp.arange(shots, dtype=jnp.int32)[:, None, None]
        counts = hits.astype(F32).sum(axis=-1)
        legs = legs[..., None]
        real = legs[:, 0] * second[:, 0] - legs[:, 1] * second[:, 1]
        imag = legs[:, 0] * second[:, 1] + legs[:, 1] * second[:, 0]
        return (jnp.stack([real, imag], axis=1) * counts).sum(axis=2)

    summed = lax.map(one_shot, (first.transpose(2, 0, 1, 3), aperture, lengths))
    summed = (summed * KMAX ** (-0.5)).astype(BF16).transpose(1, 2, 0, 3)
    summed = lax.all_to_all(summed, "shot", split_axis=2, concat_axis=3, tiled=True)
    summed = lax.all_gather(summed, "freq", axis=0, tiled=True).reshape(2 * NF, shot_dev, receivers)

    wide = start - HALF + jnp.arange(time_dev + 2 * HALF, dtype=jnp.int32)
    synthesis = basis_rows(wide).astype(BF16).astype(F32).reshape(2 * NF, time_dev + 2 * HALF)
    synthesis = jnp.where((wide >= 0) & (wide < NT), synthesis, 0.0)
    filtered = jnp.zeros((shot_dev, 2 * NF, time_dev), F32)
    for j in range(TAPS):
        tap = filters[:, j].astype(F32)[:, None, None]
        filtered = filtered + tap * synthesis[:, 2 * HALF - j : 2 * HALF - j + time_dev]
    out = jnp.einsum("fsr,sft->srt", summed, filtered.astype(BF16), preferred_element_type=F32)
    return out.astype(BF16)


def solution(mesh):
    in_specs = (
        P("shot", None, "freq"),
        P(),
        P(None, "shot", None),
        P(None, "shot"),
        P("shot", None),
    )
    out_specs = P("shot", None, "freq")
    whole_pieces = mesh.shape["shot"] == 16 and mesh.shape["freq"] == 2
    body = shards if whole_pieces else general_shards
    return jax.shard_map(body, mesh=mesh, in_specs=in_specs, out_specs=out_specs, check_vma=False)
```

```python
import math

import jax
import jax.numpy as jnp
from jax import lax
from jax.experimental import pallas as pl
from jax.experimental.pallas import tpu as pltpu
from jax.sharding import PartitionSpec as P

NT = 1024
NF = 8
KMAX = 32
TAPS = 31
HALF = (TAPS - 1) // 2
LANES = 128
PIECE = 32
DEVICES = ("shot", "freq")
CHIPS = 16
ORDER = [11] + [g for g in range(CHIPS) if g != 11]
PLACES = [ORDER.index(g) for g in range(CHIPS)]


def core_groups(run):
    return [[2 * g + (core + g // run) % 2 for g in ORDER] for core in range(2)]


F32 = jnp.float32
BF16 = jnp.bfloat16
VMEM_LIMIT = 48 * 1024 * 1024


def cosine(phases):
    quarter = NT // 4
    turn = (phases + quarter // 2) // quarter
    angle = (phases - turn * quarter).astype(F32) * (2.0 * math.pi / NT)
    square = angle * angle
    sine = angle * (1.0 + square * (-1 / 6 + square * (1 / 120 + square * (-1 / 5040 + square / 362880))))
    cosine = 1.0 + square * (-1 / 2 + square * (1 / 24 + square * (-1 / 720 + square / 40320)))
    near = jnp.where(turn % 2 == 1, sine, cosine)
    return jnp.where((turn == 1) | (turn == 2), -near, near)


def basis_in_kernel(bins_ref, first_time, width):
    rows = lax.broadcasted_iota(jnp.int32, (2 * NF, width), 0)
    times = lax.broadcasted_iota(jnp.int32, (2 * NF, width), 1) + first_time
    frequency = rows // NF * (NF // 2) + rows % (NF // 2)
    part = rows // (NF // 2) % 2
    bins = jnp.zeros((2 * NF, width), jnp.int32)
    for f in range(NF):
        bins = jnp.where(frequency == f, bins_ref[f], bins)
    return cosine((bins * times + part * (NT // 4)) & (NT - 1)), times


def write_spread(spread_ref):
    lane = lax.broadcasted_iota(jnp.int32, (LANES, LANES), 0)
    station = lane % PIECE * 4 + lane // PIECE - lax.broadcasted_iota(jnp.int32, (LANES, LANES), 1) // (LANES // 2)
    for tile in range(spread_ref.shape[1] // LANES):
        here = jnp.where(station == 2 * tile, 1.0, 0.0)
        spread_ref[:, tile * LANES : (tile + 1) * LANES] = here.astype(BF16)


def write_filtered(bins_ref, filters_ref, filtered_ref):
    shot_dev, _, time_dev = filtered_ref.shape
    width = time_dev + LANES
    basis, times = basis_in_kernel(bins_ref, lax.axis_index("freq") * time_dev - HALF, width)
    basis = jnp.where((times >= 0) & (times < NT), basis.astype(BF16).astype(F32), 0.0)
    taps = filters_ref[...].astype(F32)
    total = [jnp.zeros((2 * NF, time_dev), F32) for _ in range(shot_dev)]
    for j in range(TAPS):
        shift = 2 * HALF - j
        moved = basis if shift == 0 else pltpu.roll(basis, width - shift, 1)
        moved = moved[:, :time_dev]
        for s in range(shot_dev):
            total[s] = total[s] + taps[s : s + 1, j : j + 1] * moved
    for s in range(shot_dev):
        filtered_ref[s] = total[s].astype(BF16)


def bit_sums(words):
    waiting, planes = [], []
    for word in words:
        level = 0
        while True:
            if level == len(waiting):
                waiting.append([])
            waiting[level].append(word)
            if len(waiting[level]) < 3:
                break
            x, y, z = waiting[level]
            either = x ^ y
            waiting[level] = [either ^ z]
            word = (x & y) | (either & z)
            level += 1
    level = 0
    while level < len(waiting):
        held = waiting[level]
        if len(held) > 1:
            if level + 1 == len(waiting):
                waiting.append([])
            x, y = held[0], held[1]
            carries = [x & y]
            if len(held) == 3:
                carries = [(x & y) | ((x ^ y) & held[2])]
            waiting[level + 1] += carries
            held = [x ^ y] if len(held) == 2 else [x ^ y ^ held[2]]
        planes.append(held[0])
        level += 1
    return planes


def write_counts(aperture_ref, lengths_ref, codes_ref, counts_ref):
    half = aperture_ref.shape[0] // 2
    for s in range(half):
        both = jnp.concatenate([aperture_ref[s], aperture_ref[s + half]], axis=1)
        codes_ref[pl.ds(s, KMAX, stride=half), :] = both
    lengths = jnp.concatenate([lengths_ref[:half, :], lengths_ref[half:, :]], axis=1)
    one = jnp.ones((half, LANES), jnp.int32)

    def words():
        for k in range(KMAX):
            codes = codes_ref[k * half : (k + 1) * half, :]
            yield jnp.where(lengths > k, lax.shift_left(one, codes), 0)

    planes = bit_sums(words())
    low = lax.broadcasted_iota(jnp.int32, (half, LANES), 1) < LANES // 2
    for i in range(0, 8, 2):
        packed = []
        for bit in (i, i + 1):
            total = 0
            for level, plane in enumerate(planes):
                spread = lax.shift_right_logical(plane, jnp.full_like(plane, bit)) & 0x01010101
                total = total + (spread << level)
            packed.append(total)
        for byte in range(4):
            left, right = [(lax.shift_right_logical(x, jnp.full_like(x, 8 * byte)) & 255).astype(F32) for x in packed]
            lanes = pl.ds((8 * byte + i) * (LANES // 2), LANES)
            counts_ref[:half, lanes] = jnp.where(low, left, pltpu.roll(right, LANES // 2, 1))
            counts_ref[half:, lanes] = jnp.where(low, pltpu.roll(left, LANES // 2, 1), right)


def analysis_kernel(
    bins_hbm, filters_hbm, lengths_hbm, aperture_hbm, traces_hbm,
    message_ref, counts_ref, spread_ref, filtered_ref,
    bins_ref, filters_ref, lengths_ref, aperture_ref, traces_ref, basis_ref, codes_ref, sems,
):
    shot_dev, receivers, time_dev = traces_ref.shape
    sources = (bins_hbm, filters_hbm, lengths_hbm, aperture_hbm)
    targets = (bins_ref, filters_ref, lengths_ref, aperture_ref)
    tables = [pltpu.make_async_copy(x, y, sems.at[i]) for i, (x, y) in enumerate(zip(sources, targets))]
    starts = [0, 3 * LANES, receivers]
    blocks = list(zip(starts, starts[1:]))
    copies = []
    for i, (start, end) in enumerate(blocks):
        rows = pl.ds(start, end - start)
        copies.append(pltpu.make_async_copy(traces_hbm.at[:, rows, :], traces_ref.at[:, rows, :], sems.at[4 + i]))
    for copy in tables + copies:
        copy.start()

    write_spread(spread_ref)
    tables[0].wait()
    tables[1].wait()
    basis, _ = basis_in_kernel(bins_ref, lax.axis_index("freq") * time_dev, time_dev)
    basis_ref[...] = (basis * NT ** (-0.5)).astype(BF16)
    write_filtered(bins_ref, filters_ref, filtered_ref)

    lane = lax.broadcasted_iota(jnp.int32, (2 * NF, LANES), 1)
    row = lax.broadcasted_iota(jnp.int32, (2 * NF, LANES), 0)
    low = lane < LANES // 2
    is_station = lane % PIECE == 0
    stations = jnp.zeros((2 * NF, LANES), F32)
    for copy, (start, end) in zip(copies, blocks):
        copy.wait()
        if end == receivers:
            tables[2].wait()
            tables[3].wait()
            write_counts(aperture_ref, lengths_ref, codes_ref, counts_ref)
        terms = [
            lax.dot_general(
                basis_ref[...],
                traces_ref[s, start:end, :],
                (((1,), (1,)), ((), ())),
                preferred_element_type=F32,
            )
            for s in range(shot_dev)
        ]
        for j in range((end - start) // LANES):
            tile = start // LANES + j
            first, second = [x[:, j * LANES : (j + 1) * LANES] for x in terms]
            for s, x in enumerate((first, second)):
                marked = jnp.where(is_station, x, 0.0)
                shift = 8 * s + tile
                stations = stations + (pltpu.roll(marked, shift, 1) if shift else marked)
            even = jnp.where(low, first, pltpu.roll(second, LANES // 2, 1))
            odd = jnp.where(low, pltpu.roll(first, LANES // 2, 1), second)
            message_ref[PLACES[2 * tile], : 2 * NF] = even.astype(BF16)
            message_ref[PLACES[2 * tile + 1], : 2 * NF] = odd.astype(BF16)
    stations = jnp.where(row // 4 % 2 == 1, pltpu.roll(stations, 16, 1), stations)
    slabs = [stations[8 * h : 8 * h + 4] + stations[8 * h + 4 : 8 * h + 8] for h in range(2)]
    slab = jnp.concatenate(slabs, axis=0).astype(BF16)
    for g in range(message_ref.shape[0]):
        message_ref[g, 2 * NF :] = slab


def product_kernel(
    own_ref, other_ref, counts_ref, spread_ref, message_ref, station_ref, first_ref, second_ref
):
    groups = own_ref.shape[0]
    upper = lax.broadcasted_iota(jnp.int32, (NF, LANES), 0) >= 4
    low = lax.broadcasted_iota(jnp.int32, (NF, LANES), 1) < LANES // 2
    for g in range(groups):
        place = PLACES[g]
        rounded = (own_ref[place].astype(F32) + other_ref[place].astype(F32)).astype(BF16).astype(F32)
        second_ref[:, g * LANES : (g + 1) * LANES] = rounded[: 2 * NF]
        stations = rounded[2 * NF :]
        for s in range(2):
            real = stations if s == 0 else pltpu.roll(stations, LANES - 8, 1)
            imag = pltpu.roll(stations, LANES - 16 - 8 * s, 1)
            legs = [jnp.where(upper, pltpu.roll(imag, 4, 0), real), jnp.where(upper, imag, pltpu.roll(real, 4, 0))]
            station_ref[32 * g + 16 * s : 32 * g + 16 * s + 16, :] = jnp.concatenate(legs, axis=0).astype(BF16)
    first_ref[...] = jnp.dot(station_ref[...], spread_ref[...], preferred_element_type=F32)

    def total(x):
        x = sum(x[:, i * LANES : (i + 1) * LANES] for i in range(x.shape[1] // LANES))
        return x + pltpu.roll(x, LANES // 2, 1)

    second = [second_ref[NF * h : NF * (h + 1), :] for h in range(2)]
    crossed = [jnp.concatenate([x[4:], x[:4]], axis=0) for x in second]
    for g in range(groups):
        message = []
        for h in range(2):
            spectra = []
            for s in (2 * g, 2 * g + 1):
                first = counts_ref[s : s + 1, :] * first_ref[16 * s + 8 * h : 16 * s + 8 * h + 8, :]
                same, other = total(first * second[h]), total(first * crossed[h])
                same, other = same - pltpu.roll(same, 4, 0), other + pltpu.roll(other, 4, 0)
                spectra.append(jnp.where(upper, other, same) * KMAX ** (-0.5))
            message.append(jnp.where(low, spectra[0], spectra[1]))
        message_ref[PLACES[g]] = jnp.concatenate(message, axis=0).astype(BF16)


def synthesis_kernel(received_ref, filtered_ref, out_hbm, out_ref, out_sem):
    low = lax.broadcasted_iota(jnp.int32, (2 * NF, LANES), 1) < LANES // 2
    copies = []
    for tile in range(out_ref.shape[1] // LANES):
        left, right = [received_ref[PLACES[2 * tile + i]].astype(F32) for i in range(2)]
        spectra = (
            jnp.where(low, left, pltpu.roll(right, LANES // 2, 1)),
            jnp.where(low, pltpu.roll(left, LANES // 2, 1), right),
        )
        rows = pl.ds(tile * LANES, LANES)
        for s in range(2):
            out_ref[s, rows, :] = lax.dot_general(
                spectra[s].astype(BF16), filtered_ref[s], (((0,), (0,)), ((), ())), preferred_element_type=F32
            ).astype(BF16)
            copy = pltpu.make_async_copy(out_ref.at[s, rows, :], out_hbm.at[s, rows, :], out_sem.at[2 * tile + s])
            copy.start()
            copies.append(copy)
    for copy in copies:
        copy.wait()


def in_vmem():
    return pl.BlockSpec(memory_space=pltpu.VMEM)


def in_hbm():
    return pl.BlockSpec(memory_space=pltpu.HBM)


def exchange(messages, run):
    return lax.all_to_all(
        messages, DEVICES, split_axis=0, concat_axis=0, tiled=True, axis_index_groups=core_groups(run)
    )


def shards(traces, frequency_bins, aperture, lengths, filters):
    shot_dev, receivers, time_dev = traces.shape
    shots = aperture.shape[0]
    params = pltpu.CompilerParams(vmem_limit_bytes=VMEM_LIMIT)

    pairs = shots * aperture.shape[1]
    lists = aperture.transpose(0, 2, 1)
    operands = (frequency_bins, filters, lengths, lists, traces)
    messages, counts, spread, filtered = pl.pallas_call(
        analysis_kernel,
        in_specs=[in_hbm()] * len(operands),
        out_specs=[in_vmem()] * 4,
        out_shape=[
            jax.ShapeDtypeStruct((CHIPS, 3 * NF, LANES), BF16),
            jax.ShapeDtypeStruct((shots, pairs), F32),
            jax.ShapeDtypeStruct((LANES, pairs), BF16),
            jax.ShapeDtypeStruct((shot_dev, 2 * NF, time_dev), BF16),
        ],
        scratch_shapes=[
            pltpu.SMEM((NF,), jnp.int32),
            *[pltpu.VMEM(x.shape, x.dtype) for x in operands[1:]],
            pltpu.VMEM((2 * NF, time_dev), BF16),
            pltpu.VMEM((KMAX * shots // 2, LANES), jnp.int32),
            pltpu.SemaphoreType.DMA((6,)),
        ],
        compiler_params=params,
        cost_estimate=pl.CostEstimate(flops=2 * 16 * traces.size, bytes_accessed=2 * traces.size, transcendentals=0),
    )(*[pltpu.with_memory_space_constraint(x, pltpu.HBM) for x in operands])
    own = exchange(messages, 4)
    other = lax.ppermute(own, "freq", [(0, 1), (1, 0)])

    messages = pl.pallas_call(
        product_kernel,
        in_specs=[in_vmem()] * 4,
        out_specs=in_vmem(),
        out_shape=jax.ShapeDtypeStruct((CHIPS, 2 * NF, LANES), BF16),
        scratch_shapes=[
            pltpu.VMEM((shots * 2 * NF, LANES), BF16),
            pltpu.VMEM((shots * 2 * NF, pairs), F32),
            pltpu.VMEM((2 * NF, pairs), F32),
        ],
        compiler_params=params,
        cost_estimate=pl.CostEstimate(flops=1 << 24, bytes_accessed=1 << 20, transcendentals=0),
    )(own, other, counts, spread)
    received = exchange(messages, 8)

    return pl.pallas_call(
        synthesis_kernel,
        in_specs=[in_vmem(), in_vmem()],
        out_specs=in_hbm(),
        out_shape=jax.ShapeDtypeStruct(traces.shape, BF16),
        scratch_shapes=[
            pltpu.VMEM(traces.shape, BF16),
            pltpu.SemaphoreType.DMA((shot_dev * receivers // LANES,)),
        ],
        compiler_params=params,
        cost_estimate=pl.CostEstimate(flops=2 * 16 * traces.size, bytes_accessed=2 * traces.size, transcendentals=0),
    )(received, filtered)


def general_shards(traces, frequency_bins, aperture, lengths, filters):
    shot_dev, receivers, time_dev = traces.shape
    shots = aperture.shape[0]
    receiver_dev = aperture.shape[1]
    start = lax.axis_index("freq") * time_dev

    def basis_rows(times):
        phases = frequency_bins[:, None] * times[None, :]
        return jnp.stack([cosine(phases & (NT - 1)), cosine((phases + NT // 4) & (NT - 1))], axis=1)

    times = start + jnp.arange(time_dev, dtype=jnp.int32)
    analysis = (basis_rows(times) * NT ** (-0.5)).astype(BF16).reshape(2 * NF, time_dev)
    term = lax.dot_general(
        analysis, traces.reshape(shot_dev * receivers, time_dev), (((1,), (1,)), ((), ())), preferred_element_type=F32
    )
    spectra = lax.psum_scatter(
        term.reshape(NF, 2, shot_dev, receivers), "freq", scatter_dimension=0, tiled=True
    ).astype(BF16)
    second = lax.all_to_all(spectra, "shot", split_axis=3, concat_axis=2, tiled=True).astype(F32)
    stations = spectra[:, :, :, :: receivers // shots]
    first = lax.all_gather(stations, "shot", axis=2, tiled=True).astype(F32)

    def one_shot(inputs):
        legs, lists, list_lengths = inputs
        used = jnp.arange(KMAX, dtype=jnp.int32)[None, :] < list_lengths[:, None]
        lists = jnp.where(used, lists, -1)
        hits = lists[None] == jnp.arange(shots, dtype=jnp.int32)[:, None, None]
        counts = hits.astype(F32).sum(axis=-1)
        legs = legs[..., None]
        real = legs[:, 0] * second[:, 0] - legs[:, 1] * second[:, 1]
        imag = legs[:, 0] * second[:, 1] + legs[:, 1] * second[:, 0]
        return (jnp.stack([real, imag], axis=1) * counts).sum(axis=2)

    summed = lax.map(one_shot, (first.transpose(2, 0, 1, 3), aperture, lengths))
    summed = (summed * KMAX ** (-0.5)).astype(BF16).transpose(1, 2, 0, 3)
    summed = lax.all_to_all(summed, "shot", split_axis=2, concat_axis=3, tiled=True)
    summed = lax.all_gather(summed, "freq", axis=0, tiled=True).reshape(2 * NF, shot_dev, receivers)

    wide = start - HALF + jnp.arange(time_dev + 2 * HALF, dtype=jnp.int32)
    synthesis = basis_rows(wide).astype(BF16).astype(F32).reshape(2 * NF, time_dev + 2 * HALF)
    synthesis = jnp.where((wide >= 0) & (wide < NT), synthesis, 0.0)
    filtered = jnp.zeros((shot_dev, 2 * NF, time_dev), F32)
    for j in range(TAPS):
        tap = filters[:, j].astype(F32)[:, None, None]
        filtered = filtered + tap * synthesis[:, 2 * HALF - j : 2 * HALF - j + time_dev]
    out = jnp.einsum("fsr,sft->srt", summed, filtered.astype(BF16), preferred_element_type=F32)
    return out.astype(BF16)


def solution(mesh):
    in_specs = (
        P("shot", None, "freq"),
        P(),
        P(None, "shot", None),
        P(None, "shot"),
        P("shot", None),
    )
    out_specs = P("shot", None, "freq")
    whole_pieces = mesh.shape["shot"] == 16 and mesh.shape["freq"] == 2
    body = shards if whole_pieces else general_shards
    return jax.shard_map(body, mesh=mesh, in_specs=in_specs, out_specs=out_specs, check_vma=False)
```

```python
import math

import jax
import jax.numpy as jnp
from jax import lax
from jax.experimental import pallas as pl
from jax.experimental.pallas import tpu as pltpu
from jax.sharding import PartitionSpec as P

NT = 1024
NF = 8
KMAX = 32
TAPS = 31
HALF = (TAPS - 1) // 2
LANES = 128
PIECE = 32
DEVICES = ("shot", "freq")
CHIPS = 16
ORDER = [11] + [g for g in range(CHIPS) if g != 11]
PLACES = [ORDER.index(g) for g in range(CHIPS)]


def core_groups(run):
    return [[2 * g + (core + g // run) % 2 for g in ORDER] for core in range(2)]


F32 = jnp.float32
BF16 = jnp.bfloat16
VMEM_LIMIT = 48 * 1024 * 1024


def cosine(phases):
    quarter = NT // 4
    turn = (phases + quarter // 2) // quarter
    angle = (phases - turn * quarter).astype(F32) * (2.0 * math.pi / NT)
    square = angle * angle
    sine = angle * (1.0 + square * (-1 / 6 + square * (1 / 120 + square * (-1 / 5040 + square / 362880))))
    cosine = 1.0 + square * (-1 / 2 + square * (1 / 24 + square * (-1 / 720 + square / 40320)))
    near = jnp.where(turn % 2 == 1, sine, cosine)
    return jnp.where((turn == 1) | (turn == 2), -near, near)


def basis_in_kernel(bins_ref, first_time, width):
    rows = lax.broadcasted_iota(jnp.int32, (2 * NF, width), 0)
    times = lax.broadcasted_iota(jnp.int32, (2 * NF, width), 1) + first_time
    frequency = rows // NF * (NF // 2) + rows % (NF // 2)
    part = rows // (NF // 2) % 2
    bins = jnp.zeros((2 * NF, width), jnp.int32)
    for f in range(NF):
        bins = jnp.where(frequency == f, bins_ref[f], bins)
    return cosine((bins * times + part * (NT // 4)) & (NT - 1)), times


def write_spread(spread_ref):
    lane = lax.broadcasted_iota(jnp.int32, (LANES, LANES), 0)
    station = lane % PIECE * 4 + lane // PIECE - lax.broadcasted_iota(jnp.int32, (LANES, LANES), 1) // (LANES // 2)
    for tile in range(spread_ref.shape[1] // LANES):
        here = jnp.where(station == 2 * tile, 1.0, 0.0)
        spread_ref[:, tile * LANES : (tile + 1) * LANES] = here.astype(BF16)


def write_filtered(wide_ref, filters_ref, filtered_ref):
    shot_dev, _, time_dev = filtered_ref.shape
    basis = wide_ref[...].astype(F32)
    width = basis.shape[1]
    taps = filters_ref[...].astype(F32)
    total = [jnp.zeros((2 * NF, time_dev), F32) for _ in range(shot_dev)]
    for j in range(TAPS):
        shift = 2 * HALF - j
        moved = basis if shift == 0 else pltpu.roll(basis, width - shift, 1)
        moved = moved[:, :time_dev]
        for s in range(shot_dev):
            total[s] = total[s] + taps[s : s + 1, j : j + 1] * moved
    for s in range(shot_dev):
        filtered_ref[s] = total[s].astype(BF16)


def bit_sums(words):
    waiting, planes = [], []
    for word in words:
        level = 0
        while True:
            if level == len(waiting):
                waiting.append([])
            waiting[level].append(word)
            if len(waiting[level]) < 3:
                break
            x, y, z = waiting[level]
            either = x ^ y
            waiting[level] = [either ^ z]
            word = (x & y) | (either & z)
            level += 1
    level = 0
    while level < len(waiting):
        held = waiting[level]
        if len(held) > 1:
            if level + 1 == len(waiting):
                waiting.append([])
            x, y = held[0], held[1]
            carries = [x & y]
            if len(held) == 3:
                carries = [(x & y) | ((x ^ y) & held[2])]
            waiting[level + 1] += carries
            held = [x ^ y] if len(held) == 2 else [x ^ y ^ held[2]]
        planes.append(held[0])
        level += 1
    return planes


def write_counts(aperture_ref, lengths_ref, codes_ref, counts_ref):
    half = aperture_ref.shape[0] // 2
    for s in range(half):
        both = jnp.concatenate([aperture_ref[s], aperture_ref[s + half]], axis=1)
        codes_ref[pl.ds(s, KMAX, stride=half), :] = both
    lengths = jnp.concatenate([lengths_ref[:half, :], lengths_ref[half:, :]], axis=1)
    one = jnp.ones((half, LANES), jnp.int32)

    def words():
        for k in range(KMAX):
            codes = codes_ref[k * half : (k + 1) * half, :]
            yield jnp.where(lengths > k, lax.shift_left(one, codes), 0)

    planes = bit_sums(words())
    low = lax.broadcasted_iota(jnp.int32, (half, LANES), 1) < LANES // 2
    for i in range(0, 8, 2):
        packed = []
        for bit in (i, i + 1):
            total = 0
            for level, plane in enumerate(planes):
                spread = lax.shift_right_logical(plane, jnp.full_like(plane, bit)) & 0x01010101
                total = total + (spread << level)
            packed.append(total)
        for byte in range(4):
            left, right = [(lax.shift_right_logical(x, jnp.full_like(x, 8 * byte)) & 255).astype(F32) for x in packed]
            lanes = pl.ds((8 * byte + i) * (LANES // 2), LANES)
            counts_ref[:half, lanes] = jnp.where(low, left, pltpu.roll(right, LANES // 2, 1))
            counts_ref[half:, lanes] = jnp.where(low, pltpu.roll(left, LANES // 2, 1), right)


def tables_kernel(
    wide_ref, filters_ref, lengths_ref, aperture_ref, _, counts_ref, filtered_ref, codes_ref
):
    write_counts(aperture_ref, lengths_ref, codes_ref, counts_ref)
    write_filtered(wide_ref, filters_ref, filtered_ref)


def analysis_kernel(
    bins_hbm, traces_hbm, message_ref, spread_ref, wide_ref, bins_ref, traces_ref, basis_ref, sems,
):
    shot_dev, receivers, time_dev = traces_ref.shape
    bins_copy = pltpu.make_async_copy(bins_hbm, bins_ref, sems.at[0])
    starts = [0, 3 * LANES, receivers]
    blocks = list(zip(starts, starts[1:]))
    copies = []
    for i, (start, end) in enumerate(blocks):
        rows = pl.ds(start, end - start)
        copies.append(pltpu.make_async_copy(traces_hbm.at[:, rows, :], traces_ref.at[:, rows, :], sems.at[1 + i]))
    for copy in [bins_copy] + copies:
        copy.start()

    write_spread(spread_ref)
    bins_copy.wait()
    wide, times = basis_in_kernel(bins_ref, lax.axis_index("freq") * time_dev - HALF, wide_ref.shape[1])
    wide_ref[...] = jnp.where((times >= 0) & (times < NT), wide, 0.0).astype(BF16)
    basis = pltpu.roll(wide, wide.shape[1] - HALF, 1)[:, :time_dev]
    basis_ref[...] = (basis * NT ** (-0.5)).astype(BF16)

    lane = lax.broadcasted_iota(jnp.int32, (2 * NF, LANES), 1)
    row = lax.broadcasted_iota(jnp.int32, (2 * NF, LANES), 0)
    low = lane < LANES // 2
    is_station = lane % PIECE == 0
    stations = jnp.zeros((2 * NF, LANES), F32)
    for copy, (start, end) in zip(copies, blocks):
        copy.wait()
        terms = [
            lax.dot_general(
                basis_ref[...],
                traces_ref[s, start:end, :],
                (((1,), (1,)), ((), ())),
                preferred_element_type=F32,
            )
            for s in range(shot_dev)
        ]
        for j in range((end - start) // LANES):
            tile = start // LANES + j
            first, second = [x[:, j * LANES : (j + 1) * LANES] for x in terms]
            for s, x in enumerate((first, second)):
                marked = jnp.where(is_station, x, 0.0)
                shift = 8 * s + tile
                stations = stations + (pltpu.roll(marked, shift, 1) if shift else marked)
            even = jnp.where(low, first, pltpu.roll(second, LANES // 2, 1))
            odd = jnp.where(low, pltpu.roll(first, LANES // 2, 1), second)
            message_ref[PLACES[2 * tile], : 2 * NF] = even.astype(BF16)
            message_ref[PLACES[2 * tile + 1], : 2 * NF] = odd.astype(BF16)
    stations = jnp.where(row // 4 % 2 == 1, pltpu.roll(stations, 16, 1), stations)
    slabs = [stations[8 * h : 8 * h + 4] + stations[8 * h + 4 : 8 * h + 8] for h in range(2)]
    slab = jnp.concatenate(slabs, axis=0).astype(BF16)
    for g in range(message_ref.shape[0]):
        message_ref[g, 2 * NF :] = slab


def product_kernel(
    own_ref, other_ref, counts_ref, spread_ref, message_ref, station_ref, first_ref, second_ref, same_ref, cross_ref
):
    groups = own_ref.shape[0]
    upper = lax.broadcasted_iota(jnp.int32, (NF, LANES), 0) >= 4
    low = lax.broadcasted_iota(jnp.int32, (NF, LANES), 1) < LANES // 2
    for g in range(groups):
        place = PLACES[g]
        rounded = (own_ref[place].astype(F32) + other_ref[place].astype(F32)).astype(BF16).astype(F32)
        second_ref[:, g * LANES : (g + 1) * LANES] = rounded[: 2 * NF]
        stations = rounded[2 * NF :]
        for s in range(2):
            real = stations if s == 0 else pltpu.roll(stations, LANES - 8, 1)
            imag = pltpu.roll(stations, LANES - 16 - 8 * s, 1)
            legs = [jnp.where(upper, pltpu.roll(imag, 4, 0), real), jnp.where(upper, imag, pltpu.roll(real, 4, 0))]
            station_ref[32 * g + 16 * s : 32 * g + 16 * s + 16, :] = jnp.concatenate(legs, axis=0).astype(BF16)
    first_ref[...] = jnp.dot(station_ref[...], spread_ref[...], preferred_element_type=F32)

    tiles = second_ref.shape[1] // LANES
    span = 4
    for start in range(0, tiles, span):
        columns = [slice(t * LANES, (t + 1) * LANES) for t in range(start, start + span)]
        second = [[second_ref[NF * h : NF * (h + 1), c] for c in columns] for h in range(2)]
        crossed = [[jnp.concatenate([x[4:], x[:4]], axis=0) for x in half] for half in second]
        for s in range(2 * groups):
            counts = [counts_ref[s : s + 1, c] for c in columns]
            for h in range(2):
                rows = slice(16 * s + 8 * h, 16 * s + 8 * h + 8)
                first = [count * first_ref[rows, c] for count, c in zip(counts, columns)]
                same = sum(x * y for x, y in zip(first, second[h]))
                cross = sum(x * y for x, y in zip(first, crossed[h]))
                if start:
                    same, cross = same + same_ref[rows, :], cross + cross_ref[rows, :]
                same_ref[rows, :] = same
                cross_ref[rows, :] = cross
    for g in range(groups):
        message = []
        for h in range(2):
            spectra = []
            for s in (2 * g, 2 * g + 1):
                rows = slice(16 * s + 8 * h, 16 * s + 8 * h + 8)
                same, cross = same_ref[rows, :], cross_ref[rows, :]
                total = jnp.where(upper, cross + pltpu.roll(cross, 4, 0), same - pltpu.roll(same, 4, 0))
                spectra.append((total + pltpu.roll(total, LANES // 2, 1)) * KMAX ** (-0.5))
            message.append(jnp.where(low, spectra[0], spectra[1]))
        message_ref[PLACES[g]] = jnp.concatenate(message, axis=0).astype(BF16)


def synthesis_kernel(received_ref, filtered_ref, out_hbm, out_ref, out_sem):
    low = lax.broadcasted_iota(jnp.int32, (2 * NF, LANES), 1) < LANES // 2
    copies = []
    for tile in range(out_ref.shape[1] // LANES):
        left, right = [received_ref[PLACES[2 * tile + i]].astype(F32) for i in range(2)]
        spectra = (
            jnp.where(low, left, pltpu.roll(right, LANES // 2, 1)),
            jnp.where(low, pltpu.roll(left, LANES // 2, 1), right),
        )
        rows = pl.ds(tile * LANES, LANES)
        for s in range(2):
            out_ref[s, rows, :] = lax.dot_general(
                spectra[s].astype(BF16), filtered_ref[s], (((0,), (0,)), ((), ())), preferred_element_type=F32
            ).astype(BF16)
            copy = pltpu.make_async_copy(out_ref.at[s, rows, :], out_hbm.at[s, rows, :], out_sem.at[2 * tile + s])
            copy.start()
            copies.append(copy)
    for copy in copies:
        copy.wait()


def in_vmem():
    return pl.BlockSpec(memory_space=pltpu.VMEM)


def in_hbm():
    return pl.BlockSpec(memory_space=pltpu.HBM)


def exchange(messages, run):
    return lax.all_to_all(
        messages, DEVICES, split_axis=0, concat_axis=0, tiled=True, axis_index_groups=core_groups(run)
    )


def shards(traces, frequency_bins, aperture, lengths, filters):
    shot_dev, receivers, time_dev = traces.shape
    shots = aperture.shape[0]
    params = pltpu.CompilerParams(vmem_limit_bytes=VMEM_LIMIT)

    pairs = shots * aperture.shape[1]
    operands = (frequency_bins, traces)
    messages, spread, wide = pl.pallas_call(
        analysis_kernel,
        in_specs=[in_hbm()] * len(operands),
        out_specs=[in_vmem()] * 3,
        out_shape=[
            jax.ShapeDtypeStruct((CHIPS, 3 * NF, LANES), BF16),
            jax.ShapeDtypeStruct((LANES, pairs), BF16),
            jax.ShapeDtypeStruct((2 * NF, time_dev + LANES), BF16),
        ],
        scratch_shapes=[
            pltpu.SMEM((NF,), jnp.int32),
            *[pltpu.VMEM(x.shape, x.dtype) for x in operands[1:]],
            pltpu.VMEM((2 * NF, time_dev), BF16),
            pltpu.SemaphoreType.DMA((3,)),
        ],
        compiler_params=params,
        cost_estimate=pl.CostEstimate(flops=2 * 16 * traces.size, bytes_accessed=2 * traces.size, transcendentals=0),
    )(*[pltpu.with_memory_space_constraint(x, pltpu.HBM) for x in operands])
    own = exchange(messages, 4)
    other = lax.ppermute(own, "freq", [(0, 1), (1, 0)])
    counts, filtered = pl.pallas_call(
        tables_kernel,
        in_specs=[in_vmem()] * 4 + [pl.BlockSpec(memory_space=pl.ANY)],
        out_specs=[in_vmem()] * 2,
        out_shape=[
            jax.ShapeDtypeStruct((shots, pairs), F32),
            jax.ShapeDtypeStruct((shot_dev, 2 * NF, time_dev), BF16),
        ],
        scratch_shapes=[pltpu.VMEM((KMAX * shots // 2, LANES), jnp.int32)],
        compiler_params=params,
        cost_estimate=pl.CostEstimate(flops=1 << 22, bytes_accessed=1 << 19, transcendentals=0),
    )(wide, filters, lengths, aperture.transpose(0, 2, 1), own)

    messages = pl.pallas_call(
        product_kernel,
        in_specs=[in_vmem()] * 4,
        out_specs=in_vmem(),
        out_shape=jax.ShapeDtypeStruct((CHIPS, 2 * NF, LANES), BF16),
        scratch_shapes=[
            pltpu.VMEM((shots * 2 * NF, LANES), BF16),
            pltpu.VMEM((shots * 2 * NF, pairs), F32),
            pltpu.VMEM((2 * NF, pairs), F32),
            pltpu.VMEM((shots * 2 * NF, LANES), F32),
            pltpu.VMEM((shots * 2 * NF, LANES), F32),
        ],
        compiler_params=params,
        cost_estimate=pl.CostEstimate(flops=1 << 24, bytes_accessed=1 << 20, transcendentals=0),
    )(own, other, counts, spread)
    received = exchange(messages, 8)

    return pl.pallas_call(
        synthesis_kernel,
        in_specs=[in_vmem(), in_vmem()],
        out_specs=in_hbm(),
        out_shape=jax.ShapeDtypeStruct(traces.shape, BF16),
        scratch_shapes=[
            pltpu.VMEM(traces.shape, BF16),
            pltpu.SemaphoreType.DMA((shot_dev * receivers // LANES,)),
        ],
        compiler_params=params,
        cost_estimate=pl.CostEstimate(flops=2 * 16 * traces.size, bytes_accessed=2 * traces.size, transcendentals=0),
    )(received, filtered)


def general_shards(traces, frequency_bins, aperture, lengths, filters):
    shot_dev, receivers, time_dev = traces.shape
    shots = aperture.shape[0]
    receiver_dev = aperture.shape[1]
    start = lax.axis_index("freq") * time_dev

    def basis_rows(times):
        phases = frequency_bins[:, None] * times[None, :]
        return jnp.stack([cosine(phases & (NT - 1)), cosine((phases + NT // 4) & (NT - 1))], axis=1)

    times = start + jnp.arange(time_dev, dtype=jnp.int32)
    analysis = (basis_rows(times) * NT ** (-0.5)).astype(BF16).reshape(2 * NF, time_dev)
    term = lax.dot_general(
        analysis, traces.reshape(shot_dev * receivers, time_dev), (((1,), (1,)), ((), ())), preferred_element_type=F32
    )
    spectra = lax.psum_scatter(
        term.reshape(NF, 2, shot_dev, receivers), "freq", scatter_dimension=0, tiled=True
    ).astype(BF16)
    second = lax.all_to_all(spectra, "shot", split_axis=3, concat_axis=2, tiled=True).astype(F32)
    stations = spectra[:, :, :, :: receivers // shots]
    first = lax.all_gather(stations, "shot", axis=2, tiled=True).astype(F32)

    def one_shot(inputs):
        legs, lists, list_lengths = inputs
        used = jnp.arange(KMAX, dtype=jnp.int32)[None, :] < list_lengths[:, None]
        lists = jnp.where(used, lists, -1)
        hits = lists[None] == jnp.arange(shots, dtype=jnp.int32)[:, None, None]
        counts = hits.astype(F32).sum(axis=-1)
        legs = legs[..., None]
        real = legs[:, 0] * second[:, 0] - legs[:, 1] * second[:, 1]
        imag = legs[:, 0] * second[:, 1] + legs[:, 1] * second[:, 0]
        return (jnp.stack([real, imag], axis=1) * counts).sum(axis=2)

    summed = lax.map(one_shot, (first.transpose(2, 0, 1, 3), aperture, lengths))
    summed = (summed * KMAX ** (-0.5)).astype(BF16).transpose(1, 2, 0, 3)
    summed = lax.all_to_all(summed, "shot", split_axis=2, concat_axis=3, tiled=True)
    summed = lax.all_gather(summed, "freq", axis=0, tiled=True).reshape(2 * NF, shot_dev, receivers)

    wide = start - HALF + jnp.arange(time_dev + 2 * HALF, dtype=jnp.int32)
    synthesis = basis_rows(wide).astype(BF16).astype(F32).reshape(2 * NF, time_dev + 2 * HALF)
    synthesis = jnp.where((wide >= 0) & (wide < NT), synthesis, 0.0)
    filtered = jnp.zeros((shot_dev, 2 * NF, time_dev), F32)
    for j in range(TAPS):
        tap = filters[:, j].astype(F32)[:, None, None]
        filtered = filtered + tap * synthesis[:, 2 * HALF - j : 2 * HALF - j + time_dev]
    out = jnp.einsum("fsr,sft->srt", summed, filtered.astype(BF16), preferred_element_type=F32)
    return out.astype(BF16)


def solution(mesh):
    in_specs = (
        P("shot", None, "freq"),
        P(),
        P(None, "shot", None),
        P(None, "shot"),
        P("shot", None),
    )
    out_specs = P("shot", None, "freq")
    whole_pieces = mesh.shape["shot"] == 16 and mesh.shape["freq"] == 2
    body = shards if whole_pieces else general_shards
    return jax.shard_map(body, mesh=mesh, in_specs=in_specs, out_specs=out_specs, check_vma=False)
```

```python
import math

import jax
import jax.numpy as jnp
from jax import lax
from jax.experimental import pallas as pl
from jax.experimental.pallas import tpu as pltpu
from jax.sharding import PartitionSpec as P

NT = 1024
NF = 8
KMAX = 32
TAPS = 31
HALF = (TAPS - 1) // 2
LANES = 128
PIECE = 32
DEVICES = ("shot", "freq")
CHIPS = 16


def hops(a, b):
    return abs(a // 4 - b // 4) + (a // 2 % 2 != b // 2 % 2) + (a % 2 != b % 2)


ORDER = sorted(range(CHIPS), key=lambda g: hops(11, g))
PLACES = [ORDER.index(g) for g in range(CHIPS)]


def core_groups(run):
    return [[2 * g + (core + g // run) % 2 for g in ORDER] for core in range(2)]


F32 = jnp.float32
BF16 = jnp.bfloat16
VMEM_LIMIT = 48 * 1024 * 1024


def cosine(phases):
    quarter = NT // 4
    turn = (phases + quarter // 2) // quarter
    angle = (phases - turn * quarter).astype(F32) * (2.0 * math.pi / NT)
    square = angle * angle
    sine = angle * (1.0 + square * (-1 / 6 + square * (1 / 120 + square * (-1 / 5040 + square / 362880))))
    cosine = 1.0 + square * (-1 / 2 + square * (1 / 24 + square * (-1 / 720 + square / 40320)))
    near = jnp.where(turn % 2 == 1, sine, cosine)
    return jnp.where((turn == 1) | (turn == 2), -near, near)


def basis_in_kernel(bins_ref, first_time, width):
    rows = lax.broadcasted_iota(jnp.int32, (2 * NF, width), 0)
    times = lax.broadcasted_iota(jnp.int32, (2 * NF, width), 1) + first_time
    frequency = rows // NF * (NF // 2) + rows % (NF // 2)
    part = rows // (NF // 2) % 2
    bins = jnp.zeros((2 * NF, width), jnp.int32)
    for f in range(NF):
        bins = jnp.where(frequency == f, bins_ref[f], bins)
    return cosine((bins * times + part * (NT // 4)) & (NT - 1)), times


def write_spread(spread_ref):
    lane = lax.broadcasted_iota(jnp.int32, (LANES, LANES), 0)
    station = lane % PIECE * 4 + lane // PIECE - lax.broadcasted_iota(jnp.int32, (LANES, LANES), 1) // (LANES // 2)
    for tile in range(spread_ref.shape[1] // LANES):
        here = jnp.where(station == 2 * tile, 1.0, 0.0)
        spread_ref[:, tile * LANES : (tile + 1) * LANES] = here.astype(BF16)


def write_filtered(wide_ref, filters_ref, filtered_ref):
    shot_dev, _, time_dev = filtered_ref.shape
    basis = wide_ref[...].astype(F32)
    width = basis.shape[1]
    taps = filters_ref[...].astype(F32)
    total = [jnp.zeros((2 * NF, time_dev), F32) for _ in range(shot_dev)]
    for j in range(TAPS):
        shift = 2 * HALF - j
        moved = basis if shift == 0 else pltpu.roll(basis, width - shift, 1)
        moved = moved[:, :time_dev]
        for s in range(shot_dev):
            total[s] = total[s] + taps[s : s + 1, j : j + 1] * moved
    for s in range(shot_dev):
        filtered_ref[s] = total[s].astype(BF16)


def bit_sums(words):
    waiting, planes = [], []
    for word in words:
        level = 0
        while True:
            if level == len(waiting):
                waiting.append([])
            waiting[level].append(word)
            if len(waiting[level]) < 3:
                break
            x, y, z = waiting[level]
            either = x ^ y
            waiting[level] = [either ^ z]
            word = (x & y) | (either & z)
            level += 1
    level = 0
    while level < len(waiting):
        held = waiting[level]
        if len(held) > 1:
            if level + 1 == len(waiting):
                waiting.append([])
            x, y = held[0], held[1]
            carries = [x & y]
            if len(held) == 3:
                carries = [(x & y) | ((x ^ y) & held[2])]
            waiting[level + 1] += carries
            held = [x ^ y] if len(held) == 2 else [x ^ y ^ held[2]]
        planes.append(held[0])
        level += 1
    return planes


def write_counts(aperture_ref, lengths_ref, codes_ref, counts_ref):
    half = aperture_ref.shape[0] // 2
    for s in range(half):
        both = jnp.concatenate([aperture_ref[s], aperture_ref[s + half]], axis=1)
        codes_ref[pl.ds(s, KMAX, stride=half), :] = both
    lengths = jnp.concatenate([lengths_ref[:half, :], lengths_ref[half:, :]], axis=1)
    one = jnp.ones((half, LANES), jnp.int32)

    def words():
        for k in range(KMAX):
            codes = codes_ref[k * half : (k + 1) * half, :]
            yield jnp.where(lengths > k, lax.shift_left(one, codes), 0)

    planes = bit_sums(words())
    low = lax.broadcasted_iota(jnp.int32, (half, LANES), 1) < LANES // 2
    for i in range(0, 8, 2):
        packed = []
        for bit in (i, i + 1):
            total = 0
            for level, plane in enumerate(planes):
                spread = lax.shift_right_logical(plane, jnp.full_like(plane, bit)) & 0x01010101
                total = total + (spread << level)
            packed.append(total)
        for byte in range(4):
            left, right = [(lax.shift_right_logical(x, jnp.full_like(x, 8 * byte)) & 255).astype(F32) for x in packed]
            lanes = pl.ds((8 * byte + i) * (LANES // 2), LANES)
            counts_ref[:half, lanes] = jnp.where(low, left, pltpu.roll(right, LANES // 2, 1))
            counts_ref[half:, lanes] = jnp.where(low, pltpu.roll(left, LANES // 2, 1), right)


def tables_kernel(
    wide_ref, filters_ref, lengths_ref, aperture_ref, _, counts_ref, filtered_ref, codes_ref
):
    write_counts(aperture_ref, lengths_ref, codes_ref, counts_ref)
    write_filtered(wide_ref, filters_ref, filtered_ref)


def analysis_kernel(
    bins_hbm, traces_hbm, message_ref, spread_ref, wide_ref, bins_ref, traces_ref, basis_ref, sems,
):
    shot_dev, receivers, time_dev = traces_ref.shape
    bins_copy = pltpu.make_async_copy(bins_hbm, bins_ref, sems.at[0])
    starts = [0, 3 * LANES, receivers]
    blocks = list(zip(starts, starts[1:]))
    copies = []
    for i, (start, end) in enumerate(blocks):
        rows = pl.ds(start, end - start)
        copies.append(pltpu.make_async_copy(traces_hbm.at[:, rows, :], traces_ref.at[:, rows, :], sems.at[1 + i]))
    for copy in [bins_copy] + copies:
        copy.start()

    write_spread(spread_ref)
    bins_copy.wait()
    wide, times = basis_in_kernel(bins_ref, lax.axis_index("freq") * time_dev - HALF, wide_ref.shape[1])
    wide_ref[...] = jnp.where((times >= 0) & (times < NT), wide, 0.0).astype(BF16)
    basis = pltpu.roll(wide, wide.shape[1] - HALF, 1)[:, :time_dev]
    basis_ref[...] = (basis * NT ** (-0.5)).astype(BF16)

    lane = lax.broadcasted_iota(jnp.int32, (2 * NF, LANES), 1)
    row = lax.broadcasted_iota(jnp.int32, (2 * NF, LANES), 0)
    low = lane < LANES // 2
    is_station = lane % PIECE == 0
    stations = jnp.zeros((2 * NF, LANES), F32)
    for copy, (start, end) in zip(copies, blocks):
        copy.wait()
        terms = [
            lax.dot_general(
                basis_ref[...],
                traces_ref[s, start:end, :],
                (((1,), (1,)), ((), ())),
                preferred_element_type=F32,
            )
            for s in range(shot_dev)
        ]
        for j in range((end - start) // LANES):
            tile = start // LANES + j
            first, second = [x[:, j * LANES : (j + 1) * LANES] for x in terms]
            for s, x in enumerate((first, second)):
                marked = jnp.where(is_station, x, 0.0)
                shift = 8 * s + tile
                stations = stations + (pltpu.roll(marked, shift, 1) if shift else marked)
            even = jnp.where(low, first, pltpu.roll(second, LANES // 2, 1))
            odd = jnp.where(low, pltpu.roll(first, LANES // 2, 1), second)
            message_ref[PLACES[2 * tile], : 2 * NF] = even.astype(BF16)
            message_ref[PLACES[2 * tile + 1], : 2 * NF] = odd.astype(BF16)
    stations = jnp.where(row // 4 % 2 == 1, pltpu.roll(stations, 16, 1), stations)
    slabs = [stations[8 * h : 8 * h + 4] + stations[8 * h + 4 : 8 * h + 8] for h in range(2)]
    slab = jnp.concatenate(slabs, axis=0).astype(BF16)
    for g in range(message_ref.shape[0]):
        message_ref[g, 2 * NF :] = slab


def product_kernel(
    own_ref, other_ref, counts_ref, spread_ref, message_ref, station_ref, first_ref, second_ref, same_ref, cross_ref
):
    groups = own_ref.shape[0]
    upper = lax.broadcasted_iota(jnp.int32, (NF, LANES), 0) >= 4
    low = lax.broadcasted_iota(jnp.int32, (NF, LANES), 1) < LANES // 2
    for g in range(groups):
        place = PLACES[g]
        rounded = (own_ref[place].astype(F32) + other_ref[place].astype(F32)).astype(BF16).astype(F32)
        second_ref[:, g * LANES : (g + 1) * LANES] = rounded[: 2 * NF]
        stations = rounded[2 * NF :]
        for s in range(2):
            real = stations if s == 0 else pltpu.roll(stations, LANES - 8, 1)
            imag = pltpu.roll(stations, LANES - 16 - 8 * s, 1)
            legs = [jnp.where(upper, pltpu.roll(imag, 4, 0), real), jnp.where(upper, imag, pltpu.roll(real, 4, 0))]
            station_ref[32 * g + 16 * s : 32 * g + 16 * s + 16, :] = jnp.concatenate(legs, axis=0).astype(BF16)
    first_ref[...] = jnp.dot(station_ref[...], spread_ref[...], preferred_element_type=F32)

    tiles = second_ref.shape[1] // LANES
    span = 4
    for start in range(0, tiles, span):
        columns = [slice(t * LANES, (t + 1) * LANES) for t in range(start, start + span)]
        second = [[second_ref[NF * h : NF * (h + 1), c] for c in columns] for h in range(2)]
        crossed = [[jnp.concatenate([x[4:], x[:4]], axis=0) for x in half] for half in second]
        for s in range(2 * groups):
            counts = [counts_ref[s : s + 1, c] for c in columns]
            for h in range(2):
                rows = slice(16 * s + 8 * h, 16 * s + 8 * h + 8)
                first = [count * first_ref[rows, c] for count, c in zip(counts, columns)]
                same = sum(x * y for x, y in zip(first, second[h]))
                cross = sum(x * y for x, y in zip(first, crossed[h]))
                if start:
                    same, cross = same + same_ref[rows, :], cross + cross_ref[rows, :]
                same_ref[rows, :] = same
                cross_ref[rows, :] = cross
    for g in range(groups):
        message = []
        for h in range(2):
            spectra = []
            for s in (2 * g, 2 * g + 1):
                rows = slice(16 * s + 8 * h, 16 * s + 8 * h + 8)
                same, cross = same_ref[rows, :], cross_ref[rows, :]
                total = jnp.where(upper, cross + pltpu.roll(cross, 4, 0), same - pltpu.roll(same, 4, 0))
                spectra.append((total + pltpu.roll(total, LANES // 2, 1)) * KMAX ** (-0.5))
            message.append(jnp.where(low, spectra[0], spectra[1]))
        message_ref[PLACES[g]] = jnp.concatenate(message, axis=0).astype(BF16)


def synthesis_kernel(received_ref, filtered_ref, out_hbm, out_ref, out_sem):
    low = lax.broadcasted_iota(jnp.int32, (2 * NF, LANES), 1) < LANES // 2
    copies = []
    for tile in range(out_ref.shape[1] // LANES):
        left, right = [received_ref[PLACES[2 * tile + i]].astype(F32) for i in range(2)]
        spectra = (
            jnp.where(low, left, pltpu.roll(right, LANES // 2, 1)),
            jnp.where(low, pltpu.roll(left, LANES // 2, 1), right),
        )
        rows = pl.ds(tile * LANES, LANES)
        for s in range(2):
            out_ref[s, rows, :] = lax.dot_general(
                spectra[s].astype(BF16), filtered_ref[s], (((0,), (0,)), ((), ())), preferred_element_type=F32
            ).astype(BF16)
            copy = pltpu.make_async_copy(out_ref.at[s, rows, :], out_hbm.at[s, rows, :], out_sem.at[2 * tile + s])
            copy.start()
            copies.append(copy)
    for copy in copies:
        copy.wait()


def in_vmem():
    return pl.BlockSpec(memory_space=pltpu.VMEM)


def in_hbm():
    return pl.BlockSpec(memory_space=pltpu.HBM)


def exchange(messages, run):
    return lax.all_to_all(
        messages, DEVICES, split_axis=0, concat_axis=0, tiled=True, axis_index_groups=core_groups(run)
    )


def shards(traces, frequency_bins, aperture, lengths, filters):
    shot_dev, receivers, time_dev = traces.shape
    shots = aperture.shape[0]
    params = pltpu.CompilerParams(vmem_limit_bytes=VMEM_LIMIT)

    pairs = shots * aperture.shape[1]
    operands = (frequency_bins, traces)
    messages, spread, wide = pl.pallas_call(
        analysis_kernel,
        in_specs=[in_hbm()] * len(operands),
        out_specs=[in_vmem()] * 3,
        out_shape=[
            jax.ShapeDtypeStruct((CHIPS, 3 * NF, LANES), BF16),
            jax.ShapeDtypeStruct((LANES, pairs), BF16),
            jax.ShapeDtypeStruct((2 * NF, time_dev + LANES), BF16),
        ],
        scratch_shapes=[
            pltpu.SMEM((NF,), jnp.int32),
            *[pltpu.VMEM(x.shape, x.dtype) for x in operands[1:]],
            pltpu.VMEM((2 * NF, time_dev), BF16),
            pltpu.SemaphoreType.DMA((3,)),
        ],
        compiler_params=params,
        cost_estimate=pl.CostEstimate(flops=2 * 16 * traces.size, bytes_accessed=2 * traces.size, transcendentals=0),
    )(*[pltpu.with_memory_space_constraint(x, pltpu.HBM) for x in operands])
    own = exchange(messages, 4)
    other = lax.ppermute(own, "freq", [(0, 1), (1, 0)])
    counts, filtered = pl.pallas_call(
        tables_kernel,
        in_specs=[in_vmem()] * 4 + [pl.BlockSpec(memory_space=pl.ANY)],
        out_specs=[in_vmem()] * 2,
        out_shape=[
            jax.ShapeDtypeStruct((shots, pairs), F32),
            jax.ShapeDtypeStruct((shot_dev, 2 * NF, time_dev), BF16),
        ],
        scratch_shapes=[pltpu.VMEM((KMAX * shots // 2, LANES), jnp.int32)],
        compiler_params=params,
        cost_estimate=pl.CostEstimate(flops=1 << 22, bytes_accessed=1 << 19, transcendentals=0),
    )(wide, filters, lengths, aperture.transpose(0, 2, 1), own)

    messages = pl.pallas_call(
        product_kernel,
        in_specs=[in_vmem()] * 4,
        out_specs=in_vmem(),
        out_shape=jax.ShapeDtypeStruct((CHIPS, 2 * NF, LANES), BF16),
        scratch_shapes=[
            pltpu.VMEM((shots * 2 * NF, LANES), BF16),
            pltpu.VMEM((shots * 2 * NF, pairs), F32),
            pltpu.VMEM((2 * NF, pairs), F32),
            pltpu.VMEM((shots * 2 * NF, LANES), F32),
            pltpu.VMEM((shots * 2 * NF, LANES), F32),
        ],
        compiler_params=params,
        cost_estimate=pl.CostEstimate(flops=1 << 24, bytes_accessed=1 << 20, transcendentals=0),
    )(own, other, counts, spread)
    received = exchange(messages, 8)

    return pl.pallas_call(
        synthesis_kernel,
        in_specs=[in_vmem(), in_vmem()],
        out_specs=in_hbm(),
        out_shape=jax.ShapeDtypeStruct(traces.shape, BF16),
        scratch_shapes=[
            pltpu.VMEM(traces.shape, BF16),
            pltpu.SemaphoreType.DMA((shot_dev * receivers // LANES,)),
        ],
        compiler_params=params,
        cost_estimate=pl.CostEstimate(flops=2 * 16 * traces.size, bytes_accessed=2 * traces.size, transcendentals=0),
    )(received, filtered)


def general_shards(traces, frequency_bins, aperture, lengths, filters):
    shot_dev, receivers, time_dev = traces.shape
    shots = aperture.shape[0]
    receiver_dev = aperture.shape[1]
    start = lax.axis_index("freq") * time_dev

    def basis_rows(times):
        phases = frequency_bins[:, None] * times[None, :]
        return jnp.stack([cosine(phases & (NT - 1)), cosine((phases + NT // 4) & (NT - 1))], axis=1)

    times = start + jnp.arange(time_dev, dtype=jnp.int32)
    analysis = (basis_rows(times) * NT ** (-0.5)).astype(BF16).reshape(2 * NF, time_dev)
    term = lax.dot_general(
        analysis, traces.reshape(shot_dev * receivers, time_dev), (((1,), (1,)), ((), ())), preferred_element_type=F32
    )
    spectra = lax.psum_scatter(
        term.reshape(NF, 2, shot_dev, receivers), "freq", scatter_dimension=0, tiled=True
    ).astype(BF16)
    second = lax.all_to_all(spectra, "shot", split_axis=3, concat_axis=2, tiled=True).astype(F32)
    stations = spectra[:, :, :, :: receivers // shots]
    first = lax.all_gather(stations, "shot", axis=2, tiled=True).astype(F32)

    def one_shot(inputs):
        legs, lists, list_lengths = inputs
        used = jnp.arange(KMAX, dtype=jnp.int32)[None, :] < list_lengths[:, None]
        lists = jnp.where(used, lists, -1)
        hits = lists[None] == jnp.arange(shots, dtype=jnp.int32)[:, None, None]
        counts = hits.astype(F32).sum(axis=-1)
        legs = legs[..., None]
        real = legs[:, 0] * second[:, 0] - legs[:, 1] * second[:, 1]
        imag = legs[:, 0] * second[:, 1] + legs[:, 1] * second[:, 0]
        return (jnp.stack([real, imag], axis=1) * counts).sum(axis=2)

    summed = lax.map(one_shot, (first.transpose(2, 0, 1, 3), aperture, lengths))
    summed = (summed * KMAX ** (-0.5)).astype(BF16).transpose(1, 2, 0, 3)
    summed = lax.all_to_all(summed, "shot", split_axis=2, concat_axis=3, tiled=True)
    summed = lax.all_gather(summed, "freq", axis=0, tiled=True).reshape(2 * NF, shot_dev, receivers)

    wide = start - HALF + jnp.arange(time_dev + 2 * HALF, dtype=jnp.int32)
    synthesis = basis_rows(wide).astype(BF16).astype(F32).reshape(2 * NF, time_dev + 2 * HALF)
    synthesis = jnp.where((wide >= 0) & (wide < NT), synthesis, 0.0)
    filtered = jnp.zeros((shot_dev, 2 * NF, time_dev), F32)
    for j in range(TAPS):
        tap = filters[:, j].astype(F32)[:, None, None]
        filtered = filtered + tap * synthesis[:, 2 * HALF - j : 2 * HALF - j + time_dev]
    out = jnp.einsum("fsr,sft->srt", summed, filtered.astype(BF16), preferred_element_type=F32)
    return out.astype(BF16)


def solution(mesh):
    in_specs = (
        P("shot", None, "freq"),
        P(),
        P(None, "shot", None),
        P(None, "shot"),
        P("shot", None),
    )
    out_specs = P("shot", None, "freq")
    whole_pieces = mesh.shape["shot"] == 16 and mesh.shape["freq"] == 2
    body = shards if whole_pieces else general_shards
    return jax.shard_map(body, mesh=mesh, in_specs=in_specs, out_specs=out_specs, check_vma=False)
```

```python
import math

import jax
import jax.numpy as jnp
from jax import lax
from jax.experimental import pallas as pl
from jax.experimental.pallas import tpu as pltpu
from jax.sharding import PartitionSpec as P

NT = 1024
NF = 8
KMAX = 32
TAPS = 31
HALF = (TAPS - 1) // 2
LANES = 128
PIECE = 32
DEVICES = ("shot", "freq")
CHIPS = 16


def hops(a, b):
    return abs(a // 4 - b // 4) + (a // 2 % 2 != b // 2 % 2) + (a % 2 != b % 2)


ORDER = sorted(range(CHIPS), key=lambda g: hops(11, g))
PLACES = [ORDER.index(g) for g in range(CHIPS)]


def core_groups(run):
    return [[2 * g + (core + g // run) % 2 for g in ORDER] for core in range(2)]


F32 = jnp.float32
BF16 = jnp.bfloat16
VMEM_LIMIT = 48 * 1024 * 1024


def cosine(phases):
    quarter = NT // 4
    turn = (phases + quarter // 2) // quarter
    angle = (phases - turn * quarter).astype(F32) * (2.0 * math.pi / NT)
    square = angle * angle
    sine = angle * (1.0 + square * (-1 / 6 + square * (1 / 120 + square * (-1 / 5040 + square / 362880))))
    cosine = 1.0 + square * (-1 / 2 + square * (1 / 24 + square * (-1 / 720 + square / 40320)))
    near = jnp.where(turn % 2 == 1, sine, cosine)
    return jnp.where((turn == 1) | (turn == 2), -near, near)


def basis_in_kernel(bins_ref, first_time, width):
    rows = lax.broadcasted_iota(jnp.int32, (2 * NF, width), 0)
    times = lax.broadcasted_iota(jnp.int32, (2 * NF, width), 1) + first_time
    frequency = rows // NF * (NF // 2) + rows % (NF // 2)
    part = rows // (NF // 2) % 2
    bins = jnp.zeros((2 * NF, width), jnp.int32)
    for f in range(NF):
        bins = jnp.where(frequency == f, bins_ref[f], bins)
    return cosine((bins * times + part * (NT // 4)) & (NT - 1)), times


def write_spread(spread_ref):
    lane = lax.broadcasted_iota(jnp.int32, (LANES, LANES), 0)
    station = lane % PIECE * 4 + lane // PIECE - lax.broadcasted_iota(jnp.int32, (LANES, LANES), 1) // (LANES // 2)
    for tile in range(spread_ref.shape[1] // LANES):
        here = jnp.where(station == 2 * tile, 1.0, 0.0)
        spread_ref[:, tile * LANES : (tile + 1) * LANES] = here.astype(BF16)


def write_filtered(wide_ref, filters_ref, filtered_ref):
    shot_dev, _, time_dev = filtered_ref.shape
    basis = wide_ref[...].astype(F32)
    width = basis.shape[1]
    taps = filters_ref[...].astype(F32)
    total = [jnp.zeros((2 * NF, time_dev), F32) for _ in range(shot_dev)]
    for j in range(TAPS):
        shift = 2 * HALF - j
        moved = basis if shift == 0 else pltpu.roll(basis, width - shift, 1)
        moved = moved[:, :time_dev]
        for s in range(shot_dev):
            total[s] = total[s] + taps[s : s + 1, j : j + 1] * moved
    for s in range(shot_dev):
        filtered_ref[s] = total[s].astype(BF16)


def bit_sums(words):
    waiting, planes = [], []
    for word in words:
        level = 0
        while True:
            if level == len(waiting):
                waiting.append([])
            waiting[level].append(word)
            if len(waiting[level]) < 3:
                break
            x, y, z = waiting[level]
            either = x ^ y
            waiting[level] = [either ^ z]
            word = (x & y) | (either & z)
            level += 1
    level = 0
    while level < len(waiting):
        held = waiting[level]
        if len(held) > 1:
            if level + 1 == len(waiting):
                waiting.append([])
            x, y = held[0], held[1]
            carries = [x & y]
            if len(held) == 3:
                carries = [(x & y) | ((x ^ y) & held[2])]
            waiting[level + 1] += carries
            held = [x ^ y] if len(held) == 2 else [x ^ y ^ held[2]]
        planes.append(held[0])
        level += 1
    return planes


def write_counts(aperture_ref, lengths_ref, codes_ref, counts_ref):
    half = aperture_ref.shape[0] // 2
    for s in range(half):
        both = jnp.concatenate([aperture_ref[s], aperture_ref[s + half]], axis=1)
        codes_ref[pl.ds(s, KMAX, stride=half), :] = both
    lengths = jnp.concatenate([lengths_ref[:half, :], lengths_ref[half:, :]], axis=1)
    one = jnp.ones((half, LANES), jnp.int32)

    def words():
        for k in range(KMAX):
            codes = codes_ref[k * half : (k + 1) * half, :]
            yield jnp.where(lengths > k, lax.shift_left(one, codes), 0)

    planes = bit_sums(words())
    low = lax.broadcasted_iota(jnp.int32, (half, LANES), 1) < LANES // 2
    for i in range(0, 8, 2):
        packed = []
        for bit in (i, i + 1):
            total = 0
            for level, plane in enumerate(planes):
                spread = lax.shift_right_logical(plane, jnp.full_like(plane, bit)) & 0x01010101
                total = total + (spread << level)
            packed.append(total)
        for byte in range(4):
            left, right = [(lax.shift_right_logical(x, jnp.full_like(x, 8 * byte)) & 255).astype(F32) for x in packed]
            lanes = pl.ds((8 * byte + i) * (LANES // 2), LANES)
            counts_ref[:half, lanes] = jnp.where(low, left, pltpu.roll(right, LANES // 2, 1))
            counts_ref[half:, lanes] = jnp.where(low, pltpu.roll(left, LANES // 2, 1), right)


def tables_kernel(
    wide_ref, filters_ref, lengths_ref, aperture_ref, _, counts_ref, filtered_ref, codes_ref
):
    write_counts(aperture_ref, lengths_ref, codes_ref, counts_ref)
    write_filtered(wide_ref, filters_ref, filtered_ref)


def analysis_kernel(
    bins_hbm, traces_hbm, message_ref, spread_ref, wide_ref, bins_ref, traces_ref, basis_ref, sems,
):
    shot_dev, receivers, time_dev = traces_ref.shape
    bins_copy = pltpu.make_async_copy(bins_hbm, bins_ref, sems.at[0])
    starts = [0, 3 * LANES, receivers]
    blocks = list(zip(starts, starts[1:]))
    copies = []
    for i, (start, end) in enumerate(blocks):
        rows = pl.ds(start, end - start)
        copies.append(pltpu.make_async_copy(traces_hbm.at[:, rows, :], traces_ref.at[:, rows, :], sems.at[1 + i]))
    for copy in [bins_copy] + copies:
        copy.start()

    write_spread(spread_ref)
    bins_copy.wait()
    wide, times = basis_in_kernel(bins_ref, lax.axis_index("freq") * time_dev - HALF, wide_ref.shape[1])
    wide_ref[...] = jnp.where((times >= 0) & (times < NT), wide, 0.0).astype(BF16)
    basis = pltpu.roll(wide, wide.shape[1] - HALF, 1)[:, :time_dev]
    basis_ref[...] = (basis * NT ** (-0.5)).astype(BF16)

    lane = lax.broadcasted_iota(jnp.int32, (2 * NF, LANES), 1)
    row = lax.broadcasted_iota(jnp.int32, (2 * NF, LANES), 0)
    low = lane < LANES // 2
    is_station = lane % PIECE == 0
    stations = jnp.zeros((2 * NF, LANES), F32)
    for copy, (start, end) in zip(copies, blocks):
        copy.wait()
        terms = [
            lax.dot_general(
                basis_ref[...],
                traces_ref[s, start:end, :],
                (((1,), (1,)), ((), ())),
                preferred_element_type=F32,
            )
            for s in range(shot_dev)
        ]
        for j in range((end - start) // LANES):
            tile = start // LANES + j
            first, second = [x[:, j * LANES : (j + 1) * LANES] for x in terms]
            for s, x in enumerate((first, second)):
                marked = jnp.where(is_station, x, 0.0)
                shift = 8 * s + tile
                stations = stations + (pltpu.roll(marked, shift, 1) if shift else marked)
            even = jnp.where(low, first, pltpu.roll(second, LANES // 2, 1))
            odd = jnp.where(low, pltpu.roll(first, LANES // 2, 1), second)
            message_ref[PLACES[2 * tile], : 2 * NF] = even.astype(BF16)
            message_ref[PLACES[2 * tile + 1], : 2 * NF] = odd.astype(BF16)
    stations = jnp.where(row // 4 % 2 == 1, pltpu.roll(stations, 16, 1), stations)
    slabs = [stations[8 * h : 8 * h + 4] + stations[8 * h + 4 : 8 * h + 8] for h in range(2)]
    slab = jnp.concatenate(slabs, axis=0).astype(BF16)
    for g in range(message_ref.shape[0]):
        message_ref[g, 2 * NF :] = slab


def product_kernel(
    own_ref, other_ref, counts_ref, spread_ref, message_ref, station_ref, first_ref, second_ref, same_ref, cross_ref
):
    groups = own_ref.shape[0]
    upper = lax.broadcasted_iota(jnp.int32, (NF, LANES), 0) >= 4
    low = lax.broadcasted_iota(jnp.int32, (NF, LANES), 1) < LANES // 2
    for g in range(groups):
        place = PLACES[g]
        rounded = (own_ref[place].astype(F32) + other_ref[place].astype(F32)).astype(BF16).astype(F32)
        second_ref[:, g * LANES : (g + 1) * LANES] = rounded[: 2 * NF]
        stations = rounded[2 * NF :]
        for s in range(2):
            real = stations if s == 0 else pltpu.roll(stations, LANES - 8, 1)
            imag = pltpu.roll(stations, LANES - 16 - 8 * s, 1)
            legs = [jnp.where(upper, pltpu.roll(imag, 4, 0), real), jnp.where(upper, imag, pltpu.roll(real, 4, 0))]
            station_ref[32 * g + 16 * s : 32 * g + 16 * s + 16, :] = jnp.concatenate(legs, axis=0).astype(BF16)
    first_ref[...] = jnp.dot(station_ref[...], spread_ref[...], preferred_element_type=F32)

    tiles = second_ref.shape[1] // LANES
    span = 4
    for start in range(0, tiles, span):
        columns = [slice(t * LANES, (t + 1) * LANES) for t in range(start, start + span)]
        second = [[second_ref[NF * h : NF * (h + 1), c] for c in columns] for h in range(2)]
        crossed = [[jnp.concatenate([x[4:], x[:4]], axis=0) for x in half] for half in second]
        for s in range(2 * groups):
            counts = [counts_ref[s : s + 1, c] for c in columns]
            for h in range(2):
                rows = slice(16 * s + 8 * h, 16 * s + 8 * h + 8)
                first = [count * first_ref[rows, c] for count, c in zip(counts, columns)]
                same = sum(x * y for x, y in zip(first, second[h]))
                cross = sum(x * y for x, y in zip(first, crossed[h]))
                if start:
                    same, cross = same + same_ref[rows, :], cross + cross_ref[rows, :]
                same_ref[rows, :] = same
                cross_ref[rows, :] = cross
    for g in range(groups):
        message = []
        for h in range(2):
            spectra = []
            for s in (2 * g, 2 * g + 1):
                rows = slice(16 * s + 8 * h, 16 * s + 8 * h + 8)
                same, cross = same_ref[rows, :], cross_ref[rows, :]
                total = jnp.where(upper, cross + pltpu.roll(cross, 4, 0), same - pltpu.roll(same, 4, 0))
                spectra.append((total + pltpu.roll(total, LANES // 2, 1)) * KMAX ** (-0.5))
            message.append(jnp.where(low, spectra[0], spectra[1]))
        message_ref[PLACES[g]] = jnp.concatenate(message, axis=0).astype(BF16)


def synthesis_kernel(received_ref, filtered_ref, out_hbm, out_ref, out_sem):
    low = lax.broadcasted_iota(jnp.int32, (2 * NF, LANES), 1) < LANES // 2
    copies = []
    for tile in range(out_ref.shape[1] // LANES):
        left, right = [received_ref[PLACES[2 * tile + i]] for i in range(2)]
        spectra = (
            jnp.where(low, left, pltpu.roll(right, LANES // 2, 1)),
            jnp.where(low, pltpu.roll(left, LANES // 2, 1), right),
        )
        rows = pl.ds(tile * LANES, LANES)
        for s in range(2):
            out_ref[s, rows, :] = lax.dot_general(
                spectra[s], filtered_ref[s], (((0,), (0,)), ((), ())), preferred_element_type=F32
            ).astype(BF16)
            copy = pltpu.make_async_copy(out_ref.at[s, rows, :], out_hbm.at[s, rows, :], out_sem.at[2 * tile + s])
            copy.start()
            copies.append(copy)
    for copy in copies:
        copy.wait()


def in_vmem():
    return pl.BlockSpec(memory_space=pltpu.VMEM)


def in_hbm():
    return pl.BlockSpec(memory_space=pltpu.HBM)


def exchange(messages, run):
    return lax.all_to_all(
        messages, DEVICES, split_axis=0, concat_axis=0, tiled=True, axis_index_groups=core_groups(run)
    )


def shards(traces, frequency_bins, aperture, lengths, filters):
    shot_dev, receivers, time_dev = traces.shape
    shots = aperture.shape[0]
    params = pltpu.CompilerParams(vmem_limit_bytes=VMEM_LIMIT)

    pairs = shots * aperture.shape[1]
    operands = (frequency_bins, traces)
    messages, spread, wide = pl.pallas_call(
        analysis_kernel,
        in_specs=[in_hbm()] * len(operands),
        out_specs=[in_vmem()] * 3,
        out_shape=[
            jax.ShapeDtypeStruct((CHIPS, 3 * NF, LANES), BF16),
            jax.ShapeDtypeStruct((LANES, pairs), BF16),
            jax.ShapeDtypeStruct((2 * NF, time_dev + LANES), BF16),
        ],
        scratch_shapes=[
            pltpu.SMEM((NF,), jnp.int32),
            *[pltpu.VMEM(x.shape, x.dtype) for x in operands[1:]],
            pltpu.VMEM((2 * NF, time_dev), BF16),
            pltpu.SemaphoreType.DMA((3,)),
        ],
        compiler_params=params,
        cost_estimate=pl.CostEstimate(flops=2 * 16 * traces.size, bytes_accessed=2 * traces.size, transcendentals=0),
    )(*[pltpu.with_memory_space_constraint(x, pltpu.HBM) for x in operands])
    own = exchange(messages, 4)
    other = lax.ppermute(own, "freq", [(0, 1), (1, 0)])
    counts, filtered = pl.pallas_call(
        tables_kernel,
        in_specs=[in_vmem()] * 4 + [pl.BlockSpec(memory_space=pl.ANY)],
        out_specs=[in_vmem()] * 2,
        out_shape=[
            jax.ShapeDtypeStruct((shots, pairs), F32),
            jax.ShapeDtypeStruct((shot_dev, 2 * NF, time_dev), BF16),
        ],
        scratch_shapes=[pltpu.VMEM((KMAX * shots // 2, LANES), jnp.int32)],
        compiler_params=params,
        cost_estimate=pl.CostEstimate(flops=1 << 22, bytes_accessed=1 << 19, transcendentals=0),
    )(wide, filters, lengths, aperture.transpose(0, 2, 1), own)

    messages = pl.pallas_call(
        product_kernel,
        in_specs=[in_vmem()] * 4,
        out_specs=in_vmem(),
        out_shape=jax.ShapeDtypeStruct((CHIPS, 2 * NF, LANES), BF16),
        scratch_shapes=[
            pltpu.VMEM((shots * 2 * NF, LANES), BF16),
            pltpu.VMEM((shots * 2 * NF, pairs), F32),
            pltpu.VMEM((2 * NF, pairs), F32),
            pltpu.VMEM((shots * 2 * NF, LANES), F32),
            pltpu.VMEM((shots * 2 * NF, LANES), F32),
        ],
        compiler_params=params,
        cost_estimate=pl.CostEstimate(flops=1 << 24, bytes_accessed=1 << 20, transcendentals=0),
    )(own, other, counts, spread)
    received = exchange(messages, 8)

    return pl.pallas_call(
        synthesis_kernel,
        in_specs=[in_vmem(), in_vmem()],
        out_specs=in_hbm(),
        out_shape=jax.ShapeDtypeStruct(traces.shape, BF16),
        scratch_shapes=[
            pltpu.VMEM(traces.shape, BF16),
            pltpu.SemaphoreType.DMA((shot_dev * receivers // LANES,)),
        ],
        compiler_params=params,
        cost_estimate=pl.CostEstimate(flops=2 * 16 * traces.size, bytes_accessed=2 * traces.size, transcendentals=0),
    )(received, filtered)


def general_shards(traces, frequency_bins, aperture, lengths, filters):
    shot_dev, receivers, time_dev = traces.shape
    shots = aperture.shape[0]
    receiver_dev = aperture.shape[1]
    start = lax.axis_index("freq") * time_dev

    def basis_rows(times):
        phases = frequency_bins[:, None] * times[None, :]
        return jnp.stack([cosine(phases & (NT - 1)), cosine((phases + NT // 4) & (NT - 1))], axis=1)

    times = start + jnp.arange(time_dev, dtype=jnp.int32)
    analysis = (basis_rows(times) * NT ** (-0.5)).astype(BF16).reshape(2 * NF, time_dev)
    term = lax.dot_general(
        analysis, traces.reshape(shot_dev * receivers, time_dev), (((1,), (1,)), ((), ())), preferred_element_type=F32
    )
    spectra = lax.psum_scatter(
        term.reshape(NF, 2, shot_dev, receivers), "freq", scatter_dimension=0, tiled=True
    ).astype(BF16)
    second = lax.all_to_all(spectra, "shot", split_axis=3, concat_axis=2, tiled=True).astype(F32)
    stations = spectra[:, :, :, :: receivers // shots]
    first = lax.all_gather(stations, "shot", axis=2, tiled=True).astype(F32)

    def one_shot(inputs):
        legs, lists, list_lengths = inputs
        used = jnp.arange(KMAX, dtype=jnp.int32)[None, :] < list_lengths[:, None]
        lists = jnp.where(used, lists, -1)
        hits = lists[None] == jnp.arange(shots, dtype=jnp.int32)[:, None, None]
        counts = hits.astype(F32).sum(axis=-1)
        legs = legs[..., None]
        real = legs[:, 0] * second[:, 0] - legs[:, 1] * second[:, 1]
        imag = legs[:, 0] * second[:, 1] + legs[:, 1] * second[:, 0]
        return (jnp.stack([real, imag], axis=1) * counts).sum(axis=2)

    summed = lax.map(one_shot, (first.transpose(2, 0, 1, 3), aperture, lengths))
    summed = (summed * KMAX ** (-0.5)).astype(BF16).transpose(1, 2, 0, 3)
    summed = lax.all_to_all(summed, "shot", split_axis=2, concat_axis=3, tiled=True)
    summed = lax.all_gather(summed, "freq", axis=0, tiled=True).reshape(2 * NF, shot_dev, receivers)

    wide = start - HALF + jnp.arange(time_dev + 2 * HALF, dtype=jnp.int32)
    synthesis = basis_rows(wide).astype(BF16).astype(F32).reshape(2 * NF, time_dev + 2 * HALF)
    synthesis = jnp.where((wide >= 0) & (wide < NT), synthesis, 0.0)
    filtered = jnp.zeros((shot_dev, 2 * NF, time_dev), F32)
    for j in range(TAPS):
        tap = filters[:, j].astype(F32)[:, None, None]
        filtered = filtered + tap * synthesis[:, 2 * HALF - j : 2 * HALF - j + time_dev]
    out = jnp.einsum("fsr,sft->srt", summed, filtered.astype(BF16), preferred_element_type=F32)
    return out.astype(BF16)


def solution(mesh):
    in_specs = (
        P("shot", None, "freq"),
        P(),
        P(None, "shot", None),
        P(None, "shot"),
        P("shot", None),
    )
    out_specs = P("shot", None, "freq")
    whole_pieces = mesh.shape["shot"] == 16 and mesh.shape["freq"] == 2
    body = shards if whole_pieces else general_shards
    return jax.shard_map(body, mesh=mesh, in_specs=in_specs, out_specs=out_specs, check_vma=False)
```

```python
import math

import jax
import jax.numpy as jnp
from jax import lax
from jax.experimental import pallas as pl
from jax.experimental.pallas import tpu as pltpu
from jax.sharding import PartitionSpec as P

NT = 1024
NF = 8
KMAX = 32
TAPS = 31
HALF = (TAPS - 1) // 2
LANES = 128
PIECE = 32
DEVICES = ("shot", "freq")
CHIPS = 16


def hops(a, b):
    return abs(a // 4 - b // 4) + (a // 2 % 2 != b // 2 % 2) + (a % 2 != b % 2)


ORDER = sorted(range(CHIPS), key=lambda g: (hops(11, g), -hops(CHIPS - 1, g)))
PLACES = [ORDER.index(g) for g in range(CHIPS)]


def core_groups(run):
    return [[2 * g + (core + g // run) % 2 for g in ORDER] for core in range(2)]


F32 = jnp.float32
BF16 = jnp.bfloat16
VMEM_LIMIT = 48 * 1024 * 1024


def cosine(phases):
    quarter = NT // 4
    turn = (phases + quarter // 2) // quarter
    angle = (phases - turn * quarter).astype(F32) * (2.0 * math.pi / NT)
    square = angle * angle
    sine = angle * (1.0 + square * (-1 / 6 + square * (1 / 120 + square * (-1 / 5040 + square / 362880))))
    cosine = 1.0 + square * (-1 / 2 + square * (1 / 24 + square * (-1 / 720 + square / 40320)))
    near = jnp.where(turn % 2 == 1, sine, cosine)
    return jnp.where((turn == 1) | (turn == 2), -near, near)


def basis_in_kernel(bins_ref, first_time, width):
    rows = lax.broadcasted_iota(jnp.int32, (2 * NF, width), 0)
    times = lax.broadcasted_iota(jnp.int32, (2 * NF, width), 1) + first_time
    frequency = rows // NF * (NF // 2) + rows % (NF // 2)
    part = rows // (NF // 2) % 2
    bins = jnp.zeros((2 * NF, width), jnp.int32)
    for f in range(NF):
        bins = jnp.where(frequency == f, bins_ref[f], bins)
    return cosine((bins * times + part * (NT // 4)) & (NT - 1)), times


def write_spread(spread_ref):
    lane = lax.broadcasted_iota(jnp.int32, (LANES, LANES), 0)
    station = lane % PIECE * 4 + lane // PIECE - lax.broadcasted_iota(jnp.int32, (LANES, LANES), 1) // (LANES // 2)
    for tile in range(spread_ref.shape[1] // LANES):
        here = jnp.where(station == 2 * tile, 1.0, 0.0)
        spread_ref[:, tile * LANES : (tile + 1) * LANES] = here.astype(BF16)


def write_filtered(wide_ref, filters_ref, filtered_ref):
    shot_dev, _, time_dev = filtered_ref.shape
    basis = wide_ref[...].astype(F32)
    width = basis.shape[1]
    taps = filters_ref[...].astype(F32)
    total = [jnp.zeros((2 * NF, time_dev), F32) for _ in range(shot_dev)]
    for j in range(TAPS):
        shift = 2 * HALF - j
        moved = basis if shift == 0 else pltpu.roll(basis, width - shift, 1)
        moved = moved[:, :time_dev]
        for s in range(shot_dev):
            total[s] = total[s] + taps[s : s + 1, j : j + 1] * moved
    for s in range(shot_dev):
        filtered_ref[s] = total[s].astype(BF16)


def bit_sums(words):
    waiting, planes = [], []
    for word in words:
        level = 0
        while True:
            if level == len(waiting):
                waiting.append([])
            waiting[level].append(word)
            if len(waiting[level]) < 3:
                break
            x, y, z = waiting[level]
            either = x ^ y
            waiting[level] = [either ^ z]
            word = (x & y) | (either & z)
            level += 1
    level = 0
    while level < len(waiting):
        held = waiting[level]
        if len(held) > 1:
            if level + 1 == len(waiting):
                waiting.append([])
            x, y = held[0], held[1]
            carries = [x & y]
            if len(held) == 3:
                carries = [(x & y) | ((x ^ y) & held[2])]
            waiting[level + 1] += carries
            held = [x ^ y] if len(held) == 2 else [x ^ y ^ held[2]]
        planes.append(held[0])
        level += 1
    return planes


def write_counts(aperture_ref, lengths_ref, codes_ref, counts_ref):
    half = aperture_ref.shape[0] // 2
    for s in range(half):
        both = jnp.concatenate([aperture_ref[s], aperture_ref[s + half]], axis=1)
        codes_ref[pl.ds(s, KMAX, stride=half), :] = both
    lengths = jnp.concatenate([lengths_ref[:half, :], lengths_ref[half:, :]], axis=1)
    one = jnp.ones((half, LANES), jnp.int32)

    def words():
        for k in range(KMAX):
            codes = codes_ref[k * half : (k + 1) * half, :]
            yield jnp.where(lengths > k, lax.shift_left(one, codes), 0)

    planes = bit_sums(words())
    low = lax.broadcasted_iota(jnp.int32, (half, LANES), 1) < LANES // 2
    for i in range(0, 8, 2):
        packed = []
        for bit in (i, i + 1):
            total = 0
            for level, plane in enumerate(planes):
                spread = lax.shift_right_logical(plane, jnp.full_like(plane, bit)) & 0x01010101
                total = total + (spread << level)
            packed.append(total)
        for byte in range(4):
            left, right = [(lax.shift_right_logical(x, jnp.full_like(x, 8 * byte)) & 255).astype(F32) for x in packed]
            lanes = pl.ds((8 * byte + i) * (LANES // 2), LANES)
            counts_ref[:half, lanes] = jnp.where(low, left, pltpu.roll(right, LANES // 2, 1))
            counts_ref[half:, lanes] = jnp.where(low, pltpu.roll(left, LANES // 2, 1), right)


def tables_kernel(
    wide_ref, filters_ref, lengths_ref, aperture_ref, _, counts_ref, filtered_ref, codes_ref
):
    write_counts(aperture_ref, lengths_ref, codes_ref, counts_ref)
    write_filtered(wide_ref, filters_ref, filtered_ref)


def analysis_kernel(
    bins_hbm, traces_hbm, message_ref, spread_ref, wide_ref, bins_ref, traces_ref, basis_ref, sems,
):
    shot_dev, receivers, time_dev = traces_ref.shape
    bins_copy = pltpu.make_async_copy(bins_hbm, bins_ref, sems.at[0])
    starts = [0, 3 * LANES, receivers]
    blocks = list(zip(starts, starts[1:]))
    copies = []
    for i, (start, end) in enumerate(blocks):
        rows = pl.ds(start, end - start)
        copies.append(pltpu.make_async_copy(traces_hbm.at[:, rows, :], traces_ref.at[:, rows, :], sems.at[1 + i]))
    for copy in [bins_copy] + copies:
        copy.start()

    write_spread(spread_ref)
    bins_copy.wait()
    wide, times = basis_in_kernel(bins_ref, lax.axis_index("freq") * time_dev - HALF, wide_ref.shape[1])
    wide_ref[...] = jnp.where((times >= 0) & (times < NT), wide, 0.0).astype(BF16)
    basis = pltpu.roll(wide, wide.shape[1] - HALF, 1)[:, :time_dev]
    basis_ref[...] = (basis * NT ** (-0.5)).astype(BF16)

    lane = lax.broadcasted_iota(jnp.int32, (2 * NF, LANES), 1)
    row = lax.broadcasted_iota(jnp.int32, (2 * NF, LANES), 0)
    low = lane < LANES // 2
    is_station = lane % PIECE == 0
    stations = jnp.zeros((2 * NF, LANES), F32)
    for copy, (start, end) in zip(copies, blocks):
        copy.wait()
        terms = [
            lax.dot_general(
                basis_ref[...],
                traces_ref[s, start:end, :],
                (((1,), (1,)), ((), ())),
                preferred_element_type=F32,
            )
            for s in range(shot_dev)
        ]
        for j in range((end - start) // LANES):
            tile = start // LANES + j
            first, second = [x[:, j * LANES : (j + 1) * LANES] for x in terms]
            for s, x in enumerate((first, second)):
                marked = jnp.where(is_station, x, 0.0)
                shift = 8 * s + tile
                stations = stations + (pltpu.roll(marked, shift, 1) if shift else marked)
            even = jnp.where(low, first, pltpu.roll(second, LANES // 2, 1))
            odd = jnp.where(low, pltpu.roll(first, LANES // 2, 1), second)
            message_ref[PLACES[2 * tile], : 2 * NF] = even.astype(BF16)
            message_ref[PLACES[2 * tile + 1], : 2 * NF] = odd.astype(BF16)
    stations = jnp.where(row // 4 % 2 == 1, pltpu.roll(stations, 16, 1), stations)
    slabs = [stations[8 * h : 8 * h + 4] + stations[8 * h + 4 : 8 * h + 8] for h in range(2)]
    slab = jnp.concatenate(slabs, axis=0).astype(BF16)
    for g in range(message_ref.shape[0]):
        message_ref[g, 2 * NF :] = slab


def product_kernel(
    own_ref, other_ref, counts_ref, spread_ref, message_ref, station_ref, first_ref, second_ref, same_ref, cross_ref
):
    groups = own_ref.shape[0]
    upper = lax.broadcasted_iota(jnp.int32, (NF, LANES), 0) >= 4
    low = lax.broadcasted_iota(jnp.int32, (NF, LANES), 1) < LANES // 2
    for g in range(groups):
        place = PLACES[g]
        rounded = (own_ref[place].astype(F32) + other_ref[place].astype(F32)).astype(BF16).astype(F32)
        second_ref[:, g * LANES : (g + 1) * LANES] = rounded[: 2 * NF]
        stations = rounded[2 * NF :]
        for s in range(2):
            real = stations if s == 0 else pltpu.roll(stations, LANES - 8, 1)
            imag = pltpu.roll(stations, LANES - 16 - 8 * s, 1)
            legs = [jnp.where(upper, pltpu.roll(imag, 4, 0), real), jnp.where(upper, imag, pltpu.roll(real, 4, 0))]
            station_ref[32 * g + 16 * s : 32 * g + 16 * s + 16, :] = jnp.concatenate(legs, axis=0).astype(BF16)
    first_ref[...] = jnp.dot(station_ref[...], spread_ref[...], preferred_element_type=F32)

    tiles = second_ref.shape[1] // LANES
    span = 4
    for start in range(0, tiles, span):
        columns = [slice(t * LANES, (t + 1) * LANES) for t in range(start, start + span)]
        second = [[second_ref[NF * h : NF * (h + 1), c] for c in columns] for h in range(2)]
        crossed = [[jnp.concatenate([x[4:], x[:4]], axis=0) for x in half] for half in second]
        for s in range(2 * groups):
            counts = [counts_ref[s : s + 1, c] for c in columns]
            for h in range(2):
                rows = slice(16 * s + 8 * h, 16 * s + 8 * h + 8)
                first = [count * first_ref[rows, c] for count, c in zip(counts, columns)]
                same = sum(x * y for x, y in zip(first, second[h]))
                cross = sum(x * y for x, y in zip(first, crossed[h]))
                if start:
                    same, cross = same + same_ref[rows, :], cross + cross_ref[rows, :]
                same_ref[rows, :] = same
                cross_ref[rows, :] = cross
    for g in range(groups):
        message = []
        for h in range(2):
            spectra = []
            for s in (2 * g, 2 * g + 1):
                rows = slice(16 * s + 8 * h, 16 * s + 8 * h + 8)
                same, cross = same_ref[rows, :], cross_ref[rows, :]
                total = jnp.where(upper, cross + pltpu.roll(cross, 4, 0), same - pltpu.roll(same, 4, 0))
                spectra.append((total + pltpu.roll(total, LANES // 2, 1)) * KMAX ** (-0.5))
            message.append(jnp.where(low, spectra[0], spectra[1]))
        message_ref[PLACES[g]] = jnp.concatenate(message, axis=0).astype(BF16)


def synthesis_kernel(received_ref, filtered_ref, out_hbm, out_ref, out_sem):
    low = lax.broadcasted_iota(jnp.int32, (2 * NF, LANES), 1) < LANES // 2
    copies = []
    for tile in range(out_ref.shape[1] // LANES):
        left, right = [received_ref[PLACES[2 * tile + i]] for i in range(2)]
        spectra = (
            jnp.where(low, left, pltpu.roll(right, LANES // 2, 1)),
            jnp.where(low, pltpu.roll(left, LANES // 2, 1), right),
        )
        rows = pl.ds(tile * LANES, LANES)
        for s in range(2):
            out_ref[s, rows, :] = lax.dot_general(
                spectra[s], filtered_ref[s], (((0,), (0,)), ((), ())), preferred_element_type=F32
            ).astype(BF16)
            copy = pltpu.make_async_copy(out_ref.at[s, rows, :], out_hbm.at[s, rows, :], out_sem.at[2 * tile + s])
            copy.start()
            copies.append(copy)
    for copy in copies:
        copy.wait()


def in_vmem():
    return pl.BlockSpec(memory_space=pltpu.VMEM)


def in_hbm():
    return pl.BlockSpec(memory_space=pltpu.HBM)


def exchange(messages, run):
    return lax.all_to_all(
        messages, DEVICES, split_axis=0, concat_axis=0, tiled=True, axis_index_groups=core_groups(run)
    )


def shards(traces, frequency_bins, aperture, lengths, filters):
    shot_dev, receivers, time_dev = traces.shape
    shots = aperture.shape[0]
    params = pltpu.CompilerParams(vmem_limit_bytes=VMEM_LIMIT)

    pairs = shots * aperture.shape[1]
    operands = (frequency_bins, traces)
    messages, spread, wide = pl.pallas_call(
        analysis_kernel,
        in_specs=[in_hbm()] * len(operands),
        out_specs=[in_vmem()] * 3,
        out_shape=[
            jax.ShapeDtypeStruct((CHIPS, 3 * NF, LANES), BF16),
            jax.ShapeDtypeStruct((LANES, pairs), BF16),
            jax.ShapeDtypeStruct((2 * NF, time_dev + LANES), BF16),
        ],
        scratch_shapes=[
            pltpu.SMEM((NF,), jnp.int32),
            *[pltpu.VMEM(x.shape, x.dtype) for x in operands[1:]],
            pltpu.VMEM((2 * NF, time_dev), BF16),
            pltpu.SemaphoreType.DMA((3,)),
        ],
        compiler_params=params,
        cost_estimate=pl.CostEstimate(flops=2 * 16 * traces.size, bytes_accessed=2 * traces.size, transcendentals=0),
    )(*[pltpu.with_memory_space_constraint(x, pltpu.HBM) for x in operands])
    own = exchange(messages, 4)
    other = lax.ppermute(own, "freq", [(0, 1), (1, 0)])
    counts, filtered = pl.pallas_call(
        tables_kernel,
        in_specs=[in_vmem()] * 4 + [pl.BlockSpec(memory_space=pl.ANY)],
        out_specs=[in_vmem()] * 2,
        out_shape=[
            jax.ShapeDtypeStruct((shots, pairs), F32),
            jax.ShapeDtypeStruct((shot_dev, 2 * NF, time_dev), BF16),
        ],
        scratch_shapes=[pltpu.VMEM((KMAX * shots // 2, LANES), jnp.int32)],
        compiler_params=params,
        cost_estimate=pl.CostEstimate(flops=1 << 22, bytes_accessed=1 << 19, transcendentals=0),
    )(wide, filters, lengths, aperture.transpose(0, 2, 1), own)

    messages = pl.pallas_call(
        product_kernel,
        in_specs=[in_vmem()] * 4,
        out_specs=in_vmem(),
        out_shape=jax.ShapeDtypeStruct((CHIPS, 2 * NF, LANES), BF16),
        scratch_shapes=[
            pltpu.VMEM((shots * 2 * NF, LANES), BF16),
            pltpu.VMEM((shots * 2 * NF, pairs), F32),
            pltpu.VMEM((2 * NF, pairs), F32),
            pltpu.VMEM((shots * 2 * NF, LANES), F32),
            pltpu.VMEM((shots * 2 * NF, LANES), F32),
        ],
        compiler_params=params,
        cost_estimate=pl.CostEstimate(flops=1 << 24, bytes_accessed=1 << 20, transcendentals=0),
    )(own, other, counts, spread)
    received = exchange(messages, 8)

    return pl.pallas_call(
        synthesis_kernel,
        in_specs=[in_vmem(), in_vmem()],
        out_specs=in_hbm(),
        out_shape=jax.ShapeDtypeStruct(traces.shape, BF16),
        scratch_shapes=[
            pltpu.VMEM(traces.shape, BF16),
            pltpu.SemaphoreType.DMA((shot_dev * receivers // LANES,)),
        ],
        compiler_params=params,
        cost_estimate=pl.CostEstimate(flops=2 * 16 * traces.size, bytes_accessed=2 * traces.size, transcendentals=0),
    )(received, filtered)


def general_shards(traces, frequency_bins, aperture, lengths, filters):
    shot_dev, receivers, time_dev = traces.shape
    shots = aperture.shape[0]
    receiver_dev = aperture.shape[1]
    start = lax.axis_index("freq") * time_dev

    def basis_rows(times):
        phases = frequency_bins[:, None] * times[None, :]
        return jnp.stack([cosine(phases & (NT - 1)), cosine((phases + NT // 4) & (NT - 1))], axis=1)

    times = start + jnp.arange(time_dev, dtype=jnp.int32)
    analysis = (basis_rows(times) * NT ** (-0.5)).astype(BF16).reshape(2 * NF, time_dev)
    term = lax.dot_general(
        analysis, traces.reshape(shot_dev * receivers, time_dev), (((1,), (1,)), ((), ())), preferred_element_type=F32
    )
    spectra = lax.psum_scatter(
        term.reshape(NF, 2, shot_dev, receivers), "freq", scatter_dimension=0, tiled=True
    ).astype(BF16)
    second = lax.all_to_all(spectra, "shot", split_axis=3, concat_axis=2, tiled=True).astype(F32)
    stations = spectra[:, :, :, :: receivers // shots]
    first = lax.all_gather(stations, "shot", axis=2, tiled=True).astype(F32)

    def one_shot(inputs):
        legs, lists, list_lengths = inputs
        used = jnp.arange(KMAX, dtype=jnp.int32)[None, :] < list_lengths[:, None]
        lists = jnp.where(used, lists, -1)
        hits = lists[None] == jnp.arange(shots, dtype=jnp.int32)[:, None, None]
        counts = hits.astype(F32).sum(axis=-1)
        legs = legs[..., None]
        real = legs[:, 0] * second[:, 0] - legs[:, 1] * second[:, 1]
        imag = legs[:, 0] * second[:, 1] + legs[:, 1] * second[:, 0]
        return (jnp.stack([real, imag], axis=1) * counts).sum(axis=2)

    summed = lax.map(one_shot, (first.transpose(2, 0, 1, 3), aperture, lengths))
    summed = (summed * KMAX ** (-0.5)).astype(BF16).transpose(1, 2, 0, 3)
    summed = lax.all_to_all(summed, "shot", split_axis=2, concat_axis=3, tiled=True)
    summed = lax.all_gather(summed, "freq", axis=0, tiled=True).reshape(2 * NF, shot_dev, receivers)

    wide = start - HALF + jnp.arange(time_dev + 2 * HALF, dtype=jnp.int32)
    synthesis = basis_rows(wide).astype(BF16).astype(F32).reshape(2 * NF, time_dev + 2 * HALF)
    synthesis = jnp.where((wide >= 0) & (wide < NT), synthesis, 0.0)
    filtered = jnp.zeros((shot_dev, 2 * NF, time_dev), F32)
    for j in range(TAPS):
        tap = filters[:, j].astype(F32)[:, None, None]
        filtered = filtered + tap * synthesis[:, 2 * HALF - j : 2 * HALF - j + time_dev]
    out = jnp.einsum("fsr,sft->srt", summed, filtered.astype(BF16), preferred_element_type=F32)
    return out.astype(BF16)


def solution(mesh):
    in_specs = (
        P("shot", None, "freq"),
        P(),
        P(None, "shot", None),
        P(None, "shot"),
        P("shot", None),
    )
    out_specs = P("shot", None, "freq")
    whole_pieces = mesh.shape["shot"] == 16 and mesh.shape["freq"] == 2
    body = shards if whole_pieces else general_shards
    return jax.shard_map(body, mesh=mesh, in_specs=in_specs, out_specs=out_specs, check_vma=False)
```

```python
import math

import jax
import jax.numpy as jnp
from jax import lax
from jax.experimental import pallas as pl
from jax.experimental.pallas import tpu as pltpu
from jax.sharding import PartitionSpec as P

NT = 1024
NF = 8
KMAX = 32
TAPS = 31
HALF = (TAPS - 1) // 2
LANES = 128
PIECE = 32
DEVICES = ("shot", "freq")
CHIPS = 16


def hops(a, b):
    return abs(a // 4 - b // 4) + (a // 2 % 2 != b // 2 % 2) + (a % 2 != b % 2)


ORDER = sorted(range(CHIPS), key=lambda g: (hops(11, g), -hops(CHIPS - 1, g)))
PLACES = [ORDER.index(g) for g in range(CHIPS)]


def core_groups(run):
    return [[2 * g + (core + g // run) % 2 for g in ORDER] for core in range(2)]


F32 = jnp.float32
BF16 = jnp.bfloat16
VMEM_LIMIT = 48 * 1024 * 1024


def cosine(phases):
    quarter = NT // 4
    turn = (phases + quarter // 2) // quarter
    angle = (phases - turn * quarter).astype(F32) * (2.0 * math.pi / NT)
    square = angle * angle
    sine = angle * (1.0 + square * (-1 / 6 + square * (1 / 120 + square * (-1 / 5040 + square / 362880))))
    cosine = 1.0 + square * (-1 / 2 + square * (1 / 24 + square * (-1 / 720 + square / 40320)))
    near = jnp.where(turn % 2 == 1, sine, cosine)
    return jnp.where((turn == 1) | (turn == 2), -near, near)


def basis_in_kernel(bins_ref, first_time, width):
    rows = lax.broadcasted_iota(jnp.int32, (2 * NF, width), 0)
    times = lax.broadcasted_iota(jnp.int32, (2 * NF, width), 1) + first_time
    frequency = rows // NF * (NF // 2) + rows % (NF // 2)
    part = rows // (NF // 2) % 2
    bins = jnp.zeros((2 * NF, width), jnp.int32)
    for f in range(NF):
        bins = jnp.where(frequency == f, bins_ref[f], bins)
    return cosine((bins * times + part * (NT // 4)) & (NT - 1)), times


def write_spread(spread_ref):
    lane = lax.broadcasted_iota(jnp.int32, (LANES, LANES), 0)
    station = lane % PIECE * 4 + lane // PIECE - lax.broadcasted_iota(jnp.int32, (LANES, LANES), 1) // (LANES // 2)
    for tile in range(spread_ref.shape[1] // LANES):
        here = jnp.where(station == 2 * tile, 1.0, 0.0)
        spread_ref[:, tile * LANES : (tile + 1) * LANES] = here.astype(BF16)


def write_filtered(wide_ref, filters_ref, filtered_ref):
    shot_dev, _, time_dev = filtered_ref.shape
    basis = wide_ref[...].astype(F32)
    width = basis.shape[1]
    taps = filters_ref[...].astype(F32)
    total = [jnp.zeros((2 * NF, time_dev), F32) for _ in range(shot_dev)]
    for j in range(TAPS):
        shift = 2 * HALF - j
        moved = basis if shift == 0 else pltpu.roll(basis, width - shift, 1)
        moved = moved[:, :time_dev]
        for s in range(shot_dev):
            total[s] = total[s] + taps[s : s + 1, j : j + 1] * moved
    for s in range(shot_dev):
        filtered_ref[s] = total[s].astype(BF16)


def bit_sums(words):
    waiting, planes = [], []
    for word in words:
        level = 0
        while True:
            if level == len(waiting):
                waiting.append([])
            waiting[level].append(word)
            if len(waiting[level]) < 3:
                break
            x, y, z = waiting[level]
            either = x ^ y
            waiting[level] = [either ^ z]
            word = (x & y) | (either & z)
            level += 1
    level = 0
    while level < len(waiting):
        held = waiting[level]
        if len(held) > 1:
            if level + 1 == len(waiting):
                waiting.append([])
            x, y = held[0], held[1]
            carries = [x & y]
            if len(held) == 3:
                carries = [(x & y) | ((x ^ y) & held[2])]
            waiting[level + 1] += carries
            held = [x ^ y] if len(held) == 2 else [x ^ y ^ held[2]]
        planes.append(held[0])
        level += 1
    return planes


def write_counts(aperture_ref, lengths_ref, codes_ref, counts_ref):
    half = aperture_ref.shape[0] // 2
    for s in range(half):
        both = jnp.concatenate([aperture_ref[s], aperture_ref[s + half]], axis=1)
        codes_ref[pl.ds(s, KMAX, stride=half), :] = both
    lengths = jnp.concatenate([lengths_ref[:half, :], lengths_ref[half:, :]], axis=1)
    one = jnp.ones((half, LANES), jnp.int32)

    def words():
        for k in range(KMAX):
            codes = codes_ref[k * half : (k + 1) * half, :]
            yield jnp.where(lengths > k, lax.shift_left(one, codes), 0)

    planes = bit_sums(words())
    low = lax.broadcasted_iota(jnp.int32, (half, LANES), 1) < LANES // 2
    for i in range(0, 8, 2):
        packed = []
        for bit in (i, i + 1):
            total = 0
            for level, plane in enumerate(planes):
                spread = lax.shift_right_logical(plane, jnp.full_like(plane, bit)) & 0x01010101
                total = total + (spread << level)
            packed.append(total)
        for byte in range(4):
            left, right = [(lax.shift_right_logical(x, jnp.full_like(x, 8 * byte)) & 255).astype(F32) for x in packed]
            lanes = pl.ds((8 * byte + i) * (LANES // 2), LANES)
            counts_ref[:half, lanes] = jnp.where(low, left, pltpu.roll(right, LANES // 2, 1))
            counts_ref[half:, lanes] = jnp.where(low, pltpu.roll(left, LANES // 2, 1), right)


def tables_kernel(
    wide_ref, filters_ref, lengths_ref, aperture_ref, _, counts_ref, filtered_ref, codes_ref
):
    write_counts(aperture_ref, lengths_ref, codes_ref, counts_ref)
    write_filtered(wide_ref, filters_ref, filtered_ref)


def analysis_kernel(
    bins_hbm, traces_hbm, message_ref, spread_ref, wide_ref, bins_ref, traces_ref, basis_ref, sems,
):
    shot_dev, receivers, time_dev = traces_ref.shape
    bins_copy = pltpu.make_async_copy(bins_hbm, bins_ref, sems.at[0])
    starts = [0, 3 * LANES, receivers]
    blocks = list(zip(starts, starts[1:]))
    copies = []
    for i, (start, end) in enumerate(blocks):
        rows = pl.ds(start, end - start)
        copies.append(pltpu.make_async_copy(traces_hbm.at[:, rows, :], traces_ref.at[:, rows, :], sems.at[1 + i]))
    for copy in [bins_copy] + copies:
        copy.start()

    write_spread(spread_ref)
    bins_copy.wait()
    wide, times = basis_in_kernel(bins_ref, lax.axis_index("freq") * time_dev - HALF, wide_ref.shape[1])
    wide_ref[...] = jnp.where((times >= 0) & (times < NT), wide, 0.0).astype(BF16)
    basis = pltpu.roll(wide, wide.shape[1] - HALF, 1)[:, :time_dev]
    basis_ref[...] = (basis * NT ** (-0.5)).astype(BF16)

    lane = lax.broadcasted_iota(jnp.int32, (2 * NF, LANES), 1)
    row = lax.broadcasted_iota(jnp.int32, (2 * NF, LANES), 0)
    low = lane < LANES // 2
    is_station = lane % PIECE == 0
    stations = jnp.zeros((2 * NF, LANES), F32)
    for copy, (start, end) in zip(copies, blocks):
        copy.wait()
        terms = [
            lax.dot_general(
                basis_ref[...],
                traces_ref[s, start:end, :],
                (((1,), (1,)), ((), ())),
                preferred_element_type=F32,
            )
            for s in range(shot_dev)
        ]
        for j in range((end - start) // LANES):
            tile = start // LANES + j
            first, second = [x[:, j * LANES : (j + 1) * LANES] for x in terms]
            for s, x in enumerate((first, second)):
                marked = jnp.where(is_station, x, 0.0)
                shift = 8 * s + tile
                stations = stations + (pltpu.roll(marked, shift, 1) if shift else marked)
            even = jnp.where(low, first, pltpu.roll(second, LANES // 2, 1))
            odd = jnp.where(low, pltpu.roll(first, LANES // 2, 1), second)
            message_ref[PLACES[2 * tile], : 2 * NF] = even.astype(BF16)
            message_ref[PLACES[2 * tile + 1], : 2 * NF] = odd.astype(BF16)
    stations = jnp.where(row // 4 % 2 == 1, pltpu.roll(stations, 16, 1), stations)
    slabs = [stations[8 * h : 8 * h + 4] + stations[8 * h + 4 : 8 * h + 8] for h in range(2)]
    slab = jnp.concatenate(slabs, axis=0).astype(BF16)
    for g in range(message_ref.shape[0]):
        message_ref[g, 2 * NF :] = slab


def product_kernel(
    own_ref, other_ref, counts_ref, spread_ref, message_ref, station_ref, first_ref, second_ref, same_ref, cross_ref
):
    groups = own_ref.shape[0]
    upper = lax.broadcasted_iota(jnp.int32, (NF, LANES), 0) >= 4
    low = lax.broadcasted_iota(jnp.int32, (NF, LANES), 1) < LANES // 2
    for g in range(groups):
        place = PLACES[g]
        spectra = own_ref[place].astype(F32) + other_ref[place].astype(F32)
        second_ref[:, g * LANES : (g + 1) * LANES] = spectra[: 2 * NF]
        stations = spectra[2 * NF :]
        for s in range(2):
            real = stations if s == 0 else pltpu.roll(stations, LANES - 8, 1)
            imag = pltpu.roll(stations, LANES - 16 - 8 * s, 1)
            legs = [jnp.where(upper, pltpu.roll(imag, 4, 0), real), jnp.where(upper, imag, pltpu.roll(real, 4, 0))]
            station_ref[32 * g + 16 * s : 32 * g + 16 * s + 16, :] = jnp.concatenate(legs, axis=0).astype(BF16)
    first_ref[...] = jnp.dot(station_ref[...], spread_ref[...], preferred_element_type=F32)

    tiles = second_ref.shape[1] // LANES
    span = 4
    for start in range(0, tiles, span):
        columns = [slice(t * LANES, (t + 1) * LANES) for t in range(start, start + span)]
        second = [[second_ref[NF * h : NF * (h + 1), c] for c in columns] for h in range(2)]
        crossed = [[jnp.concatenate([x[4:], x[:4]], axis=0) for x in half] for half in second]
        for s in range(2 * groups):
            counts = [counts_ref[s : s + 1, c] for c in columns]
            for h in range(2):
                rows = slice(16 * s + 8 * h, 16 * s + 8 * h + 8)
                first = [count * first_ref[rows, c] for count, c in zip(counts, columns)]
                same = sum(x * y for x, y in zip(first, second[h]))
                cross = sum(x * y for x, y in zip(first, crossed[h]))
                if start:
                    same, cross = same + same_ref[rows, :], cross + cross_ref[rows, :]
                same_ref[rows, :] = same
                cross_ref[rows, :] = cross
    for g in range(groups):
        message = []
        for h in range(2):
            spectra = []
            for s in (2 * g, 2 * g + 1):
                rows = slice(16 * s + 8 * h, 16 * s + 8 * h + 8)
                same, cross = same_ref[rows, :], cross_ref[rows, :]
                total = jnp.where(upper, cross + pltpu.roll(cross, 4, 0), same - pltpu.roll(same, 4, 0))
                spectra.append((total + pltpu.roll(total, LANES // 2, 1)) * KMAX ** (-0.5))
            message.append(jnp.where(low, spectra[0], spectra[1]))
        message_ref[PLACES[g]] = jnp.concatenate(message, axis=0).astype(BF16)


def synthesis_kernel(received_ref, filtered_ref, out_hbm, out_ref, out_sem):
    low = lax.broadcasted_iota(jnp.int32, (2 * NF, LANES), 1) < LANES // 2
    copies = []
    for tile in range(out_ref.shape[1] // LANES):
        left, right = [received_ref[PLACES[2 * tile + i]] for i in range(2)]
        spectra = (
            jnp.where(low, left, pltpu.roll(right, LANES // 2, 1)),
            jnp.where(low, pltpu.roll(left, LANES // 2, 1), right),
        )
        rows = pl.ds(tile * LANES, LANES)
        for s in range(2):
            out_ref[s, rows, :] = lax.dot_general(
                spectra[s], filtered_ref[s], (((0,), (0,)), ((), ())), preferred_element_type=F32
            ).astype(BF16)
            copy = pltpu.make_async_copy(out_ref.at[s, rows, :], out_hbm.at[s, rows, :], out_sem.at[2 * tile + s])
            copy.start()
            copies.append(copy)
    for copy in copies:
        copy.wait()


def in_vmem():
    return pl.BlockSpec(memory_space=pltpu.VMEM)


def in_hbm():
    return pl.BlockSpec(memory_space=pltpu.HBM)


def exchange(messages, run):
    return lax.all_to_all(
        messages, DEVICES, split_axis=0, concat_axis=0, tiled=True, axis_index_groups=core_groups(run)
    )


def shards(traces, frequency_bins, aperture, lengths, filters):
    shot_dev, receivers, time_dev = traces.shape
    shots = aperture.shape[0]
    params = pltpu.CompilerParams(vmem_limit_bytes=VMEM_LIMIT)

    pairs = shots * aperture.shape[1]
    operands = (frequency_bins, traces)
    messages, spread, wide = pl.pallas_call(
        analysis_kernel,
        in_specs=[in_hbm()] * len(operands),
        out_specs=[in_vmem()] * 3,
        out_shape=[
            jax.ShapeDtypeStruct((CHIPS, 3 * NF, LANES), BF16),
            jax.ShapeDtypeStruct((LANES, pairs), BF16),
            jax.ShapeDtypeStruct((2 * NF, time_dev + LANES), BF16),
        ],
        scratch_shapes=[
            pltpu.SMEM((NF,), jnp.int32),
            *[pltpu.VMEM(x.shape, x.dtype) for x in operands[1:]],
            pltpu.VMEM((2 * NF, time_dev), BF16),
            pltpu.SemaphoreType.DMA((3,)),
        ],
        compiler_params=params,
        cost_estimate=pl.CostEstimate(flops=2 * 16 * traces.size, bytes_accessed=2 * traces.size, transcendentals=0),
    )(*[pltpu.with_memory_space_constraint(x, pltpu.HBM) for x in operands])
    own = exchange(messages, 4)
    other = lax.ppermute(own, "freq", [(0, 1), (1, 0)])
    counts, filtered = pl.pallas_call(
        tables_kernel,
        in_specs=[in_vmem()] * 4 + [pl.BlockSpec(memory_space=pl.ANY)],
        out_specs=[in_vmem()] * 2,
        out_shape=[
            jax.ShapeDtypeStruct((shots, pairs), F32),
            jax.ShapeDtypeStruct((shot_dev, 2 * NF, time_dev), BF16),
        ],
        scratch_shapes=[pltpu.VMEM((KMAX * shots // 2, LANES), jnp.int32)],
        compiler_params=params,
        cost_estimate=pl.CostEstimate(flops=1 << 22, bytes_accessed=1 << 19, transcendentals=0),
    )(wide, filters, lengths, aperture.transpose(0, 2, 1), own)

    messages = pl.pallas_call(
        product_kernel,
        in_specs=[in_vmem()] * 4,
        out_specs=in_vmem(),
        out_shape=jax.ShapeDtypeStruct((CHIPS, 2 * NF, LANES), BF16),
        scratch_shapes=[
            pltpu.VMEM((shots * 2 * NF, LANES), BF16),
            pltpu.VMEM((shots * 2 * NF, pairs), F32),
            pltpu.VMEM((2 * NF, pairs), F32),
            pltpu.VMEM((shots * 2 * NF, LANES), F32),
            pltpu.VMEM((shots * 2 * NF, LANES), F32),
        ],
        compiler_params=params,
        cost_estimate=pl.CostEstimate(flops=1 << 24, bytes_accessed=1 << 20, transcendentals=0),
    )(own, other, counts, spread)
    received = exchange(messages, 8)

    return pl.pallas_call(
        synthesis_kernel,
        in_specs=[in_vmem(), in_vmem()],
        out_specs=in_hbm(),
        out_shape=jax.ShapeDtypeStruct(traces.shape, BF16),
        scratch_shapes=[
            pltpu.VMEM(traces.shape, BF16),
            pltpu.SemaphoreType.DMA((shot_dev * receivers // LANES,)),
        ],
        compiler_params=params,
        cost_estimate=pl.CostEstimate(flops=2 * 16 * traces.size, bytes_accessed=2 * traces.size, transcendentals=0),
    )(received, filtered)


def general_shards(traces, frequency_bins, aperture, lengths, filters):
    shot_dev, receivers, time_dev = traces.shape
    shots = aperture.shape[0]
    receiver_dev = aperture.shape[1]
    start = lax.axis_index("freq") * time_dev

    def basis_rows(times):
        phases = frequency_bins[:, None] * times[None, :]
        return jnp.stack([cosine(phases & (NT - 1)), cosine((phases + NT // 4) & (NT - 1))], axis=1)

    times = start + jnp.arange(time_dev, dtype=jnp.int32)
    analysis = (basis_rows(times) * NT ** (-0.5)).astype(BF16).reshape(2 * NF, time_dev)
    term = lax.dot_general(
        analysis, traces.reshape(shot_dev * receivers, time_dev), (((1,), (1,)), ((), ())), preferred_element_type=F32
    )
    spectra = lax.psum_scatter(
        term.reshape(NF, 2, shot_dev, receivers), "freq", scatter_dimension=0, tiled=True
    ).astype(BF16)
    second = lax.all_to_all(spectra, "shot", split_axis=3, concat_axis=2, tiled=True).astype(F32)
    stations = spectra[:, :, :, :: receivers // shots]
    first = lax.all_gather(stations, "shot", axis=2, tiled=True).astype(F32)

    def one_shot(inputs):
        legs, lists, list_lengths = inputs
        used = jnp.arange(KMAX, dtype=jnp.int32)[None, :] < list_lengths[:, None]
        lists = jnp.where(used, lists, -1)
        hits = lists[None] == jnp.arange(shots, dtype=jnp.int32)[:, None, None]
        counts = hits.astype(F32).sum(axis=-1)
        legs = legs[..., None]
        real = legs[:, 0] * second[:, 0] - legs[:, 1] * second[:, 1]
        imag = legs[:, 0] * second[:, 1] + legs[:, 1] * second[:, 0]
        return (jnp.stack([real, imag], axis=1) * counts).sum(axis=2)

    summed = lax.map(one_shot, (first.transpose(2, 0, 1, 3), aperture, lengths))
    summed = (summed * KMAX ** (-0.5)).astype(BF16).transpose(1, 2, 0, 3)
    summed = lax.all_to_all(summed, "shot", split_axis=2, concat_axis=3, tiled=True)
    summed = lax.all_gather(summed, "freq", axis=0, tiled=True).reshape(2 * NF, shot_dev, receivers)

    wide = start - HALF + jnp.arange(time_dev + 2 * HALF, dtype=jnp.int32)
    synthesis = basis_rows(wide).astype(BF16).astype(F32).reshape(2 * NF, time_dev + 2 * HALF)
    synthesis = jnp.where((wide >= 0) & (wide < NT), synthesis, 0.0)
    filtered = jnp.zeros((shot_dev, 2 * NF, time_dev), F32)
    for j in range(TAPS):
        tap = filters[:, j].astype(F32)[:, None, None]
        filtered = filtered + tap * synthesis[:, 2 * HALF - j : 2 * HALF - j + time_dev]
    out = jnp.einsum("fsr,sft->srt", summed, filtered.astype(BF16), preferred_element_type=F32)
    return out.astype(BF16)


def solution(mesh):
    in_specs = (
        P("shot", None, "freq"),
        P(),
        P(None, "shot", None),
        P(None, "shot"),
        P("shot", None),
    )
    out_specs = P("shot", None, "freq")
    whole_pieces = mesh.shape["shot"] == 16 and mesh.shape["freq"] == 2
    body = shards if whole_pieces else general_shards
    return jax.shard_map(body, mesh=mesh, in_specs=in_specs, out_specs=out_specs, check_vma=False)
```
